256 devices in a mesh: ctx: 32 (over z, y_hi, core), head: 8 (over y_lo, x).
Axes of the slice: x: 4, y: 4 (y_hi: 2, y_lo: 2; y = y_hi * 2 + y_lo), z: 8, core: 2. Of those that a mesh axis runs over, the one named last changes fastest.
Arguments:
- tokens: bfloat16 [8192, 2048], P('ctx'), may hold values from -6 to 6
- w_qkv: bfloat16 [2048, 3, 2048], P(None, None, 'head'), may hold values from -0.125 to 0.125
- w_out: bfloat16 [2048, 2048], P('head'), may hold values from -0.125 to 0.125
- grad_out: bfloat16 [8192, 2048], P('ctx'), may hold values from -6 to 6
Outputs:
- grad_x: bfloat16 [8192, 2048], P('ctx', 'head')
- grad_wqkv: float32 [2048, 3, 2048], P('ctx', None, 'head')
- grad_wout: float32 [2048, 2048], P('head', 'ctx')
The draws below stay inside these ranges and needn't reach their ends.
All inputs are finite; a program needn't handle non-finite values.
Results may differ from the reference program's by a relative error of at most 0.023.
Values may be sent and summed in bfloat16 or wider, within the bound.
No kernel may reach another device: no remote copies, remote signals or barrier semaphores. Data moves between devices by JAX's collectives and lax.ppermute only.
A program may use at most 128 MiB of HBM per device.

```python
import jax
import jax.numpy as jnp
from jax import lax

D = 2048
HEADS = 16
DH = 128
BLK = 16
LEVELS = 7
TOKENS = 8192


def levels(key, shape, split, least, largest):
    gain, own = 1.0, jax.random.fold_in(key, 6)
    for position, blocks in split:
        heights = jnp.exp(jax.random.uniform(jax.random.fold_in(own, position), (blocks,), jnp.float32, least / len(split), largest / len(split)))
        gain = gain * jnp.repeat(heights, shape[position] // blocks).reshape([-1 if axis == position else 1 for axis in range(len(shape))])
    return gain


def normal_values(key, shape, spread, reach, pieces=(), held_as=jnp.bfloat16):
    array = jax.random.normal(key, shape, jnp.float32) * spread
    if len(pieces) > 0:
        array = levels(key, shape, pieces, -0.22, 0.18) * array
    return jnp.clip(array, min=-reach, max=reach).astype(held_as)


def setup_inputs(seed: int = 0) -> dict:
    key_list = jax.random.split(jax.random.key(seed), 5)
    return {
        "tokens": normal_values(key_list[0], (TOKENS, D), 1.0, 6.0, ((0, 32),)),
        "w_qkv": normal_values(key_list[1], (D, 3, D), D ** -0.5, 0.125, ((2, 8),)),
        "w_out": normal_values(key_list[2], (D, D), D ** -0.5, 0.125, ((0, 8),)),
        "grad_out": normal_values(key_list[3], (TOKENS, D), 1.0, 6.0, ((0, 32),)),
    }


HIGHEST = lax.Precision.HIGHEST

def rms_norm(values):
    return values * lax.rsqrt(lax.optimization_barrier(jnp.mean(values * values, axis=-1, keepdims=True)) + 1e-06)

def coarse_mean(values, factor):
    return lax.optimization_barrier(jnp.mean(values.reshape((values.shape[0] // factor, factor) + values.shape[1:]), axis=1))

def windows(padded, nblocks):
    stacked = padded.reshape((nblocks + 2, BLK) + padded.shape[1:])
    return jnp.concatenate([stacked[:-2], stacked[1:-1], stacked[2:]], axis=1)

def attend_blocks(queries, keys, values, weight_mask):
    scores = jnp.einsum('bqhd,bkhd->bqhk', queries, keys, precision=HIGHEST) * DH ** (-0.5)
    weights = jnp.exp(scores) * weight_mask[:, None, None, :]
    numerator = jnp.einsum('bqhk,bkhd->bqhd', weights, values, precision=HIGHEST)
    return (numerator, lax.optimization_barrier(jnp.sum(weights, axis=-1)))

def swap_halves(stacked):
    paired = stacked.reshape((stacked.shape[0] // 2, 2) + stacked.shape[1:])
    return paired[:, ::-1].reshape(stacked.shape)

def hier_attention(queries, keys, values):
    total_rows = queries.shape[0]
    head_count = queries.shape[1]
    nblocks = total_rows // BLK
    q_norm = rms_norm(queries)
    k_norm = rms_norm(keys)
    padding = ((BLK, BLK), (0, 0), (0, 0))
    key_win = windows(jnp.pad(k_norm, padding), nblocks)
    val_win = windows(jnp.pad(values, padding), nblocks)
    block_ids = jnp.arange(nblocks)
    left_keep = jnp.broadcast_to((block_ids >= 1)[:, None], (nblocks, BLK))
    right_keep = jnp.broadcast_to((block_ids <= nblocks - 2)[:, None], (nblocks, BLK))
    middle_keep = jnp.ones((nblocks, BLK), dtype=bool)
    block_mask = jnp.concatenate([left_keep, middle_keep, right_keep], axis=1).astype(jnp.float32)
    numerator, denominator = attend_blocks(q_norm.reshape(nblocks, BLK, head_count, DH), key_win, val_win, block_mask)
    numerator = numerator.reshape(total_rows, head_count, DH)
    denominator = denominator.reshape(total_rows, head_count)
    for level_no in range(1, LEVELS + 1):
        factor = 2 ** level_no
        coarse_rows = total_rows // factor
        coarse_blocks = coarse_rows // BLK
        shape_four = (coarse_blocks, BLK, head_count, DH)
        coarse_q = rms_norm(coarse_mean(queries, factor)).reshape(shape_four)
        coarse_k = swap_halves(rms_norm(coarse_mean(keys, factor)).reshape(shape_four))
        coarse_v = swap_halves(coarse_mean(values, factor).reshape(shape_four))
        part_num, part_den = attend_blocks(coarse_q, coarse_k, coarse_v, jnp.ones((coarse_blocks, BLK), jnp.float32))
        numerator = numerator + jnp.repeat(part_num.reshape(coarse_rows, head_count, DH), factor, axis=0)
        denominator = denominator + jnp.repeat(part_den.reshape(coarse_rows, head_count), factor, axis=0)
    return numerator / denominator[:, :, None]

def reference(tokens, w_qkv, w_out, grad_out):
    total_rows = tokens.shape[0]
    model_width = tokens.shape[1]
    flat_w = w_qkv.reshape(model_width, 3 * model_width)
    projected = jnp.dot(tokens, flat_w, preferred_element_type=jnp.float32).astype(jnp.bfloat16)
    split_shape = (total_rows, HEADS, DH)
    queries = projected[:, :model_width].astype(jnp.float32).reshape(split_shape)
    keys = projected[:, model_width:2 * model_width].astype(jnp.float32).reshape(split_shape)
    values = projected[:, 2 * model_width:].astype(jnp.float32).reshape(split_shape)
    attention, attention_back = jax.vjp(hier_attention, queries, keys, values)
    attn_out = attention.reshape(total_rows, model_width).astype(jnp.bfloat16)
    d_attn = jnp.dot(grad_out, w_out.T, preferred_element_type=jnp.float32).astype(jnp.bfloat16)
    d_queries, d_keys, d_values = attention_back(d_attn.astype(jnp.float32).reshape(split_shape))
    d_qkv = jnp.concatenate([d_queries.reshape(total_rows, model_width), d_keys.reshape(total_rows, model_width), d_values.reshape(total_rows, model_width)], axis=1).astype(jnp.bfloat16)
    grad_x = jnp.dot(d_qkv, flat_w.T, preferred_element_type=jnp.float32).astype(jnp.bfloat16)
    grad_wqkv = jnp.dot(tokens.T, d_qkv, preferred_element_type=jnp.float32).reshape(model_width, 3, model_width)
    grad_wout = jnp.dot(attn_out.T, grad_out, preferred_element_type=jnp.float32)
    return (grad_x, grad_wqkv, grad_wout)
```

```python
import functools

import jax
import jax.numpy as jnp
import numpy as np
from jax import lax
from jax.experimental import pallas as pl
from jax.experimental.pallas import tpu as pltpu
from jax.sharding import PartitionSpec as P

DH = 128
BLK = 16
T = 256
ROWS = 256
NEAR = 2 * BLK
REM = 64
FAR = 96
SCALE = DH**-0.5
BF = jnp.bfloat16
F32 = jnp.float32

STARTS = {1: 0, 2: 128, 3: 192, 4: 224, 5: 240, 6: 248, 7: 252}


def tables():
    spread = np.zeros((T, ROWS), np.float32)
    mean = np.zeros((ROWS, T), np.float32)
    pairs = np.zeros((ROWS, ROWS), np.float32)
    for level, start in STARTS.items():
        factor = 2**level
        for row in range(T // factor):
            spread[row * factor : (row + 1) * factor, start + row] = 1.0
            mean[start + row, row * factor : (row + 1) * factor] = 1.0 / factor
        if level <= 3:
            for block in range(T // factor // BLK):
                other = start + (block ^ 1) * BLK
                mine = start + block * BLK
                pairs[mine : mine + BLK, other : other + BLK] = 1.0
    block_of = np.arange(T) // BLK
    band = (np.abs(block_of[:, None] - block_of[None, :]) <= 1).astype(np.float32)
    rim = np.zeros((T, REM), np.float32)
    rim[:BLK, :BLK] = np.eye(BLK)
    rim[T - BLK :, BLK:NEAR] = np.eye(BLK)
    rim[:, NEAR:] = spread[:, 224:]
    meets = np.zeros((REM, FAR), np.float32)
    meets[0:16, 0:16] = 1.0
    meets[16:32, 16:32] = 1.0
    meets[32:48, 32:48] = 1.0
    meets[48:56, 48:64] = 1.0
    meets[56:60, 64:80] = 1.0
    meets[60:62, 80:96] = 1.0
    bf = lambda array: np.asarray(array, dtype=BF)
    return {
        "spread": bf(spread),
        "gather": bf(spread.T),
        "mean": bf(mean),
        "unmean": bf(mean.T),
        "band": band,
        "pairs": pairs,
        "rim": bf(rim),
        "unrim": bf(rim.T),
        "meets": meets,
        "met": np.ascontiguousarray(meets.T),
    }


def dot(left, right):
    return jnp.dot(left, right, preferred_element_type=F32)


def dot_nt(left, right):
    return lax.dot_general(left, right, (((1,), (1,)), ((), ())), preferred_element_type=F32)


def dot_tn(left, right):
    return lax.dot_general(left, right, (((0,), (0,)), ((), ())), preferred_element_type=F32)


def dot_two(exact, right):
    high = right.astype(BF)
    low = (right - high.astype(F32)).astype(BF)
    return dot(exact, high) + dot(exact, low)


def normed(values):
    scale = lax.rsqrt(jnp.mean(values * values, axis=-1, keepdims=True) + 1e-06)
    return values * scale, scale


def norm_back(unit, scale, grad):
    return scale * (grad - unit * jnp.mean(grad * unit, axis=-1, keepdims=True))


def head(array, number):
    return array[:, number * DH : (number + 1) * DH]


def with_ones(values):
    return jnp.concatenate([values, jnp.ones_like(values)], axis=1)


def call(kernel, outs, *args, scalars=None, flops=1e9, moved=2e6):
    specs = [pl.BlockSpec(memory_space=pltpu.VMEM)] * len(args)
    if scalars is not None:
        specs = [pl.BlockSpec(memory_space=pltpu.SMEM)] + specs
        args = (scalars,) + args
    return pl.pallas_call(
        kernel,
        out_shape=tuple(jax.ShapeDtypeStruct(shape, dtype) for shape, dtype in outs),
        in_specs=specs,
        out_specs=tuple(pl.BlockSpec(memory_space=pltpu.VMEM) for _ in outs),
        compiler_params=pltpu.CompilerParams(vmem_limit_bytes=44 * 1024 * 1024),
        cost_estimate=pl.CostEstimate(
            flops=int(flops), bytes_accessed=int(moved), transcendentals=0
        ),
    )(*args)


def project_kernel(pos, tokens, weights, mean, qkv_out, coarse_out, near_out, far_out):
    tok = tokens[...]
    parts = [dot(tok, weights[number]).astype(BF) for number in range(3)]
    qkv = jnp.concatenate(parts, axis=1)
    qkv_out[...] = qkv
    coarse = dot(mean[...], qkv)
    coarse_out[...] = coarse
    even = pos[0] % 2 == 0
    first = qkv[:BLK].astype(F32)
    last = qkv[T - BLK :].astype(F32)
    near_out[:BLK] = coarse[224:240].astype(BF)
    near_out[BLK:] = jnp.where(even, last, first).astype(BF)
    far_out[...] = jnp.where(even, first, last).astype(BF)


def d_attn_kernel(pos, grad_out, w_out, tokens, d_attn_out, own_out, other_out):
    d_attn_out[...] = dot_nt(grad_out[...], w_out[...]).astype(BF)
    even = pos[0] % 2 == 0
    width = tokens.shape[1] // 32
    for number, array in enumerate((tokens, grad_out)):
        rows = slice(number * T, (number + 1) * T)
        whole = array[...]
        halves = [
            jnp.concatenate(
                [whole[:, (2 * j + c) * width : (2 * j + c + 1) * width] for j in range(16)],
                axis=1,
            )
            for c in (0, 1)
        ]
        own_out[rows] = jnp.where(even, halves[0], halves[1])
        other_out[rows] = jnp.where(even, halves[1], halves[0])


def merge_kernel(factor, first, second, out):
    row = lax.broadcasted_iota(jnp.int32, (BLK, BLK), 0)
    col = lax.broadcasted_iota(jnp.int32, (BLK, BLK), 1)
    left = jnp.where(col // 2 == row, factor, 0.0).astype(BF)
    right = jnp.where(col // 2 + BLK // 2 == row, factor, 0.0).astype(BF)
    out[...] = (dot(left, first[...]) + dot(right, second[...])).astype(BF)


def local_units(qkv, coarse, number):
    query = head(qkv, number).astype(F32)
    key = head(qkv, 2 + number).astype(F32)
    return (
        normed(query),
        normed(key),
        head(qkv, 4 + number),
        normed(head(coarse, number)),
        normed(head(coarse, 2 + number)),
        head(coarse, 4 + number).astype(BF),
    )


def local_weights(units, band, pairs):
    (qn, _), (kn, _), _, (qc, _), (kc, _), _ = units
    near = jnp.exp(dot_nt(qn.astype(BF), kn.astype(BF)) * SCALE) * band
    far = jnp.exp(dot_nt(qc.astype(BF), kc.astype(BF)) * SCALE) * pairs
    return near, far


def local_forward_kernel(qkv_ref, coarse_ref, band, pairs, spread, out):
    qkv = qkv_ref[...]
    coarse = coarse_ref[...]
    for number in range(2):
        units = local_units(qkv, coarse, number)
        near, far = local_weights(units, band[...], pairs[...])
        total = dot(near.astype(BF), with_ones(units[2]))
        part = dot(far.astype(BF), with_ones(units[5]))
        out[:, number * 2 * DH : (number + 1) * 2 * DH] = total + dot_two(spread[...], part)


def sides(even, near, far):
    left = jnp.where(even, far, near)
    right = jnp.where(even, near, far)
    return left, right


def remote_rows(pos, near, far, level_5, level_6, level_7):
    even = pos[0] % 2 == 0
    arrived = near[...].astype(F32)
    left, right = sides(even, arrived[BLK:], far[...].astype(F32))
    return jnp.concatenate(
        [
            left,
            right,
            arrived[:BLK],
            level_5[...].astype(F32),
            level_6[...].astype(F32),
            level_7[...].astype(F32),
        ],
        axis=0,
    )


def own_rows(fine, coarse):
    return jnp.concatenate([fine[:BLK], fine[T - BLK :], coarse[224:]], axis=0)


def exists(pos, shape, axis):
    where = lax.broadcasted_iota(jnp.int32, shape, axis)
    no_left = jnp.logical_and(pos[0] == 0, where < BLK)
    no_right = jnp.logical_and(pos[0] == 31, jnp.logical_and(where >= BLK, where < NEAR))
    return jnp.where(jnp.logical_or(no_left, no_right), 0.0, 1.0)


def remote_weights(pos, units, remote, meets, number):
    (qn, _), _, _, (qc, _), _, _ = units
    query = own_rows(qn, qc).astype(BF)
    key = normed(head(remote, 2 + number))[0].astype(BF)
    value = head(remote, 4 + number).astype(BF)
    weights = jnp.exp(dot_nt(query, key) * SCALE) * meets * exists(pos, (REM, FAR), 1)
    return weights, query, key, value


def remote_forward_kernel(
    pos, qkv_ref, coarse_ref, local_ref, d_attn, near, far, level_5, level_6, level_7,
    meets, rim, gather, attn_out, d_num_out, d_den_out, near_out, far_out,
):
    qkv = qkv_ref[...]
    coarse = coarse_ref[...]
    remote = remote_rows(pos, near, far, level_5, level_6, level_7)
    even = pos[0] % 2 == 0
    for number in range(2):
        units = local_units(qkv, coarse, number)
        weights, _, _, value = remote_weights(pos, units, remote, meets[...], number)
        part = dot(weights.astype(BF), with_ones(value))
        total = local_ref[:, number * 2 * DH : (number + 1) * 2 * DH] + dot_two(rim[...], part)
        cols = slice(number * DH, (number + 1) * DH)
        inverse = 1.0 / total[:, DH:]
        attn = total[:, :DH] * inverse
        attn_out[:, cols] = attn.astype(BF)
        d_num = (d_attn[:, cols].astype(F32) * inverse).astype(BF)
        d_den = -jnp.sum(d_num.astype(F32) * attn, axis=-1, keepdims=True)
        d_den = jnp.broadcast_to(d_den, (T, DH))
        d_num_out[:, cols] = d_num
        d_den_out[:, cols] = d_den
        sums = dot_two(
            gather[224:240, :], jnp.concatenate([d_num.astype(F32), d_den], axis=1)
        )
        for offset, full, row_sums in (
            (0, d_num.astype(F32), sums[:, :DH]),
            (2 * DH, d_den, sums[:, DH:]),
        ):
            at = slice(offset + number * DH, offset + (number + 1) * DH)
            first = full[:BLK]
            last = full[T - BLK :]
            near_out[:BLK, at] = row_sums.astype(BF)
            near_out[BLK:, at] = jnp.where(even, last, first).astype(BF)
            far_out[:, at] = jnp.where(even, first, last).astype(BF)


def local_backward_kernel(
    pos, qkv_ref, coarse_ref, d_num_ref, d_den_ref, near, far, level_5, level_6, level_7,
    meets, unrim, gather, unmean, band, pairs,
    dq_out, fine_out, coarse_out,
):
    qkv = qkv_ref[...]
    coarse = coarse_ref[...]
    remote = remote_rows(pos, near, far, level_5, level_6, level_7)
    for number in range(2):
        cols = slice(number * DH, (number + 1) * DH)
        units = local_units(qkv, coarse, number)
        (qn, q_scale), (kn, _), value, (qc, qc_scale), (kc, _), value_c = units
        d_num = d_num_ref[:, cols]
        d_den = d_den_ref[:, cols]
        both = jnp.concatenate([d_num.astype(F32), d_den], axis=1)
        sums = dot_two(gather[...], both)
        d_num_c = sums[:, :DH].astype(BF)
        d_den_c = sums[:, DH : DH + 1]
        near_w, far_w = local_weights(units, band[...], pairs[...])
        d_near = (near_w * (dot_nt(d_num, value) + d_den[:, :1]) * SCALE).astype(BF)
        d_far = (far_w * (dot_nt(d_num_c, value_c) + d_den_c) * SCALE).astype(BF)
        dqn = dot(d_near, kn.astype(BF))
        dqc = dot(d_far, kc.astype(BF))
        fine_out[:, cols] = dot_tn(d_near, qn.astype(BF))
        coarse_out[:, cols] = dot_tn(d_far, qc.astype(BF))
        vals = slice((2 + number) * DH, (3 + number) * DH)
        fine_out[:, vals] = dot_tn(near_w.astype(BF), d_num)
        coarse_out[:, vals] = dot_tn(far_w.astype(BF), d_num_c)
        weights, _, key_r, value_r = remote_weights(pos, units, remote, meets[...], number)
        sums_r = dot_two(unrim[...], both)
        d_rem = dot_nt(sums_r[:, :DH].astype(BF), value_r) + sums_r[:, DH : DH + 1]
        dqr = dot((weights * d_rem * SCALE).astype(BF), key_r)
        dqn = jnp.concatenate(
            [dqn[:BLK] + dqr[:BLK], dqn[BLK : T - BLK], dqn[T - BLK :] + dqr[BLK:NEAR]], axis=0
        )
        dqc = jnp.concatenate([dqc[:224], dqc[224:] + dqr[NEAR:]], axis=0)
        dq = norm_back(qn, q_scale, dqn) + dot_two(unmean[...], norm_back(qc, qc_scale, dqc))
        dq_out[:, cols] = dq.astype(BF)


def remote_backward_kernel(
    pos, qkv_ref, coarse_ref, fine_ref, coarse_grad_ref,
    near, far, level_5, level_6, level_7, g_near, g_far, g_5, g_6, g_7,
    met, unmean, dkv_out,
):
    qkv = qkv_ref[...]
    coarse = coarse_ref[...]
    remote = remote_rows(pos, near, far, level_5, level_6, level_7)
    grads = remote_rows(pos, g_near, g_far, g_5, g_6, g_7)
    for number in range(2):
        units = local_units(qkv, coarse, number)
        _, (kn, k_scale), value, _, (kc, kc_scale), value_c = units
        query = normed(head(remote, number))[0].astype(BF)
        key = own_rows(kn, kc).astype(BF)
        vals = own_rows(value.astype(F32), value_c.astype(F32)).astype(BF)
        weights = jnp.exp(dot_nt(query, key) * SCALE) * met[...] * exists(pos, (FAR, REM), 0)
        d_num = head(grads, number).astype(BF)
        d_den = head(grads, 2 + number)[:, :1]
        d_score = (weights * (dot_nt(d_num, vals) + d_den) * SCALE).astype(BF)
        dk = dot_tn(d_score, query)
        dv = dot_tn(weights.astype(BF), d_num)

        def joined(part, table, small, cols):
            rim = jnp.concatenate(
                [
                    part[:BLK, cols] + small[:BLK],
                    part[BLK : T - BLK, cols],
                    part[T - BLK :, cols] + small[BLK:NEAR],
                ],
                axis=0,
            )
            rows = jnp.concatenate([table[:224, cols], table[224:, cols] + small[NEAR:]], axis=0)
            return rim, rows

        k_cols = slice(number * DH, (number + 1) * DH)
        v_cols = slice((2 + number) * DH, (3 + number) * DH)
        dkn, dkc = joined(fine_ref, coarse_grad_ref, dk, k_cols)
        dvn, dvc = joined(fine_ref, coarse_grad_ref, dv, v_cols)
        spread = dot_two(
            unmean[...], jnp.concatenate([norm_back(kc, kc_scale, dkc), dvc], axis=1)
        )
        dkv_out[:, k_cols] = (norm_back(kn, k_scale, dkn) + spread[:, :DH]).astype(BF)
        dkv_out[:, v_cols] = (dvn + spread[:, DH:]).astype(BF)


def weight_kernel(split, pos, own_rows_ref, other_rows_ref, own, other, *outs):
    z = pos[0] // 4
    width = own_rows_ref.shape[1] // 8
    for step in range(8):
        at = pl.ds(pl.multiple_of((z + step) % 8 * width, width), width)
        if split:
            for part in range(2):
                rows = slice(part * T, (part + 1) * T)
                cols = slice(part * T, (part + 1) * T)
                total = dot_tn(own_rows_ref[rows, at], own[:, cols])
                total += dot_tn(other_rows_ref[rows, at], other[:, cols])
                outs[step][:, cols] = total.astype(BF)
        else:
            total = dot_tn(own_rows_ref[:T, at], own[...])
            total += dot_tn(other_rows_ref[:T, at], other[...])
            outs[step][...] = total.astype(BF)


def sum_z_kernel(pos, *refs):
    keep, send = refs[-2:]
    total = refs[0][...].astype(F32)
    for ref in refs[1:-2]:
        total = total + ref[...].astype(F32)
    half = total.shape[0] // 2
    low = pos[0] // 2 % 2 == 0
    keep[...] = jnp.where(low, total[:half], total[half:])
    send[...] = jnp.where(low, total[half:], total[:half]).astype(BF)


def finish_kernel(keep_1, came_1, keep_2, came_2, w_qkv, w_out):
    early = keep_1[...] + came_1[...].astype(F32)
    late = keep_2[...] + came_2[...].astype(F32)
    w_qkv[0] = early[:, :T]
    w_qkv[1] = late[:, :T]
    w_qkv[2] = late[:, T:]
    w_out[...] = early[:, T:]


def grad_x_kernel(pos, dq, dkv, weights, *outs):
    x = pos[1] % 4
    y = pos[1] // 4
    for step in range(4):
        for turn in range(2):
            target = (y + turn) % 2 * 4 + (x + step) % 4
            rows = pl.ds(pl.multiple_of(target * T, T), T)
            total = dot_nt(dq[...], weights[0, rows, :])
            total += dot_nt(dkv[:, :T], weights[1, rows, :])
            total += dot_nt(dkv[:, T:], weights[2, rows, :])
            outs[step][turn * T : (turn + 1) * T] = total.astype(BF)


def sum_x_kernel(first, second, third, fourth, keep, send):
    total = first[...].astype(F32) + second[...].astype(F32)
    total = total + third[...].astype(F32) + fourth[...].astype(F32)
    keep[...] = total[:T]
    send[...] = total[T:].astype(BF)


def last_x_kernel(keep, came, out):
    out[...] = (keep[...] + came[...].astype(F32)).astype(BF)


def local(tokens, w_qkv, w_out, grad_out):
    const = {name: jnp.asarray(array) for name, array in tables().items()}
    head_count = lax.axis_size("head")
    pos = jnp.stack([lax.axis_index("ctx"), lax.axis_index("head")]).astype(jnp.int32)
    weights = jnp.transpose(w_qkv, (1, 0, 2))
    width = tokens.shape[1]
    wide = 3 * T

    def swap(array, bit):
        return lax.ppermute(array, "ctx", [(i, i ^ bit) for i in range(32)])

    def chain(array):
        pairs = [(i, i + 1) for i in range(1, 31, 2)]
        return lax.ppermute(array, "ctx", pairs + [(b, a) for a, b in pairs])

    def turn_z(array, step):
        return lax.ppermute(
            array, "ctx", [(i, (i // 4 + step) % 8 * 4 + i % 4) for i in range(32)]
        )

    def exchange(near, far, factor):
        arrived = swap(near, 1)
        other = chain(far)
        shape = [((BLK, near.shape[1]), BF)]
        merge = functools.partial(merge_kernel, factor)
        (block_5,) = call(merge, shape, near[:BLK], arrived[:BLK])
        level_5 = swap(block_5, 2)
        (block_6,) = call(merge, shape, block_5, level_5)
        level_6 = swap(block_6, 4)
        (block_7,) = call(merge, shape, block_6, level_6)
        level_7 = swap(block_7, 8)
        return arrived, other, level_5, level_6, level_7

    qkv, coarse, near, far = call(
        project_kernel,
        [((T, wide), BF), ((ROWS, wide), F32), ((NEAR, wide), BF), ((BLK, wide), BF)],
        tokens, weights, const["mean"], scalars=pos,
    )
    remote = exchange(near, far, 0.5)
    d_attn, own_half, other_half = call(
        d_attn_kernel,
        [((T, T), BF), ((2 * T, width // 2), BF), ((2 * T, width // 2), BF)],
        grad_out, w_out, tokens, scalars=pos,
    )
    sent_half = swap(other_half, 1)
    (forward,) = call(
        local_forward_kernel, [((T, 2 * T), F32)],
        qkv, coarse, const["band"], const["pairs"], const["spread"],
    )
    attn, d_num, d_den, g_near, g_far = call(
        remote_forward_kernel,
        [((T, T), BF), ((T, T), BF), ((T, T), F32), ((NEAR, 2 * T), BF), ((BLK, 2 * T), BF)],
        qkv, coarse, forward, d_attn, *remote, const["meets"], const["rim"], const["gather"],
        scalars=pos,
    )
    grads = exchange(g_near, g_far, 1.0)
    dq, fine, coarse_grad = call(
        local_backward_kernel,
        [((T, T), BF), ((T, 2 * T), F32), ((ROWS, 2 * T), F32)],
        qkv, coarse, d_num, d_den, *remote, const["meets"], const["unrim"], const["gather"],
        const["unmean"], const["band"], const["pairs"], scalars=pos,
    )
    chunk = width // 16

    def weight_part(columns, split):
        pieces = call(
            functools.partial(weight_kernel, split),
            [((chunk, 2 * T), BF)] * 8,
            own_half, sent_half, columns, swap(columns, 1), scalars=pos,
        )
        came = [turn_z(pieces[step], step) for step in range(1, 8)]
        keep, send = call(
            sum_z_kernel, [((chunk // 2, 2 * T), F32), ((chunk // 2, 2 * T), BF)],
            pieces[0], *came, scalars=pos,
        )
        return keep, swap(send, 2)

    early = weight_part(jnp.concatenate([dq, attn], axis=1), True)
    (dkv,) = call(
        remote_backward_kernel, [((T, 2 * T), BF)],
        qkv, coarse, fine, coarse_grad, *remote, *grads, const["met"], const["unmean"],
        scalars=pos,
    )
    late = weight_part(dkv, False)
    if head_count == 8:
        pieces = call(
            grad_x_kernel, [((2 * T, T), BF)] * 4, dq, dkv, weights, scalars=pos
        )

        def turn_x(array, step):
            pairs = [(i, i // 4 * 4 + (i % 4 + step) % 4) for i in range(8)]
            return lax.ppermute(array, "head", pairs)

        came = [turn_x(pieces[step], step) for step in range(1, 4)]
        keep, send = call(sum_x_kernel, [((T, T), F32), ((T, T), BF)], pieces[0], *came)
        other = lax.ppermute(send, "head", [(i, i ^ 4) for i in range(8)])
        (grad_x,) = call(last_x_kernel, [((T, T), BF)], keep, other)
    else:
        flat = jnp.transpose(weights, (1, 0, 2)).reshape(width, wide)
        grad_x = dot_nt(jnp.concatenate([dq, dkv], axis=1), flat).astype(BF)
    grad_wqkv, grad_wout = call(
        finish_kernel, [((3, chunk // 2, T), F32), ((chunk // 2, T), F32)], *early, *late
    )
    return grad_x, jnp.transpose(grad_wqkv, (1, 0, 2)), grad_wout.T


def solution(mesh):
    placed = (P("ctx", None), P(None, None, "head"), P("head", None), P("ctx", None))
    return jax.shard_map(
        local,
        mesh=mesh,
        in_specs=placed,
        out_specs=(P("ctx", "head"), P("ctx", None, "head"), P("head", "ctx")),
        check_vma=False,
    )
```

```python
import functools

import jax
import jax.numpy as jnp
import numpy as np
from jax import lax
from jax.experimental import pallas as pl
from jax.experimental.pallas import tpu as pltpu
from jax.sharding import PartitionSpec as P

DH = 128
BLK = 16
T = 256
ROWS = 256
NEAR = 2 * BLK
REM = 64
FAR = 96
SCALE = DH**-0.5
BF = jnp.bfloat16
F32 = jnp.float32

STARTS = {1: 0, 2: 128, 3: 192, 4: 224, 5: 240, 6: 248, 7: 252}


def tables():
    spread = np.zeros((T, ROWS), np.float32)
    mean = np.zeros((ROWS, T), np.float32)
    pairs = np.zeros((ROWS, ROWS), np.float32)
    for level, start in STARTS.items():
        factor = 2**level
        for row in range(T // factor):
            spread[row * factor : (row + 1) * factor, start + row] = 1.0
            mean[start + row, row * factor : (row + 1) * factor] = 1.0 / factor
        if level <= 3:
            for block in range(T // factor // BLK):
                other = start + (block ^ 1) * BLK
                mine = start + block * BLK
                pairs[mine : mine + BLK, other : other + BLK] = 1.0
    block_of = np.arange(T) // BLK
    band = (np.abs(block_of[:, None] - block_of[None, :]) <= 1).astype(np.float32)
    rim = np.zeros((T, REM), np.float32)
    rim[:BLK, :BLK] = np.eye(BLK)
    rim[T - BLK :, BLK:NEAR] = np.eye(BLK)
    rim[:, NEAR:] = spread[:, 224:]
    rim_mean = rim.copy()
    rim_mean[:, NEAR:] = mean.T[:, 224:]
    meets = np.zeros((REM, FAR), np.float32)
    meets[0:16, 0:16] = 1.0
    meets[16:32, 16:32] = 1.0
    meets[32:48, 32:48] = 1.0
    meets[48:56, 48:64] = 1.0
    meets[56:60, 64:80] = 1.0
    meets[60:62, 80:96] = 1.0
    bf = lambda array: np.asarray(array, dtype=BF)
    return {
        "spread": bf(spread),
        "gather": bf(spread.T),
        "mean": bf(mean),
        "unmean": bf(mean.T),
        "band": band,
        "pairs": pairs,
        "mean_4": bf(mean[224:240]),
        "rim": bf(rim),
        "rim_mean": bf(rim_mean),
        "unrim": bf(rim.T),
        "meets": meets,
        "met": np.ascontiguousarray(meets.T),
    }


def dot(left, right):
    return jnp.dot(left, right, preferred_element_type=F32)


def dot_nt(left, right):
    return lax.dot_general(left, right, (((1,), (1,)), ((), ())), preferred_element_type=F32)


def dot_tn(left, right):
    return lax.dot_general(left, right, (((0,), (0,)), ((), ())), preferred_element_type=F32)


def dot_two(exact, right):
    high = right.astype(BF)
    low = (right - high.astype(F32)).astype(BF)
    return dot(exact, high) + dot(exact, low)


def normed(values):
    scale = lax.rsqrt(jnp.mean(values * values, axis=-1, keepdims=True) + 1e-06)
    return values * scale, scale


def norm_back(unit, scale, grad):
    return scale * (grad - unit * jnp.mean(grad * unit, axis=-1, keepdims=True))


def head(array, number):
    return array[:, number * DH : (number + 1) * DH]


def with_ones(values):
    return jnp.concatenate([values, jnp.ones_like(values)], axis=1)


def call(kernel, outs, *args, scalars=None, flops=1e9, moved=2e6):
    specs = [pl.BlockSpec(memory_space=pltpu.VMEM)] * len(args)
    if scalars is not None:
        specs = [pl.BlockSpec(memory_space=pltpu.SMEM)] + specs
        args = (scalars,) + args
    return pl.pallas_call(
        kernel,
        out_shape=tuple(jax.ShapeDtypeStruct(shape, dtype) for shape, dtype in outs),
        in_specs=specs,
        out_specs=tuple(pl.BlockSpec(memory_space=pltpu.VMEM) for _ in outs),
        compiler_params=pltpu.CompilerParams(vmem_limit_bytes=44 * 1024 * 1024),
        cost_estimate=pl.CostEstimate(
            flops=int(flops), bytes_accessed=int(moved), transcendentals=0
        ),
    )(*args)


def edges_kernel(pos, tokens, mean, near_out, far_out):
    even = pos[0] % 2 == 0
    first = tokens[:BLK].astype(F32)
    last = tokens[T - BLK :].astype(F32)
    near_out[:BLK] = dot(mean[...], tokens[...]).astype(BF)
    near_out[BLK:] = jnp.where(even, last, first).astype(BF)
    far_out[...] = jnp.where(even, first, last).astype(BF)


def project_kernel(tokens, weights, mean, qkv_out, coarse_out):
    tok = tokens[...]
    parts = [dot(tok, weights[number]).astype(BF) for number in range(3)]
    qkv = jnp.concatenate(parts, axis=1)
    qkv_out[...] = qkv
    coarse_out[...] = dot(mean[...], qkv)


def halved(whole, even):
    width = whole.shape[1] // 32
    halves = [
        jnp.concatenate(
            [whole[:, (2 * j + c) * width : (2 * j + c + 1) * width] for j in range(16)], axis=1
        )
        for c in (0, 1)
    ]
    return jnp.where(even, halves[0], halves[1]), jnp.where(even, halves[1], halves[0])


def d_attn_kernel(pos, grad_out, w_out, tokens, d_attn_out, own_out, other_out):
    d_attn_out[...] = dot_nt(grad_out[...], w_out[...]).astype(BF)
    even = pos[0] % 2 == 0
    for number, array in enumerate((tokens, grad_out)):
        rows = slice(number * T, (number + 1) * T)
        own_out[rows], other_out[rows] = halved(array[...], even)


def merge_kernel(factor, first, second, out):
    row = lax.broadcasted_iota(jnp.int32, (BLK, BLK), 0)
    col = lax.broadcasted_iota(jnp.int32, (BLK, BLK), 1)
    left = jnp.where(col // 2 == row, factor, 0.0).astype(BF)
    right = jnp.where(col // 2 + BLK // 2 == row, factor, 0.0).astype(BF)
    out[...] = (dot(left, first[...]) + dot(right, second[...])).astype(BF)


def local_units(qkv, coarse, number):
    query = head(qkv, number).astype(F32)
    key = head(qkv, 2 + number).astype(F32)
    return (
        normed(query),
        normed(key),
        head(qkv, 4 + number),
        normed(head(coarse, number)),
        normed(head(coarse, 2 + number)),
        head(coarse, 4 + number).astype(BF),
    )


def local_weights(units, band, pairs):
    (qn, _), (kn, _), _, (qc, _), (kc, _), _ = units
    near = jnp.exp(dot_nt(qn.astype(BF), kn.astype(BF)) * SCALE) * band
    far = jnp.exp(dot_nt(qc.astype(BF), kc.astype(BF)) * SCALE) * pairs
    return near, far


def local_forward_kernel(qkv_ref, coarse_ref, band, pairs, spread, out):
    qkv = qkv_ref[...]
    coarse = coarse_ref[...]
    for number in range(2):
        units = local_units(qkv, coarse, number)
        near, far = local_weights(units, band[...], pairs[...])
        total = dot(near.astype(BF), with_ones(units[2]))
        part = dot(far.astype(BF), with_ones(units[5]))
        out[:, number * 2 * DH : (number + 1) * 2 * DH] = total + dot_two(spread[...], part)


def sides(even, near, far):
    left = jnp.where(even, far, near)
    right = jnp.where(even, near, far)
    return left, right


def remote_rows(pos, near, far, level_5, level_6, level_7):
    even = pos[0] % 2 == 0
    arrived = near[...].astype(F32)
    left, right = sides(even, arrived[BLK:], far[...].astype(F32))
    return jnp.concatenate(
        [
            left,
            right,
            arrived[:BLK],
            level_5[...].astype(F32),
            level_6[...].astype(F32),
            level_7[...].astype(F32),
        ],
        axis=0,
    )


def own_rows(fine, coarse):
    return jnp.concatenate([fine[:BLK], fine[T - BLK :], coarse[224:]], axis=0)


def exists(pos, shape, axis):
    where = lax.broadcasted_iota(jnp.int32, shape, axis)
    no_left = jnp.logical_and(pos[0] == 0, where < BLK)
    no_right = jnp.logical_and(pos[0] == 31, jnp.logical_and(where >= BLK, where < NEAR))
    return jnp.where(jnp.logical_or(no_left, no_right), 0.0, 1.0)


def remote_weights(pos, units, remote, meets, number):
    (qn, _), _, _, (qc, _), _, _ = units
    query = own_rows(qn, qc).astype(BF)
    key, key_scale = normed(head(remote, 2 + number))
    value = head(remote, 4 + number).astype(BF)
    weights = jnp.exp(dot_nt(query, key.astype(BF)) * SCALE) * meets * exists(pos, (REM, FAR), 1)
    return weights, query, key, key_scale, value


def remote_forward_kernel(
    pos, weights_ref, qkv_ref, coarse_ref, local_ref, d_attn, near, far, level_5, level_6, level_7,
    meets, rim, gather,
    attn_out, d_num_out, d_den_out, near_out, far_out, remote_out, own_out, other_out,
):
    qkv = qkv_ref[...]
    coarse = coarse_ref[...]
    rows = remote_rows(pos, near, far, level_5, level_6, level_7).astype(BF)
    own_out[...], other_out[...] = halved(rows, pos[0] % 2 == 0)
    remote = jnp.concatenate([dot(rows, weights_ref[part]) for part in range(3)], axis=1)
    remote = remote.astype(BF)
    remote_out[...] = remote
    remote = remote.astype(F32)
    even = pos[0] % 2 == 0
    for number in range(2):
        units = local_units(qkv, coarse, number)
        weights, _, _, _, value = remote_weights(pos, units, remote, meets[...], number)
        part = dot(weights.astype(BF), with_ones(value))
        total = local_ref[:, number * 2 * DH : (number + 1) * 2 * DH] + dot_two(rim[...], part)
        cols = slice(number * DH, (number + 1) * DH)
        inverse = 1.0 / total[:, DH:]
        attn = total[:, :DH] * inverse
        attn_out[:, cols] = attn.astype(BF)
        d_num = (d_attn[:, cols].astype(F32) * inverse).astype(BF)
        d_den = -jnp.sum(d_num.astype(F32) * attn, axis=-1, keepdims=True)
        d_den = jnp.broadcast_to(d_den, (T, DH))
        d_num_out[:, cols] = d_num
        d_den_out[:, cols] = d_den
        sums = dot_two(
            gather[224:240, :], jnp.concatenate([d_num.astype(F32), d_den], axis=1)
        )
        for offset, full, row_sums in (
            (0, d_num.astype(F32), sums[:, :DH]),
            (2 * DH, d_den, sums[:, DH:]),
        ):
            at = slice(offset + number * DH, offset + (number + 1) * DH)
            first = full[:BLK]
            last = full[T - BLK :]
            near_out[:BLK, at] = row_sums.astype(BF)
            near_out[BLK:, at] = jnp.where(even, last, first).astype(BF)
            far_out[:, at] = jnp.where(even, first, last).astype(BF)


def local_backward_kernel(
    pos, qkv_ref, coarse_ref, attn_ref, d_num_ref, d_den_ref, remote_ref,
    meets, unrim, gather, unmean, band, pairs,
    y_out, dkv_out,
):
    qkv = qkv_ref[...]
    coarse = coarse_ref[...]
    remote = remote_ref[...].astype(F32)
    y_out[:T, T:] = attn_ref[...]
    for number in range(2):
        cols = slice(number * DH, (number + 1) * DH)
        vals = slice((2 + number) * DH, (3 + number) * DH)
        units = local_units(qkv, coarse, number)
        (qn, q_scale), (kn, k_scale), value, (qc, qc_scale), (kc, kc_scale), value_c = units
        d_num = d_num_ref[:, cols]
        d_den = d_den_ref[:, cols]
        both = jnp.concatenate([d_num.astype(F32), d_den], axis=1)
        sums = dot_two(gather[...], both)
        d_num_c = sums[:, :DH].astype(BF)
        d_den_c = sums[:, DH : DH + 1]
        near_w, far_w = local_weights(units, band[...], pairs[...])
        d_near = (near_w * (dot_nt(d_num, value) + d_den[:, :1]) * SCALE).astype(BF)
        d_far = (far_w * (dot_nt(d_num_c, value_c) + d_den_c) * SCALE).astype(BF)
        dqn = dot(d_near, kn.astype(BF))
        dqc = dot(d_far, kc.astype(BF))
        weights, query, key_r, key_scale, value_r = remote_weights(
            pos, units, remote, meets[...], number
        )
        sums_r = dot_two(unrim[...], both)
        d_num_r = sums_r[:, :DH].astype(BF)
        d_rem = dot_nt(d_num_r, value_r) + sums_r[:, DH : DH + 1]
        d_rem = (weights * d_rem * SCALE).astype(BF)
        y_out[2 * T :, cols] = norm_back(key_r, key_scale, dot_tn(d_rem, query)).astype(BF)
        y_out[2 * T :, vals] = dot_tn(weights.astype(BF), d_num_r).astype(BF)
        dqr = dot(d_rem, key_r.astype(BF))
        dqn = jnp.concatenate(
            [dqn[:BLK] + dqr[:BLK], dqn[BLK : T - BLK], dqn[T - BLK :] + dqr[BLK:NEAR]], axis=0
        )
        dqc = jnp.concatenate([dqc[:224], dqc[224:] + dqr[NEAR:]], axis=0)
        table = jnp.concatenate(
            [
                norm_back(qc, qc_scale, dqc),
                norm_back(kc, kc_scale, dot_tn(d_far, qc.astype(BF))),
                dot_tn(far_w.astype(BF), d_num_c),
            ],
            axis=1,
        )
        table = dot_two(unmean[...], table)
        y_out[:T, cols] = (norm_back(qn, q_scale, dqn) + table[:, :DH]).astype(BF)
        dk = norm_back(kn, k_scale, dot_tn(d_near, qn.astype(BF))) + table[:, DH : 2 * DH]
        dv = dot_tn(near_w.astype(BF), d_num) + table[:, 2 * DH :]
        dkv_out[:, cols] = dk
        dkv_out[:, vals] = dv
        y_out[T : 2 * T, cols] = dk.astype(BF)
        y_out[T : 2 * T, vals] = dv.astype(BF)


def remote_backward_kernel(
    pos, qkv_ref, coarse_ref, local_ref, remote_ref, g_near, g_far, g_5, g_6, g_7,
    met, rim_mean, dkv_out,
):
    qkv = qkv_ref[...]
    coarse = coarse_ref[...]
    remote = remote_ref[...].astype(F32)
    grads = remote_rows(pos, g_near, g_far, g_5, g_6, g_7)
    for number in range(2):
        units = local_units(qkv, coarse, number)
        _, (kn, k_scale), value, _, (kc, kc_scale), value_c = units
        query = normed(head(remote, number))[0].astype(BF)
        key = own_rows(kn, kc)
        key_scale = own_rows(k_scale, kc_scale)
        vals = own_rows(value.astype(F32), value_c.astype(F32)).astype(BF)
        weights = jnp.exp(dot_nt(query, key.astype(BF)) * SCALE)
        weights = weights * met[...] * exists(pos, (FAR, REM), 0)
        d_num = head(grads, number).astype(BF)
        d_den = head(grads, 2 + number)[:, :1]
        d_score = (weights * (dot_nt(d_num, vals) + d_den) * SCALE).astype(BF)
        dk = norm_back(key, key_scale, dot_tn(d_score, query))
        dv = dot_tn(weights.astype(BF), d_num)
        more = dot_two(rim_mean[...], jnp.concatenate([dk, dv], axis=1))
        k_cols = slice(number * DH, (number + 1) * DH)
        v_cols = slice((2 + number) * DH, (3 + number) * DH)
        dkv_out[:, k_cols] = (local_ref[:, k_cols] + more[:, :DH]).astype(BF)
        dkv_out[:, v_cols] = (local_ref[:, v_cols] + more[:, DH:]).astype(BF)


def weight_kernel(pos, own_half, own_far, own, other_half, other_far, other, *outs):
    z = pos[0] // 4
    width = own_half.shape[1] // 8
    for step in range(8):
        at = pl.ds(pl.multiple_of((z + step) % 8 * width, width), width)
        for rows, y_rows, x_cols, y_cols in (
            (slice(0, T), slice(0, T), slice(0, T), slice(0, T)),
            (slice(T, 2 * T), slice(0, T), slice(T, 2 * T), slice(T, 2 * T)),
            (slice(0, T), slice(T, 2 * T), slice(2 * T, 4 * T), slice(0, 2 * T)),
        ):
            total = dot_tn(own_half[rows, at], own[y_rows, y_cols])
            total += dot_tn(other_half[rows, at], other[y_rows, y_cols])
            if y_rows.start == T:
                total += dot_tn(own_far[:, at], own[2 * T :, :])
                total += dot_tn(other_far[:, at], other[2 * T :, :])
            outs[step][:, x_cols] = total.astype(BF)


def add_kernel(*refs):
    count = len(refs) // 3
    for number in range(count):
        total = refs[2 * number][...].astype(F32) + refs[2 * number + 1][...].astype(F32)
        refs[2 * count + number][...] = total.astype(BF)


def sum_z_kernel(pos, *refs):
    keep, send = refs[-2:]
    total = refs[0][...].astype(F32)
    for ref in refs[1:-2]:
        total = total + ref[...].astype(F32)
    half = total.shape[0] // 2
    low = pos[0] // 2 % 2 == 0
    keep[...] = jnp.where(low, total[:half], total[half:])
    send[...] = jnp.where(low, total[half:], total[:half]).astype(BF)


def finish_kernel(keep, came, w_qkv, w_out):
    total = keep[...] + came[...].astype(F32)
    w_qkv[0] = total[:, :T]
    w_qkv[1] = total[:, 2 * T : 3 * T]
    w_qkv[2] = total[:, 3 * T :]
    w_out[...] = total[:, T : 2 * T]


def grad_x_kernel(pos, y, dkv, weights, *outs):
    x = pos[1] % 4
    side = pos[1] // 4
    for step in range(4):
        for turn in range(2):
            target = (side + turn) % 2 * 4 + (x + step) % 4
            rows = pl.ds(pl.multiple_of(target * T, T), T)
            total = dot_nt(y[:T, :T], weights[0, rows, :])
            total += dot_nt(dkv[:, :T], weights[1, rows, :])
            total += dot_nt(dkv[:, T:], weights[2, rows, :])
            outs[step][turn * T : (turn + 1) * T] = total.astype(BF)


def sum_x_kernel(first, second, third, keep, send):
    total = first[...].astype(F32) + second[...].astype(F32) + third[...].astype(F32)
    keep[...] = total[:T]
    send[...] = total[T:].astype(BF)


def last_x_kernel(keep, came, out):
    out[...] = (keep[...] + came[...].astype(F32)).astype(BF)


def local(tokens, w_qkv, w_out, grad_out):
    const = {name: jnp.asarray(array) for name, array in tables().items()}
    head_count = lax.axis_size("head")
    pos = jnp.stack([lax.axis_index("ctx"), lax.axis_index("head")]).astype(jnp.int32)
    weights = jnp.transpose(w_qkv, (1, 0, 2))
    width = tokens.shape[1]
    wide = 3 * T

    def swap(array, bit):
        return lax.ppermute(array, "ctx", [(i, i ^ bit) for i in range(32)])

    def chain(array):
        pairs = [(i, i + 1) for i in range(1, 31, 2)]
        return lax.ppermute(array, "ctx", pairs + [(b, a) for a, b in pairs])

    def turn_z(array, step):
        return lax.ppermute(
            array, "ctx", [(i, (i // 4 + step) % 8 * 4 + i % 4) for i in range(32)]
        )

    def add(*pairs):
        shapes = [(pair[0].shape, BF) for pair in pairs]
        return call(add_kernel, shapes, *[array for pair in pairs for array in pair], flops=1e8)

    def exchange(near, far, factor):
        arrived = swap(near, 1)
        other = chain(far)
        shape = [((BLK, near.shape[1]), BF)]
        merge = functools.partial(merge_kernel, factor)
        (block_5,) = call(merge, shape, near[:BLK], arrived[:BLK])
        level_5 = swap(block_5, 2)
        (block_6,) = call(merge, shape, block_5, level_5)
        level_6 = swap(block_6, 4)
        (block_7,) = call(merge, shape, block_6, level_6)
        level_7 = swap(block_7, 8)
        return arrived, other, level_5, level_6, level_7

    near, far = call(
        edges_kernel, [((NEAR, width), BF), ((BLK, width), BF)],
        tokens, const["mean_4"], scalars=pos,
    )
    gathered = exchange(near, far, 0.5)
    qkv, coarse = call(
        project_kernel, [((T, wide), BF), ((ROWS, wide), F32)], tokens, weights, const["mean"]
    )
    d_attn, own_half, other_half = call(
        d_attn_kernel,
        [((T, T), BF), ((2 * T, width // 2), BF), ((2 * T, width // 2), BF)],
        grad_out, w_out, tokens, scalars=pos,
    )
    sent_half = swap(other_half, 1)
    (forward,) = call(
        local_forward_kernel, [((T, 2 * T), F32)],
        qkv, coarse, const["band"], const["pairs"], const["spread"],
    )
    attn, d_num, d_den, g_near, g_far, remote, own_far, other_far = call(
        remote_forward_kernel,
        [
            ((T, T), BF), ((T, T), BF), ((T, T), F32), ((NEAR, 2 * T), BF), ((BLK, 2 * T), BF),
            ((FAR, wide), BF), ((FAR, width // 2), BF), ((FAR, width // 2), BF),
        ],
        weights, qkv, coarse, forward, d_attn, *gathered, const["meets"], const["rim"],
        const["gather"], scalars=pos,
    )
    grads = exchange(g_near, g_far, 1.0)
    sent_far = swap(other_far, 1)
    y, dkv_local = call(
        local_backward_kernel, [((2 * T + FAR, 2 * T), BF), ((T, 2 * T), F32)],
        qkv, coarse, attn, d_num, d_den, remote, const["meets"], const["unrim"], const["gather"],
        const["unmean"], const["band"], const["pairs"], scalars=pos,
    )
    chunk = width // 16
    parts = call(
        weight_kernel, [((chunk, 4 * T), BF)] * 8,
        own_half, own_far, y, sent_half, sent_far, swap(y, 1), scalars=pos,
    )
    up = turn_z(parts[4], 1)
    down = turn_z(parts[5], -1)
    for step in (3, 2):
        next_up, next_down = add((up, parts[step]), (down, parts[9 - step]))
        up = turn_z(next_up, 1)
        down = turn_z(next_down, -1)
    (next_up,) = add((up, parts[1]))
    up = turn_z(next_up, 1)
    keep, send = call(
        sum_z_kernel, [((chunk // 2, 4 * T), F32), ((chunk // 2, 4 * T), BF)],
        parts[0], up, down, scalars=pos,
    )
    came = swap(send, 2)
    grad_wqkv, grad_wout = call(
        finish_kernel, [((3, chunk // 2, T), F32), ((chunk // 2, T), F32)], keep, came
    )
    (dkv,) = call(
        remote_backward_kernel, [((T, 2 * T), BF)],
        qkv, coarse, dkv_local, remote, *grads, const["met"], const["rim_mean"], scalars=pos,
    )
    if head_count == 8:
        pieces = call(grad_x_kernel, [((2 * T, T), BF)] * 4, y, dkv, weights, scalars=pos)

        def turn_x(array, step):
            pairs = [(i, i // 4 * 4 + (i % 4 + step) % 4) for i in range(8)]
            return lax.ppermute(array, "head", pairs)

        left = turn_x(pieces[3], -1)
        (next_right,) = add((turn_x(pieces[2], 1), pieces[1]))
        right = turn_x(next_right, 1)
        keep_x, send_x = call(
            sum_x_kernel, [((T, T), F32), ((T, T), BF)], pieces[0], left, right
        )
        came_x = lax.ppermute(send_x, "head", [(i, i ^ 4) for i in range(8)])
        (grad_x,) = call(last_x_kernel, [((T, T), BF)], keep_x, came_x)
    else:
        flat = jnp.transpose(weights, (1, 0, 2)).reshape(width, wide)
        grad_x = dot_nt(jnp.concatenate([y[:T, :T], dkv], axis=1), flat).astype(BF)
    return grad_x, jnp.transpose(grad_wqkv, (1, 0, 2)), grad_wout.T


def solution(mesh):
    placed = (P("ctx", None), P(None, None, "head"), P("head", None), P("ctx", None))
    return jax.shard_map(
        local,
        mesh=mesh,
        in_specs=placed,
        out_specs=(P("ctx", "head"), P("ctx", None, "head"), P("head", "ctx")),
        check_vma=False,
    )
```

```python
import functools

import jax
import jax.numpy as jnp
import numpy as np
from jax import lax
from jax.experimental import pallas as pl
from jax.experimental.pallas import tpu as pltpu
from jax.sharding import PartitionSpec as P

DH = 128
BLK = 16
T = 256
ROWS = 256
NEAR = 2 * BLK
REM = 64
FAR = 96
SCALE = DH**-0.5
BF = jnp.bfloat16
F32 = jnp.float32

STARTS = {1: 0, 2: 128, 3: 192, 4: 224, 5: 240, 6: 248, 7: 252}


def tables():
    spread = np.zeros((T, ROWS), np.float32)
    mean = np.zeros((ROWS, T), np.float32)
    pairs = np.zeros((ROWS, ROWS), np.float32)
    for level, start in STARTS.items():
        factor = 2**level
        for row in range(T // factor):
            spread[row * factor : (row + 1) * factor, start + row] = 1.0
            mean[start + row, row * factor : (row + 1) * factor] = 1.0 / factor
        if level <= 3:
            for block in range(T // factor // BLK):
                other = start + (block ^ 1) * BLK
                mine = start + block * BLK
                pairs[mine : mine + BLK, other : other + BLK] = 1.0
    block_of = np.arange(T) // BLK
    band = (np.abs(block_of[:, None] - block_of[None, :]) <= 1).astype(np.float32)
    rim = np.zeros((T, REM), np.float32)
    rim[:BLK, :BLK] = np.eye(BLK)
    rim[T - BLK :, BLK:NEAR] = np.eye(BLK)
    rim[:, NEAR:] = spread[:, 224:]
    rim_mean = rim.copy()
    rim_mean[:, NEAR:] = mean.T[:, 224:]
    meets = np.zeros((REM, FAR), np.float32)
    meets[0:16, 0:16] = 1.0
    meets[16:32, 16:32] = 1.0
    meets[32:48, 32:48] = 1.0
    meets[48:56, 48:64] = 1.0
    meets[56:60, 64:80] = 1.0
    meets[60:62, 80:96] = 1.0
    bf = lambda array: np.asarray(array, dtype=BF)
    return {
        "spread": bf(spread),
        "gather": bf(spread.T),
        "mean": bf(mean),
        "unmean": bf(mean.T),
        "band": band,
        "pairs": pairs,
        "rim": bf(rim),
        "rim_mean": bf(rim_mean),
        "unrim": bf(rim.T),
        "meets": meets,
        "met": np.ascontiguousarray(meets.T),
    }


def dot(left, right):
    return jnp.dot(left, right, preferred_element_type=F32)


def dot_nt(left, right):
    return lax.dot_general(left, right, (((1,), (1,)), ((), ())), preferred_element_type=F32)


def dot_tn(left, right):
    return lax.dot_general(left, right, (((0,), (0,)), ((), ())), preferred_element_type=F32)


def dot_two(exact, right):
    high = right.astype(BF)
    low = (right - high.astype(F32)).astype(BF)
    return dot(exact, high) + dot(exact, low)


def normed(values):
    scale = lax.rsqrt(jnp.mean(values * values, axis=-1, keepdims=True) + 1e-06)
    return values * scale, scale


def norm_back(unit, scale, grad):
    return scale * (grad - unit * jnp.mean(grad * unit, axis=-1, keepdims=True))


def head(array, number):
    return array[:, number * DH : (number + 1) * DH]


def with_ones(values):
    return jnp.concatenate([values, jnp.ones_like(values)], axis=1)


class Calls:
    def __init__(self):
        self.token = None

    def __call__(self, kernel, outs, *args, scalars=None, flops=1e9, moved=2e6):
        specs = [pl.BlockSpec(memory_space=pltpu.VMEM)] * len(args)
        skipped = 0
        if scalars is not None:
            specs = [pl.BlockSpec(memory_space=pltpu.SMEM)] + specs
            args = (scalars,) + args
        if self.token is not None:
            specs = [pl.BlockSpec(memory_space=pltpu.VMEM)] + specs
            args = (self.token,) + args
            skipped = 1

        def body(*refs):
            kernel(*refs[skipped:-1])

        shapes = [jax.ShapeDtypeStruct(shape, dtype) for shape, dtype in outs]
        shapes.append(jax.ShapeDtypeStruct((8, 128), F32))
        results = pl.pallas_call(
            body,
            out_shape=tuple(shapes),
            in_specs=specs,
            out_specs=tuple(pl.BlockSpec(memory_space=pltpu.VMEM) for _ in shapes),
            compiler_params=pltpu.CompilerParams(vmem_limit_bytes=44 * 1024 * 1024),
            cost_estimate=pl.CostEstimate(
                flops=int(flops), bytes_accessed=int(moved), transcendentals=0
            ),
        )(*args)
        self.token = results[-1]
        return results[:-1]


def packed(rows):
    half = rows.shape[1] // 2
    return jnp.concatenate([rows[:, :half], rows[:, half:]], axis=0)


def unpacked(rows):
    half = rows.shape[0] // 2
    return jnp.concatenate([rows[:half], rows[half:]], axis=1)


def edges_kernel(pos, tokens, near_out, far_out, level_5_out):
    even = pos[0] % 2 == 0
    row = lax.broadcasted_iota(jnp.int32, (BLK, T), 0)
    col = lax.broadcasted_iota(jnp.int32, (BLK, T), 1)
    mean = dot(jnp.where(col // BLK == row, 1.0 / BLK, 0.0).astype(BF), tokens[...])
    row = lax.broadcasted_iota(jnp.int32, (8, T), 0)
    col = lax.broadcasted_iota(jnp.int32, (8, T), 1)
    wide = dot(jnp.where(col // NEAR == row, 1.0 / NEAR, 0.0).astype(BF), tokens[...])
    first = tokens[:BLK].astype(F32)
    last = tokens[T - BLK :].astype(F32)
    near_out[:BLK] = mean.astype(BF)
    near_out[BLK:] = jnp.where(even, last, first).astype(BF)
    far_out[...] = jnp.where(even, first, last).astype(BF)
    level_5_out[...] = packed(wide).astype(BF)


def project_kernel(tokens, weights, mean, qkv_out, coarse_out):
    tok = tokens[...]
    parts = [dot(tok, weights[number]).astype(BF) for number in range(3)]
    qkv = jnp.concatenate(parts, axis=1)
    qkv_out[...] = qkv
    coarse_out[...] = dot(mean[...], qkv)


def half_of_rows(whole, number):
    width = whole.shape[0] // 32
    return jnp.concatenate(
        [whole[(2 * j + number) * width : (2 * j + number + 1) * width] for j in range(16)], axis=0
    )


def d_attn_kernel(pos, grad_out, w_out, tokens, d_attn_out, own_out, other_out):
    d_attn_out[...] = dot_nt(grad_out[...], w_out[...]).astype(BF)
    even = pos[0] % 2 == 0
    for number, array in enumerate((tokens, grad_out)):
        cols = slice(number * T, (number + 1) * T)
        turned = array[...].T
        halves = half_of_rows(turned, 0), half_of_rows(turned, 1)
        own_out[:, cols] = jnp.where(even, halves[0], halves[1])
        other_out[:, cols] = jnp.where(even, halves[1], halves[0])


def merged(factor, first, second):
    row = lax.broadcasted_iota(jnp.int32, (BLK, BLK), 0)
    col = lax.broadcasted_iota(jnp.int32, (BLK, BLK), 1)
    same = row // 8 == col // 8
    source = col % 8 // 2
    left = jnp.where(jnp.logical_and(same, source == row % 8), factor, 0.0).astype(BF)
    right = jnp.where(jnp.logical_and(same, source + 4 == row % 8), factor, 0.0).astype(BF)
    return (dot(left, first) + dot(right, second)).astype(BF)


def merge_kernel(factor, first, second, out):
    out[...] = merged(factor, first[...], second[...])


def bundle_kernel(factor, level_5, level_6, third, fourth, *rest):
    out = rest[-1]
    out[:BLK] = level_5[...]
    out[BLK : 2 * BLK] = level_6[...]
    out[2 * BLK : 3 * BLK] = merged(factor, third[...], fourth[...])
    if len(rest) > 1:
        out[3 * BLK :] = packed(rest[0][...].astype(F32)).astype(BF)


def local_units(qkv, coarse, number):
    query = head(qkv, number).astype(F32)
    key = head(qkv, 2 + number).astype(F32)
    return (
        normed(query),
        normed(key),
        head(qkv, 4 + number),
        normed(head(coarse, number)),
        normed(head(coarse, 2 + number)),
        head(coarse, 4 + number).astype(BF),
    )


def local_weights(units, band, pairs):
    (qn, _), (kn, _), _, (qc, _), (kc, _), _ = units
    near = jnp.exp(dot_nt(qn.astype(BF), kn.astype(BF)) * SCALE) * band
    far = jnp.exp(dot_nt(qc.astype(BF), kc.astype(BF)) * SCALE) * pairs
    return near, far


def local_forward_kernel(qkv_ref, coarse_ref, band, pairs, spread, out):
    qkv = qkv_ref[...]
    coarse = coarse_ref[...]
    for number in range(2):
        units = local_units(qkv, coarse, number)
        near, far = local_weights(units, band[...], pairs[...])
        total = dot(near.astype(BF), with_ones(units[2]))
        part = dot(far.astype(BF), with_ones(units[5]))
        out[:, number * 2 * DH : (number + 1) * 2 * DH] = total + dot_two(spread[...], part)


def remote_rows(pos, arrived_ref, far_ref, mine_ref, theirs_ref):
    even = pos[0] % 2 == 0
    arrived = arrived_ref[...].astype(F32)
    far = far_ref[...].astype(F32)
    mine = mine_ref[...].astype(F32)
    theirs = theirs_ref[...].astype(F32)
    left = jnp.where(even, far, arrived[BLK:])
    right = jnp.where(even, arrived[BLK:], far)
    rows = [left, right, arrived[:BLK]]
    for level in range(3):
        at = slice(level * BLK, (level + 1) * BLK)
        ours, others = unpacked(mine[at]), unpacked(theirs[at])
        rows += [jnp.where(even, ours, others), jnp.where(even, others, ours)]
    return jnp.concatenate(rows, axis=0)


def own_rows(fine, coarse):
    return jnp.concatenate([fine[:BLK], fine[T - BLK :], coarse[224:]], axis=0)


def exists(pos, shape, axis):
    where = lax.broadcasted_iota(jnp.int32, shape, axis)
    no_left = jnp.logical_and(pos[0] == 0, where < BLK)
    no_right = jnp.logical_and(pos[0] == 31, jnp.logical_and(where >= BLK, where < NEAR))
    return jnp.where(jnp.logical_or(no_left, no_right), 0.0, 1.0)


def remote_weights(pos, units, remote, meets, number):
    (qn, _), _, _, (qc, _), _, _ = units
    query = own_rows(qn, qc).astype(BF)
    key, key_scale = normed(head(remote, 2 + number))
    value = head(remote, 4 + number).astype(BF)
    weights = jnp.exp(dot_nt(query, key.astype(BF)) * SCALE) * meets * exists(pos, (REM, FAR), 1)
    return weights, query, key, key_scale, value


def remote_forward_kernel(
    pos, weights_ref, qkv_ref, coarse_ref, local_ref, d_attn, near, arrived, far, mine, theirs,
    meets, rim, gather,
    attn_out, d_num_out, d_den_out, near_out, far_out, level_5_out, remote_out, own_out, other_out,
):
    qkv = qkv_ref[...]
    coarse = coarse_ref[...]
    rows = remote_rows(pos, arrived, far, mine, theirs)
    even = pos[0] % 2 == 0
    known = near[...].astype(F32)
    partner = unpacked(theirs[3 * BLK :].astype(F32))
    other = jnp.concatenate(
        [
            jnp.where(even, known[BLK:], partner),
            jnp.where(even, partner, known[BLK:]),
            known[:BLK],
            rows[3 * BLK :],
        ],
        axis=0,
    )
    for array, out in ((rows, own_out), (other, other_out)):
        turned = array.T
        out[...] = jnp.where(even, half_of_rows(turned, 0), half_of_rows(turned, 1)).astype(BF)
    rows = rows.astype(BF)
    remote = jnp.concatenate([dot(rows, weights_ref[part]) for part in range(3)], axis=1)
    remote = remote.astype(BF)
    remote_out[...] = remote
    remote = remote.astype(F32)
    wide = [None] * 4
    for number in range(2):
        units = local_units(qkv, coarse, number)
        weights, _, _, _, value = remote_weights(pos, units, remote, meets[...], number)
        part = dot(weights.astype(BF), with_ones(value))
        total = local_ref[:, number * 2 * DH : (number + 1) * 2 * DH] + dot_two(rim[...], part)
        cols = slice(number * DH, (number + 1) * DH)
        inverse = 1.0 / total[:, DH:]
        attn = total[:, :DH] * inverse
        attn_out[:, cols] = attn.astype(BF)
        d_num = (d_attn[:, cols].astype(F32) * inverse).astype(BF)
        d_den = -jnp.sum(d_num.astype(F32) * attn, axis=-1, keepdims=True)
        d_den = jnp.broadcast_to(d_den, (T, DH))
        d_num_out[:, cols] = d_num
        d_den_out[:, cols] = d_den
        sums = dot_two(
            gather[224:256, :], jnp.concatenate([d_num.astype(F32), d_den], axis=1)
        )
        for offset, full, row_sums in (
            (0, d_num.astype(F32), sums[:, :DH]),
            (2 * DH, d_den, sums[:, DH:]),
        ):
            at = slice(offset + number * DH, offset + (number + 1) * DH)
            first = full[:BLK]
            last = full[T - BLK :]
            near_out[:BLK, at] = row_sums[:BLK].astype(BF)
            wide[offset // DH + number] = row_sums[BLK : BLK + 8]
            near_out[BLK:, at] = jnp.where(even, last, first).astype(BF)
            far_out[:, at] = jnp.where(even, first, last).astype(BF)
    level_5_out[...] = packed(jnp.concatenate(wide, axis=1)).astype(BF)


def local_backward_kernel(
    pos, qkv_ref, coarse_ref, attn_ref, d_num_ref, d_den_ref, remote_ref,
    meets, unrim, gather, unmean, band, pairs,
    y_out, dkv_out,
):
    qkv = qkv_ref[...]
    coarse = coarse_ref[...]
    remote = remote_ref[...].astype(F32)
    y_out[:T, T:] = attn_ref[...]
    for number in range(2):
        cols = slice(number * DH, (number + 1) * DH)
        vals = slice((2 + number) * DH, (3 + number) * DH)
        units = local_units(qkv, coarse, number)
        (qn, q_scale), (kn, k_scale), value, (qc, qc_scale), (kc, kc_scale), value_c = units
        d_num = d_num_ref[:, cols]
        d_den = d_den_ref[:, cols]
        both = jnp.concatenate([d_num.astype(F32), d_den], axis=1)
        sums = dot_two(gather[...], both)
        d_num_c = sums[:, :DH].astype(BF)
        d_den_c = sums[:, DH : DH + 1]
        near_w, far_w = local_weights(units, band[...], pairs[...])
        d_near = (near_w * (dot_nt(d_num, value) + d_den[:, :1]) * SCALE).astype(BF)
        d_far = (far_w * (dot_nt(d_num_c, value_c) + d_den_c) * SCALE).astype(BF)
        dqn = dot(d_near, kn.astype(BF))
        dqc = dot(d_far, kc.astype(BF))
        weights, query, key_r, key_scale, value_r = remote_weights(
            pos, units, remote, meets[...], number
        )
        sums_r = dot_two(unrim[...], both)
        d_num_r = sums_r[:, :DH].astype(BF)
        d_rem = dot_nt(d_num_r, value_r) + sums_r[:, DH : DH + 1]
        d_rem = (weights * d_rem * SCALE).astype(BF)
        y_out[2 * T :, cols] = norm_back(key_r, key_scale, dot_tn(d_rem, query)).astype(BF)
        y_out[2 * T :, vals] = dot_tn(weights.astype(BF), d_num_r).astype(BF)
        dqr = dot(d_rem, key_r.astype(BF))
        dqn = jnp.concatenate(
            [dqn[:BLK] + dqr[:BLK], dqn[BLK : T - BLK], dqn[T - BLK :] + dqr[BLK:NEAR]], axis=0
        )
        dqc = jnp.concatenate([dqc[:224], dqc[224:] + dqr[NEAR:]], axis=0)
        table = jnp.concatenate(
            [
                norm_back(qc, qc_scale, dqc),
                norm_back(kc, kc_scale, dot_tn(d_far, qc.astype(BF))),
                dot_tn(far_w.astype(BF), d_num_c),
            ],
            axis=1,
        )
        table = dot_two(unmean[...], table)
        y_out[:T, cols] = (norm_back(qn, q_scale, dqn) + table[:, :DH]).astype(BF)
        dk = norm_back(kn, k_scale, dot_tn(d_near, qn.astype(BF))) + table[:, DH : 2 * DH]
        dv = dot_tn(near_w.astype(BF), d_num) + table[:, 2 * DH :]
        dkv_out[:, cols] = dk
        dkv_out[:, vals] = dv
        y_out[T : 2 * T, cols] = dk.astype(BF)
        y_out[T : 2 * T, vals] = dv.astype(BF)


def remote_backward_kernel(
    pos, qkv_ref, coarse_ref, local_ref, remote_ref, g_near, g_far, g_mine, g_theirs,
    met, rim_mean, dkv_out,
):
    qkv = qkv_ref[...]
    coarse = coarse_ref[...]
    remote = remote_ref[...].astype(F32)
    grads = remote_rows(pos, g_near, g_far, g_mine, g_theirs)
    for number in range(2):
        units = local_units(qkv, coarse, number)
        _, (kn, k_scale), value, _, (kc, kc_scale), value_c = units
        query = normed(head(remote, number))[0].astype(BF)
        key = own_rows(kn, kc)
        key_scale = own_rows(k_scale, kc_scale)
        vals = own_rows(value.astype(F32), value_c.astype(F32)).astype(BF)
        weights = jnp.exp(dot_nt(query, key.astype(BF)) * SCALE)
        weights = weights * met[...] * exists(pos, (FAR, REM), 0)
        d_num = head(grads, number).astype(BF)
        d_den = head(grads, 2 + number)[:, :1]
        d_score = (weights * (dot_nt(d_num, vals) + d_den) * SCALE).astype(BF)
        dk = norm_back(key, key_scale, dot_tn(d_score, query))
        dv = dot_tn(weights.astype(BF), d_num)
        more = dot_two(rim_mean[...], jnp.concatenate([dk, dv], axis=1))
        k_cols = slice(number * DH, (number + 1) * DH)
        v_cols = slice((2 + number) * DH, (3 + number) * DH)
        dkv_out[:, k_cols] = (local_ref[:, k_cols] + more[:, :DH]).astype(BF)
        dkv_out[:, v_cols] = (local_ref[:, v_cols] + more[:, DH:]).astype(BF)


def weight_kernel(early, pos, own_half, other_half, own, other, *rest):
    outs = rest[-8:]
    z = pos[0] // 4
    width = own_half.shape[0] // 8
    for step in range(8):
        at = pl.ds(pl.multiple_of((z + step) % 8 * width, width), width)
        if early:
            for cols in (slice(0, T), slice(T, 2 * T)):
                total = dot(own_half[at, cols], own[:T, cols])
                total += dot(other_half[at, cols], other[:T, cols])
                outs[step][:, cols] = total.astype(BF)
        else:
            own_far, other_far = rest[:2]
            total = dot(own_half[at, :T], own[T : 2 * T]) + dot(own_far[at, :], own[2 * T :])
            total += dot(other_half[at, :T], other[T : 2 * T])
            total += dot(other_far[at, :], other[2 * T :])
            outs[step][...] = total.astype(BF)


def add_kernel(*refs):
    count = len(refs) // 3
    for number in range(count):
        total = refs[2 * number][...].astype(F32) + refs[2 * number + 1][...].astype(F32)
        refs[2 * count + number][...] = total.astype(BF)


def sum_z_kernel(pos, *refs):
    keep, send = refs[-2:]
    low = pos[0] // 2 % 2 == 0
    width = refs[0].shape[1]
    for number in range((len(refs) - 2) // 3):
        total = refs[3 * number][...].astype(F32)
        for ref in refs[3 * number + 1 : 3 * number + 3]:
            total = total + ref[...].astype(F32)
        half = total.shape[0] // 2
        cols = slice(number * width, (number + 1) * width)
        keep[:, cols] = jnp.where(low, total[:half], total[half:])
        send[:, cols] = jnp.where(low, total[half:], total[:half]).astype(BF)


def finish_kernel(keep, came, w_qkv, w_out):
    total = keep[...] + came[...].astype(F32)
    w_qkv[0] = total[:, :T]
    w_qkv[1] = total[:, 2 * T : 3 * T]
    w_qkv[2] = total[:, 3 * T :]
    w_out[...] = total[:, T : 2 * T]


def grad_x_kernel(pos, y, dkv, weights, *outs):
    x = pos[1] % 4
    side = pos[1] // 4
    for step in range(4):
        for turn in range(2):
            target = (side + turn) % 2 * 4 + (x + step) % 4
            rows = pl.ds(pl.multiple_of(target * T, T), T)
            total = dot_nt(y[:T, :T], weights[0, rows, :])
            total += dot_nt(dkv[:, :T], weights[1, rows, :])
            total += dot_nt(dkv[:, T:], weights[2, rows, :])
            outs[step][turn * T : (turn + 1) * T] = total.astype(BF)


def sum_x_kernel(first, second, third, keep, send):
    total = first[...].astype(F32) + second[...].astype(F32) + third[...].astype(F32)
    keep[...] = total[:T]
    send[...] = total[T:].astype(BF)


def last_x_kernel(keep, came, out):
    out[...] = (keep[...] + came[...].astype(F32)).astype(BF)


def local(tokens, w_qkv, w_out, grad_out):
    const = {name: jnp.asarray(array) for name, array in tables().items()}
    head_count = lax.axis_size("head")
    pos = jnp.stack([lax.axis_index("ctx"), lax.axis_index("head")]).astype(jnp.int32)
    weights = jnp.transpose(w_qkv, (1, 0, 2))
    width = tokens.shape[1]
    wide = 3 * T

    def swap(array, bit):
        return lax.ppermute(array, "ctx", [(i, i ^ bit) for i in range(32)])

    def chain(array):
        pairs = [(i, i + 1) for i in range(1, 31, 2)]
        return lax.ppermute(array, "ctx", pairs + [(b, a) for a, b in pairs])

    def turn_z(array, step):
        return lax.ppermute(
            array, "ctx", [(i, (i // 4 + step) % 8 * 4 + i % 4) for i in range(32)]
        )

    def add(*pairs):
        shapes = [(pair[0].shape, BF) for pair in pairs]
        return call(add_kernel, shapes, *[array for pair in pairs for array in pair], flops=1e8)

    call = Calls()

    near, far, level_5 = call(
        edges_kernel, [((NEAR, width), BF), ((BLK, width), BF), ((BLK, width // 2), BF)],
        tokens, scalars=pos,
    )
    side = swap(level_5, 2)
    arrived = swap(near, 1)
    chained = chain(far)
    d_attn, own_half, other_half = call(
        d_attn_kernel,
        [((T, T), BF), ((width // 2, 2 * T), BF), ((width // 2, 2 * T), BF)],
        grad_out, w_out, tokens, scalars=pos,
    )
    (level_6,) = call(
        functools.partial(merge_kernel, 0.5), [((BLK, width // 2), BF)], level_5, side
    )
    sixes = [swap(level_6, bit) for bit in (4, 8, 12)]
    sent_half = swap(other_half, 1)
    qkv, coarse = call(
        project_kernel, [((T, wide), BF), ((ROWS, wide), F32)], tokens, weights, const["mean"]
    )
    (forward,) = call(
        local_forward_kernel, [((T, 2 * T), F32)],
        qkv, coarse, const["band"], const["pairs"], const["spread"],
    )
    (mine,) = call(
        functools.partial(bundle_kernel, 0.5), [((5 * BLK, width // 2), BF)],
        side, *sixes, chained,
    )
    theirs = swap(mine, 1)
    attn, d_num, d_den, g_near, g_far, g_5, remote, own_far, other_far = call(
        remote_forward_kernel,
        [
            ((T, T), BF), ((T, T), BF), ((T, T), F32), ((NEAR, 2 * T), BF), ((BLK, 2 * T), BF),
            ((BLK, T), BF), ((FAR, wide), BF), ((width // 2, FAR), BF), ((width // 2, FAR), BF),
        ],
        weights, qkv, coarse, forward, d_attn, near, arrived, chained, mine, theirs,
        const["meets"], const["rim"], const["gather"], scalars=pos,
    )
    g_side = swap(g_5, 2)
    g_arrived = swap(g_near, 1)
    g_chained = chain(g_far)
    y, dkv_local = call(
        local_backward_kernel, [((2 * T + FAR, 2 * T), BF), ((T, 2 * T), F32)],
        qkv, coarse, attn, d_num, d_den, remote, const["meets"], const["unrim"], const["gather"],
        const["unmean"], const["band"], const["pairs"], scalars=pos,
    )
    other_y = swap(y, 1)
    (g_6,) = call(functools.partial(merge_kernel, 1.0), [((BLK, T), BF)], g_5, g_side)
    g_sixes = [swap(g_6, bit) for bit in (4, 8, 12)]
    chunk = width // 16
    shapes = [((chunk, 2 * T), BF)] * 8
    parts_1 = call(
        functools.partial(weight_kernel, True), shapes,
        own_half, sent_half, y, other_y, scalars=pos,
    )
    up_1, down_1 = turn_z(parts_1[4], 1), turn_z(parts_1[5], -1)
    parts_2 = call(
        functools.partial(weight_kernel, False), shapes,
        own_half, sent_half, y, other_y, own_far, other_far, scalars=pos,
    )
    up_2, down_2 = turn_z(parts_2[4], 1), turn_z(parts_2[5], -1)
    (g_mine,) = call(
        functools.partial(bundle_kernel, 1.0), [((3 * BLK, T), BF)], g_side, *g_sixes
    )
    g_theirs = swap(g_mine, 1)

    def onward(up, down, parts, step):
        up, down = add((up, parts[step]), (down, parts[9 - step]))
        return turn_z(up, 1), turn_z(down, -1)

    up_1, down_1 = onward(up_1, down_1, parts_1, 3)
    (dkv,) = call(
        remote_backward_kernel, [((T, 2 * T), BF)],
        qkv, coarse, dkv_local, remote, g_arrived, g_chained, g_mine, g_theirs,
        const["met"], const["rim_mean"], scalars=pos,
    )
    up_2, down_2 = onward(up_2, down_2, parts_2, 3)
    if head_count == 8:
        pieces = call(grad_x_kernel, [((2 * T, T), BF)] * 4, y, dkv, weights, scalars=pos)

        def turn_x(array, step):
            pairs = [(i, i // 4 * 4 + (i % 4 + step) % 4) for i in range(8)]
            return lax.ppermute(array, "head", pairs)

        right, left = turn_x(pieces[2], 1), turn_x(pieces[3], -1)
    up_1, down_1 = onward(up_1, down_1, parts_1, 2)
    up_2, down_2 = onward(up_2, down_2, parts_2, 2)
    if head_count == 8:
        (next_right,) = add((right, pieces[1]))
        right = turn_x(next_right, 1)
    (up_1,) = add((up_1, parts_1[1]))
    up_1 = turn_z(up_1, 1)
    (up_2,) = add((up_2, parts_2[1]))
    up_2 = turn_z(up_2, 1)
    if head_count == 8:
        keep_x, send_x = call(
            sum_x_kernel, [((T, T), F32), ((T, T), BF)], pieces[0], left, right
        )
        came_x = lax.ppermute(send_x, "head", [(i, i ^ 4) for i in range(8)])
    keep, send = call(
        sum_z_kernel, [((chunk // 2, 4 * T), F32), ((chunk // 2, 4 * T), BF)],
        parts_1[0], up_1, down_1, parts_2[0], up_2, down_2, scalars=pos,
    )
    came = swap(send, 2)
    if head_count == 8:
        (grad_x,) = call(last_x_kernel, [((T, T), BF)], keep_x, came_x)
    else:
        flat = jnp.transpose(weights, (1, 0, 2)).reshape(width, wide)
        grad_x = dot_nt(jnp.concatenate([y[:T, :T], dkv], axis=1), flat).astype(BF)
    grad_wqkv, grad_wout = call(
        finish_kernel, [((3, chunk // 2, T), F32), ((chunk // 2, T), F32)], keep, came
    )
    return grad_x, jnp.transpose(grad_wqkv, (1, 0, 2)), grad_wout.T


def solution(mesh):
    placed = (P("ctx", None), P(None, None, "head"), P("head", None), P("ctx", None))
    return jax.shard_map(
        local,
        mesh=mesh,
        in_specs=placed,
        out_specs=(P("ctx", "head"), P("ctx", None, "head"), P("head", "ctx")),
        check_vma=False,
    )
```

```python
import functools

import jax
import jax.numpy as jnp
import numpy as np
from jax import lax
from jax.experimental import pallas as pl
from jax.experimental.pallas import tpu as pltpu
from jax.sharding import PartitionSpec as P

DH = 128
BLK = 16
T = 256
ROWS = 256
NEAR = 2 * BLK
REM = 64
FAR = 96
SCALE = DH**-0.5
BF = jnp.bfloat16
F32 = jnp.float32

STARTS = {1: 0, 2: 128, 3: 192, 4: 224, 5: 240, 6: 248, 7: 252}


def tables():
    spread = np.zeros((T, ROWS), np.float32)
    mean = np.zeros((ROWS, T), np.float32)
    pairs = np.zeros((ROWS, ROWS), np.float32)
    for level, start in STARTS.items():
        factor = 2**level
        for row in range(T // factor):
            spread[row * factor : (row + 1) * factor, start + row] = 1.0
            mean[start + row, row * factor : (row + 1) * factor] = 1.0 / factor
        if level <= 3:
            for block in range(T // factor // BLK):
                other = start + (block ^ 1) * BLK
                mine = start + block * BLK
                pairs[mine : mine + BLK, other : other + BLK] = 1.0
    block_of = np.arange(T) // BLK
    band = (np.abs(block_of[:, None] - block_of[None, :]) <= 1).astype(np.float32)
    rim = np.zeros((T, REM), np.float32)
    rim[:BLK, :BLK] = np.eye(BLK)
    rim[T - BLK :, BLK:NEAR] = np.eye(BLK)
    rim[:, NEAR:] = spread[:, 224:]
    rim_mean = rim.copy()
    rim_mean[:, NEAR:] = mean.T[:, 224:]
    meets = np.zeros((REM, FAR), np.float32)
    meets[0:16, 0:16] = 1.0
    meets[16:32, 16:32] = 1.0
    meets[32:48, 32:48] = 1.0
    meets[48:56, 48:64] = 1.0
    meets[56:60, 64:80] = 1.0
    meets[60:62, 80:96] = 1.0
    bf = lambda array: np.asarray(array, dtype=BF)
    return {
        "spread": bf(spread),
        "gather": bf(spread.T),
        "mean": bf(mean),
        "unmean": bf(mean.T),
        "band": band,
        "pairs": pairs,
        "rim": bf(rim),
        "rim_mean": bf(rim_mean),
        "unrim": bf(rim.T),
        "meets": meets,
        "met": np.ascontiguousarray(meets.T),
    }


def dot(left, right):
    return jnp.dot(left, right, preferred_element_type=F32)


def dot_nt(left, right):
    return lax.dot_general(left, right, (((1,), (1,)), ((), ())), preferred_element_type=F32)


def dot_tn(left, right):
    return lax.dot_general(left, right, (((0,), (0,)), ((), ())), preferred_element_type=F32)


def dot_two(exact, right):
    high = right.astype(BF)
    low = (right - high.astype(F32)).astype(BF)
    return dot(exact, high) + dot(exact, low)


def normed(values):
    scale = lax.rsqrt(jnp.mean(values * values, axis=-1, keepdims=True) + 1e-06)
    return values * scale, scale


def norm_back(unit, scale, grad):
    return scale * (grad - unit * jnp.mean(grad * unit, axis=-1, keepdims=True))


def head(array, number):
    return array[:, number * DH : (number + 1) * DH]


def with_ones(values):
    return jnp.concatenate([values, jnp.ones_like(values)], axis=1)


class Calls:
    def __init__(self):
        self.token = None

    def __call__(self, kernel, outs, *args, placed=False, after=(), flops=1e10):
        first = tuple(after) if self.token is None else (self.token,) + tuple(after)
        skipped = len(first)
        args = first + args
        specs = [pl.BlockSpec(memory_space=pltpu.VMEM)] * len(args)

        def body(*refs):
            refs = refs[skipped:-1]
            if placed:
                kernel((lax.axis_index("ctx"), lax.axis_index("head")), *refs)
            else:
                kernel(*refs)

        shapes = [jax.ShapeDtypeStruct(shape, dtype) for shape, dtype in outs]
        shapes.append(jax.ShapeDtypeStruct((8, 128), F32))
        results = pl.pallas_call(
            body,
            out_shape=tuple(shapes),
            in_specs=specs,
            out_specs=tuple(pl.BlockSpec(memory_space=pltpu.VMEM) for _ in shapes),
            compiler_params=pltpu.CompilerParams(vmem_limit_bytes=44 * 1024 * 1024),
            cost_estimate=pl.CostEstimate(
                flops=int(flops), bytes_accessed=1000, transcendentals=0
            ),
        )(*args)
        self.token = results[-1]
        return results[:-1]


def packed(rows):
    half = rows.shape[1] // 2
    return jnp.concatenate([rows[:, :half], rows[:, half:]], axis=0)


def unpacked(rows):
    half = rows.shape[0] // 2
    return jnp.concatenate([rows[:half], rows[half:]], axis=1)


def edges_kernel(pos, tokens, near_out, far_out, level_5_out):
    even = pos[0] % 2 == 0
    row = lax.broadcasted_iota(jnp.int32, (BLK, T), 0)
    col = lax.broadcasted_iota(jnp.int32, (BLK, T), 1)
    mean = dot(jnp.where(col // BLK == row, 1.0 / BLK, 0.0).astype(BF), tokens[...])
    row = lax.broadcasted_iota(jnp.int32, (8, T), 0)
    col = lax.broadcasted_iota(jnp.int32, (8, T), 1)
    wide = dot(jnp.where(col // NEAR == row, 1.0 / NEAR, 0.0).astype(BF), tokens[...])
    first = tokens[:BLK].astype(F32)
    last = tokens[T - BLK :].astype(F32)
    near_out[:BLK] = mean.astype(BF)
    near_out[BLK:] = jnp.where(even, last, first).astype(BF)
    far_out[...] = jnp.where(even, first, last).astype(BF)
    level_5_out[...] = packed(wide).astype(BF)


def project_kernel(tokens, weights, mean, qkv_out, coarse_out):
    tok = tokens[...]
    parts = [dot(tok, weights[number]).astype(BF) for number in range(3)]
    qkv = jnp.concatenate(parts, axis=1)
    qkv_out[...] = qkv
    coarse_out[...] = dot(mean[...], qkv)


def half_of_rows(whole, number):
    width = whole.shape[0] // 32
    return jnp.concatenate(
        [whole[(2 * j + number) * width : (2 * j + number + 1) * width] for j in range(16)], axis=0
    )


def d_attn_kernel(pos, grad_out, w_out, tokens, d_attn_out, own_out, other_out):
    d_attn_out[...] = dot_nt(grad_out[...], w_out[...]).astype(BF)
    even = pos[0] % 2 == 0
    for number, array in enumerate((tokens, grad_out)):
        cols = slice(number * T, (number + 1) * T)
        turned = array[...].T
        halves = half_of_rows(turned, 0), half_of_rows(turned, 1)
        own_out[:, cols] = jnp.where(even, halves[0], halves[1])
        other_out[:, cols] = jnp.where(even, halves[1], halves[0])


def merged(factor, first, second):
    row = lax.broadcasted_iota(jnp.int32, (BLK, BLK), 0)
    col = lax.broadcasted_iota(jnp.int32, (BLK, BLK), 1)
    same = row // 8 == col // 8
    source = col % 8 // 2
    left = jnp.where(jnp.logical_and(same, source == row % 8), factor, 0.0).astype(BF)
    right = jnp.where(jnp.logical_and(same, source + 4 == row % 8), factor, 0.0).astype(BF)
    return (dot(left, first) + dot(right, second)).astype(BF)


def merge_kernel(factor, first, second, *rest):
    if len(rest) > 1:
        rest[1][...] = rest[0][...]
    rest[-1][...] = merged(factor, first[...], second[...])


def bundle_kernel(level_5, level_6, third, fourth, chained, near, out):
    out[:BLK] = level_5[...]
    out[BLK : 2 * BLK] = level_6[...]
    out[2 * BLK : 3 * BLK] = merged(0.5, third[...], fourth[...])
    out[3 * BLK : 5 * BLK] = packed(chained[...].astype(F32)).astype(BF)
    out[5 * BLK :] = packed(near[...].astype(F32)).astype(BF)


def grads_5_kernel(near, level_5, side, out):
    out[:NEAR] = near[...]
    rows = [unpacked(ref[...].astype(F32)) for ref in (level_5, side)]
    out[NEAR:] = jnp.concatenate(rows, axis=0).astype(BF)


def grads_6_kernel(pos, own, other, far, out, far_out):
    even = pos[0] % 2 == 0
    row = lax.broadcasted_iota(jnp.int32, (8, BLK), 0)
    col = lax.broadcasted_iota(jnp.int32, (8, BLK), 1)
    pairs = jnp.where(col // 2 == row, 1.0, 0.0).astype(BF)
    ours, others = dot(pairs, own[NEAR:]), dot(pairs, other[NEAR:])
    first, second = jnp.where(even, ours, others), jnp.where(even, others, ours)
    out[...] = jnp.concatenate([first, second], axis=0).astype(BF)
    far_out[...] = far[...]


def local_units(qkv, coarse, number):
    query = head(qkv, number).astype(F32)
    key = head(qkv, 2 + number).astype(F32)
    return (
        normed(query),
        normed(key),
        head(qkv, 4 + number),
        normed(head(coarse, number)),
        normed(head(coarse, 2 + number)),
        head(coarse, 4 + number).astype(BF),
    )


def local_weights(units, band, pairs):
    (qn, _), (kn, _), _, (qc, _), (kc, _), _ = units
    near = jnp.exp(dot_nt(qn.astype(BF), kn.astype(BF)) * SCALE) * band
    far = jnp.exp(dot_nt(qc.astype(BF), kc.astype(BF)) * SCALE) * pairs
    return near, far


def local_forward_kernel(qkv_ref, coarse_ref, band, pairs, spread, out, probs, units_out, scales_out):
    qkv = qkv_ref[...]
    coarse = coarse_ref[...]
    for number in range(2):
        units = local_units(qkv, coarse, number)
        near, far = (array.astype(BF) for array in local_weights(units, band[...], pairs[...]))
        total = dot(near, with_ones(units[2]))
        part = dot(far, with_ones(units[5]))
        out[:, number * 2 * DH : (number + 1) * 2 * DH] = total + dot_two(spread[...], part)
        probs[:, number * T : (number + 1) * T] = near
        probs[:, (2 + number) * T : (3 + number) * T] = far
        for place, (unit, scale) in enumerate((units[0], units[1], units[3], units[4])):
            at = slice((2 * place + number) * DH, (2 * place + number + 1) * DH)
            units_out[:, at] = unit
            scales_out[:, at] = jnp.broadcast_to(scale, (T, DH))


def by_side(pos, ours, others):
    even = pos[0] % 2 == 0
    return jnp.where(even, ours, others), jnp.where(even, others, ours)


def remote_rows(pos, arrived, far, levels):
    left, right = by_side(pos, far, arrived[BLK:])
    return jnp.concatenate([left, right, arrived[:BLK]] + levels, axis=0)


def own_rows(fine, coarse):
    return jnp.concatenate([fine[:BLK], fine[T - BLK :], coarse[224:]], axis=0)


def exists(pos, shape, axis):
    where = lax.broadcasted_iota(jnp.int32, shape, axis)
    no_left = jnp.logical_and(pos[0] == 0, where < BLK)
    no_right = jnp.logical_and(pos[0] == 31, jnp.logical_and(where >= BLK, where < NEAR))
    return jnp.where(jnp.logical_or(no_left, no_right), 0.0, 1.0)


def remote_weights(pos, query, remote, meets, number):
    key, key_scale = normed(head(remote, 2 + number))
    value = head(remote, 4 + number).astype(BF)
    weights = jnp.exp(dot_nt(query, key.astype(BF)) * SCALE) * meets * exists(pos, (REM, FAR), 1)
    return weights, key, key_scale, value


def gathered_rows(pos, far, mine_ref, theirs_ref):
    mine = mine_ref[...].astype(F32)
    theirs = theirs_ref[...].astype(F32)
    levels = []
    for level in range(3):
        at = slice(level * BLK, (level + 1) * BLK)
        levels += by_side(pos, unpacked(mine[at]), unpacked(theirs[at]))
    arrived = unpacked(theirs[5 * BLK :])
    return remote_rows(pos, arrived, far[...].astype(F32), levels), theirs


def turn_far_kernel(pos, near, far, mine_ref, theirs_ref, own_out, other_out):
    even = pos[0] % 2 == 0
    rows, theirs = gathered_rows(pos, far, mine_ref, theirs_ref)
    known = near[...].astype(F32)
    left, right = by_side(pos, known[BLK:], unpacked(theirs[3 * BLK : 5 * BLK]))
    other = jnp.concatenate([left, right, known[:BLK], rows[3 * BLK :]], axis=0)
    for array, out in ((rows, own_out), (other, other_out)):
        turned = array.T
        out[...] = jnp.where(even, half_of_rows(turned, 0), half_of_rows(turned, 1)).astype(BF)


def remote_forward_kernel(
    pos, weights_ref, qkv_ref, coarse_ref, local_ref, d_attn, far, mine_ref, theirs_ref,
    meets, rim, gather,
    attn_out, d_num_out, d_den_out, near_out, far_out, level_5_out, remote_out,
):
    rows, _ = gathered_rows(pos, far, mine_ref, theirs_ref)
    even = pos[0] % 2 == 0
    rows = rows.astype(BF)
    remote = jnp.concatenate([dot(rows, weights_ref[part]) for part in range(3)], axis=1)
    remote = remote.astype(BF)
    remote_out[...] = remote
    remote = remote.astype(F32)
    wide = [None] * 4
    for number in range(2):
        fine = qkv_ref[:, number * DH : (number + 1) * DH].astype(F32)
        query = normed(own_rows(fine, coarse_ref[:, number * DH : (number + 1) * DH]))[0]
        weights, _, _, value = remote_weights(
            pos, query.astype(BF), remote, meets[...], number
        )
        part = dot(weights.astype(BF), with_ones(value))
        total = local_ref[:, number * 2 * DH : (number + 1) * 2 * DH] + dot_two(rim[...], part)
        cols = slice(number * DH, (number + 1) * DH)
        inverse = 1.0 / total[:, DH:]
        attn = total[:, :DH] * inverse
        attn_out[:, cols] = attn.astype(BF)
        d_num = (d_attn[:, cols].astype(F32) * inverse).astype(BF)
        d_den = -jnp.sum(d_num.astype(F32) * attn, axis=-1, keepdims=True)
        d_den = jnp.broadcast_to(d_den, (T, DH))
        d_num_out[:, cols] = d_num
        d_den_out[:, cols] = d_den
        sums = dot_two(
            gather[224:256, :], jnp.concatenate([d_num.astype(F32), d_den], axis=1)
        )
        for offset, full, row_sums in (
            (0, d_num.astype(F32), sums[:, :DH]),
            (2 * DH, d_den, sums[:, DH:]),
        ):
            at = slice(offset + number * DH, offset + (number + 1) * DH)
            first = full[:BLK]
            last = full[T - BLK :]
            near_out[:BLK, at] = row_sums[:BLK].astype(BF)
            wide[offset // DH + number] = row_sums[BLK : BLK + 8]
            near_out[BLK:, at] = jnp.where(even, last, first).astype(BF)
            far_out[:, at] = jnp.where(even, first, last).astype(BF)
    level_5_out[...] = packed(jnp.concatenate(wide, axis=1)).astype(BF)


def local_backward_kernel(
    pos, qkv_ref, coarse_ref, probs, units_ref, scales_ref, attn_ref, d_num_ref, d_den_ref,
    remote_ref, meets, unrim, gather, unmean,
    y_out, dkv_out,
):
    remote = remote_ref[...].astype(F32)
    y_out[:T, T:] = attn_ref[...]
    for number in range(2):
        cols = slice(number * DH, (number + 1) * DH)
        vals = slice((2 + number) * DH, (3 + number) * DH)
        qn, kn, qc, kc = (head(units_ref, 2 * place + number) for place in range(4))
        q_scale, k_scale, qc_scale, kc_scale = (
            head(scales_ref, 2 * place + number) for place in range(4)
        )
        value = head(qkv_ref, 4 + number)
        value_c = head(coarse_ref, 4 + number).astype(BF)
        near_w = probs[:, number * T : (number + 1) * T]
        far_w = probs[:, (2 + number) * T : (3 + number) * T]
        d_num = d_num_ref[:, cols]
        d_den = d_den_ref[:, cols]
        both = jnp.concatenate([d_num.astype(F32), d_den], axis=1)
        sums = dot_two(gather[...], both)
        d_num_c = sums[:, :DH].astype(BF)
        d_den_c = sums[:, DH : DH + 1]
        d_near = (near_w * (dot_nt(d_num, value) + d_den[:, :1]) * SCALE).astype(BF)
        d_far = (far_w * (dot_nt(d_num_c, value_c) + d_den_c) * SCALE).astype(BF)
        dqn = dot(d_near, kn.astype(BF))
        dqc = dot(d_far, kc.astype(BF))
        query = own_rows(qn, qc).astype(BF)
        weights, key_r, key_scale, value_r = remote_weights(
            pos, query, remote, meets[...], number
        )
        sums_r = dot_two(unrim[...], both)
        d_num_r = sums_r[:, :DH].astype(BF)
        d_rem = dot_nt(d_num_r, value_r) + sums_r[:, DH : DH + 1]
        d_rem = (weights * d_rem * SCALE).astype(BF)
        y_out[2 * T : 2 * T + FAR, cols] = norm_back(key_r, key_scale, dot_tn(d_rem, query)).astype(BF)
        y_out[2 * T : 2 * T + FAR, vals] = dot_tn(weights.astype(BF), d_num_r).astype(BF)
        dqr = dot(d_rem, key_r.astype(BF))
        dqn = jnp.concatenate(
            [dqn[:BLK] + dqr[:BLK], dqn[BLK : T - BLK], dqn[T - BLK :] + dqr[BLK:NEAR]], axis=0
        )
        dqc = jnp.concatenate([dqc[:224], dqc[224:] + dqr[NEAR:]], axis=0)
        table = jnp.concatenate(
            [
                norm_back(qc, qc_scale, dqc),
                norm_back(kc, kc_scale, dot_tn(d_far, qc.astype(BF))),
                dot_tn(far_w, d_num_c),
            ],
            axis=1,
        )
        table = dot_two(unmean[...], table)
        y_out[:T, cols] = (norm_back(qn, q_scale, dqn) + table[:, :DH]).astype(BF)
        dk = norm_back(kn, k_scale, dot_tn(d_near, qn.astype(BF))) + table[:, DH : 2 * DH]
        dv = dot_tn(near_w, d_num) + table[:, 2 * DH :]
        dkv_out[:, cols] = dk
        dkv_out[:, vals] = dv
        y_out[T : 2 * T, cols] = dk.astype(BF)
        y_out[T : 2 * T, vals] = dv.astype(BF)


def remote_backward_kernel(
    pos, qkv_ref, coarse_ref, local_ref, remote_ref, own_ref, other_ref, g_far, g_6, g_7,
    met, rim_mean, dkv_out,
):
    remote = remote_ref[...].astype(F32)
    other = other_ref[...].astype(F32)
    sides = by_side(pos, own_ref[...].astype(F32)[NEAR + 8 :], other[NEAR + 8 :])
    levels = list(sides) + [g_6[...].astype(F32), g_7[...].astype(F32)]
    grads = remote_rows(pos, other[:NEAR], g_far[...].astype(F32), levels)
    for number in range(2):
        query = normed(head(remote, number))[0].astype(BF)
        k_cols = slice((2 + number) * DH, (3 + number) * DH)
        v_cols = slice((4 + number) * DH, (5 + number) * DH)
        key, key_scale = normed(
            own_rows(qkv_ref[:, k_cols].astype(F32), coarse_ref[:, k_cols])
        )
        vals = own_rows(qkv_ref[:, v_cols].astype(F32), coarse_ref[:, v_cols]).astype(BF)
        weights = jnp.exp(dot_nt(query, key.astype(BF)) * SCALE)
        weights = weights * met[...] * exists(pos, (FAR, REM), 0)
        d_num = head(grads, number).astype(BF)
        d_den = head(grads, 2 + number)[:, :1]
        d_score = (weights * (dot_nt(d_num, vals) + d_den) * SCALE).astype(BF)
        dk = norm_back(key, key_scale, dot_tn(d_score, query))
        dv = dot_tn(weights.astype(BF), d_num)
        more = dot_two(rim_mean[...], jnp.concatenate([dk, dv], axis=1))
        k_cols = slice(number * DH, (number + 1) * DH)
        v_cols = slice((2 + number) * DH, (3 + number) * DH)
        dkv_out[:, k_cols] = (local_ref[:, k_cols] + more[:, :DH]).astype(BF)
        dkv_out[:, v_cols] = (local_ref[:, v_cols] + more[:, DH:]).astype(BF)


def weight_kernel(steps, pos, own_half, other_half, own, other, own_far, other_far, *outs):
    z = pos[0] // 4
    width = own_half.shape[0] // 8
    for step, out in zip(steps, outs):
        at = pl.ds(pl.multiple_of((z + step) % 8 * width, width), width)
        for cols in (slice(0, T), slice(T, 2 * T)):
            total = dot(own_half[at, cols], own[:T, cols])
            total += dot(other_half[at, cols], other[:T, cols])
            out[:, cols] = total.astype(BF)
        total = dot(own_half[at, :T], own[T : 2 * T]) + dot(own_far[at, :], own[2 * T : 2 * T + FAR])
        total += dot(other_half[at, :T], other[T : 2 * T])
        total += dot(other_far[at, :], other[2 * T : 2 * T + FAR])
        out[:, 2 * T :] = total.astype(BF)


def add_kernel(*refs):
    count = len(refs) // 3
    for number in range(count):
        total = refs[2 * number][...].astype(F32) + refs[2 * number + 1][...].astype(F32)
        refs[2 * count + number][...] = total.astype(BF)


def last_step_kernel(pos, up, down, part_1, part_0, straight, cross, keep, send):
    low = pos[0] // 2 % 2 == 0
    onward = up[...].astype(F32) + part_1[...].astype(F32)
    here = down[...].astype(F32) + part_0[...].astype(F32)
    half = onward.shape[0] // 2
    straight[...] = jnp.where(low, onward[:half], onward[half:]).astype(BF)
    cross[...] = jnp.where(low, onward[half:], onward[:half]).astype(BF)
    keep[...] = jnp.where(low, here[:half], here[half:])
    send[...] = jnp.where(low, here[half:], here[:half]).astype(BF)


def finish_kernel(keep, straight, cross, side, w_qkv, w_out):
    total = keep[...] + side[...].astype(F32)
    total += straight[...].astype(F32) + cross[...].astype(F32)
    w_qkv[0] = total[:, :T]
    w_qkv[1] = total[:, 2 * T : 3 * T]
    w_qkv[2] = total[:, 3 * T :]
    w_out[...] = total[:, T : 2 * T]


def grad_x_kernel(pos, y, dkv, weights, *outs):
    x = pos[1] % 4
    side = pos[1] // 4
    for step in range(4):
        for turn in range(2):
            target = (side + turn) % 2 * 4 + (x + step) % 4
            rows = pl.ds(pl.multiple_of(target * T, T), T)
            total = dot_nt(y[:T, :T], weights[0, rows, :])
            total += dot_nt(dkv[:, :T], weights[1, rows, :])
            total += dot_nt(dkv[:, T:], weights[2, rows, :])
            outs[step][turn * T : (turn + 1) * T] = total.astype(BF)


def sum_x_kernel(first, second, third, fourth, keep, send):
    total = first[...].astype(F32) + second[...].astype(F32)
    total = total + third[...].astype(F32) + fourth[...].astype(F32)
    keep[...] = total[:T]
    send[...] = total[T:].astype(BF)


def last_x_kernel(keep, came, out):
    out[...] = (keep[...] + came[...].astype(F32)).astype(BF)


def local(tokens, w_qkv, w_out, grad_out):
    const = {name: jnp.asarray(array) for name, array in tables().items()}
    head_count = lax.axis_size("head")
    weights = jnp.transpose(w_qkv, (1, 0, 2))
    width = tokens.shape[1]
    wide = 3 * T

    def swap(array, bit):
        return lax.ppermute(array, "ctx", [(i, i ^ bit) for i in range(32)])

    def chain(array):
        pairs = [(i, (i + 1) % 32) for i in range(1, 32, 2)]
        return lax.ppermute(array, "ctx", pairs + [(b, a) for a, b in pairs])

    def turn_z(array, step, side=0):
        return lax.ppermute(
            array, "ctx", [(i, (i // 4 + step) % 8 * 4 + (i % 4 ^ side)) for i in range(32)]
        )

    def add(*pairs):
        shapes = [(pair[0].shape, BF) for pair in pairs]
        return call(add_kernel, shapes, *[array for pair in pairs for array in pair], flops=1e3)

    call = Calls()

    near, far, level_5 = call(
        edges_kernel, [((NEAR, width), BF), ((BLK, width), BF), ((BLK, width // 2), BF)],
        tokens, placed=True,
    )
    side = swap(level_5, 2)
    qkv, coarse = call(
        project_kernel, [((T, wide), BF), ((ROWS, wide), F32)], tokens, weights, const["mean"]
    )
    far, level_6 = call(
        functools.partial(merge_kernel, 0.5), [((BLK, width), BF), ((BLK, width // 2), BF)],
        level_5, side, far, flops=1e3)
    sixes = [swap(level_6, bit) for bit in (4, 8, 12)]
    chained = chain(far)
    forward, probs, units, scales = call(
        local_forward_kernel,
        [((T, 2 * T), F32), ((T, 4 * T), BF), ((T, 4 * T), F32), ((T, 4 * T), F32)],
        qkv, coarse, const["band"], const["pairs"], const["spread"],
    )
    (mine,) = call(
        bundle_kernel, [((9 * BLK, width // 2), BF)], side, *sixes, chained, near, flops=1e3)
    theirs = swap(mine, 1)
    d_attn, own_half, other_half = call(
        d_attn_kernel,
        [((T, T), BF), ((width // 2, 2 * T), BF), ((width // 2, 2 * T), BF)],
        grad_out, w_out, tokens, placed=True,
    )
    sent_half = swap(other_half, 1)
    attn, d_num, d_den, g_near, g_far, g_5, remote = call(
        remote_forward_kernel,
        [
            ((T, T), BF), ((T, T), BF), ((T, T), F32), ((NEAR, 2 * T), BF), ((BLK, 2 * T), BF),
            ((BLK, T), BF), ((FAR, wide), BF),
        ],
        weights, qkv, coarse, forward, d_attn, chained, mine, theirs,
        const["meets"], const["rim"], const["gather"], placed=True,
    )
    g_side = swap(g_5, 2)
    y, dkv_local = call(
        local_backward_kernel, [((2 * T + FAR, 2 * T), BF), ((T, 2 * T), F32)],
        qkv, coarse, probs, units, scales, attn, d_num, d_den, remote,
        const["meets"], const["unrim"], const["gather"], const["unmean"], placed=True,
    )
    other_y = swap(y, 1)
    (g_own,) = call(grads_5_kernel, [((3 * BLK, 2 * T), BF)], g_near, g_5, g_side, flops=1e3)
    g_other = swap(g_own, 1)
    own_far, other_far = call(
        turn_far_kernel, [((width // 2, FAR), BF)] * 2, near, chained, mine, theirs, placed=True
    )
    chunk = width // 16
    parts = {}

    def weight_parts(*steps):
        shapes = [((chunk, 4 * T), BF)] * len(steps)
        products = call(
            functools.partial(weight_kernel, steps), shapes,
            own_half, sent_half, y, other_y, own_far, other_far, placed=True,
        )
        parts.update(zip(steps, products))

    def onward(step):
        sums = add((up, parts[step]), (down, parts[9 - step]))
        return turn_z(sums[0], 1), turn_z(sums[1], -1)

    weight_parts(4, 5)
    up, down = turn_z(parts[4], 1), turn_z(parts[5], -1)
    weight_parts(3, 6, 2, 7, 1, 0)
    grads = [((BLK, 2 * T), BF)]
    g_6, g_far = call(grads_6_kernel, grads * 2, g_own, g_other, g_far, placed=True, flops=1e3)
    came_6 = swap(g_6, 4)
    g_chained = chain(g_far)
    (g_7,) = call(functools.partial(merge_kernel, 1.0), grads, g_6, came_6, flops=1e3)
    came_7 = swap(g_7, 8)
    up, down = onward(3)
    (dkv,) = call(
        remote_backward_kernel, [((T, 2 * T), BF)],
        qkv, coarse, dkv_local, remote, g_own, g_other, g_chained, came_6, came_7,
        const["met"], const["rim_mean"], placed=True,
    )
    if head_count == 8:
        pieces = call(grad_x_kernel, [((2 * T, T), BF)] * 4, y, dkv, weights, placed=True)

        def turn_x(array, step):
            pairs = [(i, i // 4 * 4 + (i % 4 + step) % 4) for i in range(8)]
            return lax.ppermute(array, "head", pairs)

        came = [turn_x(pieces[step], step) for step in (1, 2, 3)]
    up, down = onward(2)
    if head_count == 8:
        keep_x, send_x = call(
            sum_x_kernel, [((T, T), F32), ((T, T), BF)], pieces[0], *came, flops=1e3)
        came_x = lax.ppermute(send_x, "head", [(i, i ^ 4) for i in range(8)])
    straight, cross, keep, send = call(
        last_step_kernel,
        [((chunk // 2, 4 * T), BF)] * 2 + [((chunk // 2, 4 * T), F32), ((chunk // 2, 4 * T), BF)],
        up, down, parts[1], parts[0], placed=True, flops=1e3)
    side = swap(send, 2)
    straight, cross = turn_z(straight, 1), turn_z(cross, 1, 2)
    grad_wqkv, grad_wout = call(
        finish_kernel, [((3, chunk // 2, T), F32), ((chunk // 2, T), F32)],
        keep, straight, cross, side,
    )
    if head_count == 8:
        (grad_x,) = call(last_x_kernel, [((T, T), BF)], keep_x, came_x)
    else:
        flat = jnp.transpose(weights, (1, 0, 2)).reshape(width, wide)
        grad_x = dot_nt(jnp.concatenate([y[:T, :T], dkv], axis=1), flat).astype(BF)
    return grad_x, jnp.transpose(grad_wqkv, (1, 0, 2)), grad_wout.T


def solution(mesh):
    placed = (P("ctx", None), P(None, None, "head"), P("head", None), P("ctx", None))
    return jax.shard_map(
        local,
        mesh=mesh,
        in_specs=placed,
        out_specs=(P("ctx", "head"), P("ctx", None, "head"), P("head", "ctx")),
        check_vma=False,
    )
```

```python
import functools

import jax
import jax.numpy as jnp
import numpy as np
from jax import lax
from jax.experimental import pallas as pl
from jax.experimental.pallas import tpu as pltpu
from jax.sharding import PartitionSpec as P

DH = 128
BLK = 16
T = 256
ROWS = 256
NEAR = 2 * BLK
REM = 64
FAR = 96
SCALE = DH**-0.5
BF = jnp.bfloat16
F32 = jnp.float32

STARTS = {1: 0, 2: 128, 3: 192, 4: 224, 5: 240, 6: 248, 7: 252}


def tables():
    spread = np.zeros((T, ROWS), np.float32)
    mean = np.zeros((ROWS, T), np.float32)
    pairs = np.zeros((ROWS, ROWS), np.float32)
    for level, start in STARTS.items():
        factor = 2**level
        for row in range(T // factor):
            spread[row * factor : (row + 1) * factor, start + row] = 1.0
            mean[start + row, row * factor : (row + 1) * factor] = 1.0 / factor
        if level <= 3:
            for block in range(T // factor // BLK):
                other = start + (block ^ 1) * BLK
                mine = start + block * BLK
                pairs[mine : mine + BLK, other : other + BLK] = 1.0
    block_of = np.arange(T) // BLK
    band = (np.abs(block_of[:, None] - block_of[None, :]) <= 1).astype(np.float32)
    rim = np.zeros((T, REM), np.float32)
    rim[:BLK, :BLK] = np.eye(BLK)
    rim[T - BLK :, BLK:NEAR] = np.eye(BLK)
    rim[:, NEAR:] = spread[:, 224:]
    rim_mean = rim.copy()
    rim_mean[:, NEAR:] = mean.T[:, 224:]
    meets = np.zeros((REM, FAR), np.float32)
    meets[0:16, 0:16] = 1.0
    meets[16:32, 16:32] = 1.0
    meets[32:48, 32:48] = 1.0
    meets[48:56, 48:64] = 1.0
    meets[56:60, 64:80] = 1.0
    meets[60:62, 80:96] = 1.0
    bf = lambda array: np.asarray(array, dtype=BF)
    return {
        "spread": bf(spread),
        "gather": bf(spread.T),
        "mean": bf(mean),
        "unmean": bf(mean.T),
        "band": band,
        "pairs": pairs,
        "rim": bf(rim),
        "rim_mean": bf(rim_mean),
        "meets": meets,
        "met": np.ascontiguousarray(meets.T),
    }


def dot(left, right):
    return jnp.dot(left, right, preferred_element_type=F32)


def dot_nt(left, right):
    return lax.dot_general(left, right, (((1,), (1,)), ((), ())), preferred_element_type=F32)


def dot_tn(left, right):
    return lax.dot_general(left, right, (((0,), (0,)), ((), ())), preferred_element_type=F32)


def dot_two(exact, right):
    high = right.astype(BF)
    low = (right - high.astype(F32)).astype(BF)
    return dot(exact, high) + dot(exact, low)


def normed(values):
    scale = lax.rsqrt(jnp.mean(values * values, axis=-1, keepdims=True) + 1e-06)
    return values * scale, scale


def norm_back(unit, scale, grad):
    return scale * (grad - unit * jnp.mean(grad * unit, axis=-1, keepdims=True))


def head(array, number):
    return array[:, number * DH : (number + 1) * DH]


def pack_den(d_den_0, d_den_1):
    lane = lax.broadcasted_iota(jnp.int32, (T, DH), 1)
    total = jnp.zeros((T, DH), F32)
    for number, array in enumerate((d_den_0, d_den_1)):
        high = array.astype(BF).astype(F32)
        total = jnp.where(lane == 2 * number, high, total)
        total = jnp.where(lane == 2 * number + 1, array - high, total)
    return total.astype(BF)


def packed_den(sums, number):
    at = 2 * DH + 2 * number
    return sums[:, at : at + 1] + sums[:, at + 1 : at + 2]


def with_ones(values):
    return jnp.concatenate([values, jnp.ones_like(values)], axis=1)


class Calls:
    def __init__(self):
        self.token = None

    def __call__(self, kernel, outs, *args, placed=False, after=(), flops=1e10):
        first = tuple(after) if self.token is None else (self.token,) + tuple(after)
        skipped = len(first)
        args = first + args
        specs = [pl.BlockSpec(memory_space=pltpu.VMEM)] * len(args)

        def body(*refs):
            refs = refs[skipped:-1]
            if placed:
                kernel((lax.axis_index("ctx"), lax.axis_index("head")), *refs)
            else:
                kernel(*refs)

        shapes = [jax.ShapeDtypeStruct(shape, dtype) for shape, dtype in outs]
        shapes.append(jax.ShapeDtypeStruct((8, 128), F32))
        results = pl.pallas_call(
            body,
            out_shape=tuple(shapes),
            in_specs=specs,
            out_specs=tuple(pl.BlockSpec(memory_space=pltpu.VMEM) for _ in shapes),
            compiler_params=pltpu.CompilerParams(vmem_limit_bytes=44 * 1024 * 1024),
            cost_estimate=pl.CostEstimate(
                flops=int(flops), bytes_accessed=1000, transcendentals=0
            ),
        )(*args)
        self.token = results[-1]
        return results[:-1]


def packed(rows):
    half = rows.shape[1] // 2
    return jnp.concatenate([rows[:, :half], rows[:, half:]], axis=0)


def unpacked(rows):
    half = rows.shape[0] // 2
    return jnp.concatenate([rows[:half], rows[half:]], axis=1)


def edges_kernel(pos, tokens, near_out, far_out, level_5_out):
    even = pos[0] % 2 == 0
    row = lax.broadcasted_iota(jnp.int32, (BLK, T), 0)
    col = lax.broadcasted_iota(jnp.int32, (BLK, T), 1)
    mean = dot(jnp.where(col // BLK == row, 1.0 / BLK, 0.0).astype(BF), tokens[...])
    row = lax.broadcasted_iota(jnp.int32, (8, T), 0)
    col = lax.broadcasted_iota(jnp.int32, (8, T), 1)
    wide = dot(jnp.where(col // NEAR == row, 1.0 / NEAR, 0.0).astype(BF), tokens[...])
    first = tokens[:BLK].astype(F32)
    last = tokens[T - BLK :].astype(F32)
    near_out[:BLK] = mean.astype(BF)
    near_out[BLK:] = jnp.where(even, last, first).astype(BF)
    far_out[...] = jnp.where(even, first, last).astype(BF)
    level_5_out[...] = packed(wide).astype(BF)


def project_kernel(tokens, weights, mean, qkv_out, coarse_out):
    tok = tokens[...]
    parts = [dot(tok, weights[number]).astype(BF) for number in range(3)]
    qkv = jnp.concatenate(parts, axis=1)
    qkv_out[...] = qkv
    coarse_out[...] = dot(mean[...], qkv)


def half_of_rows(whole, number):
    width = whole.shape[0] // 32
    return jnp.concatenate(
        [whole[(2 * j + number) * width : (2 * j + number + 1) * width] for j in range(16)], axis=0
    )


def d_attn_kernel(pos, grad_out, w_out, tokens, d_attn_out, own_out, other_out):
    d_attn_out[...] = dot_nt(grad_out[...], w_out[...]).astype(BF)
    even = pos[0] % 2 == 0
    for number, array in enumerate((tokens, grad_out)):
        cols = slice(number * T, (number + 1) * T)
        turned = array[...].T
        halves = half_of_rows(turned, 0), half_of_rows(turned, 1)
        own_out[:, cols] = jnp.where(even, halves[0], halves[1])
        other_out[:, cols] = jnp.where(even, halves[1], halves[0])


def merged(factor, first, second):
    row = lax.broadcasted_iota(jnp.int32, (BLK, BLK), 0)
    col = lax.broadcasted_iota(jnp.int32, (BLK, BLK), 1)
    same = row // 8 == col // 8
    source = col % 8 // 2
    left = jnp.where(jnp.logical_and(same, source == row % 8), factor, 0.0).astype(BF)
    right = jnp.where(jnp.logical_and(same, source + 4 == row % 8), factor, 0.0).astype(BF)
    return (dot(left, first) + dot(right, second)).astype(BF)


def merge_kernel(factor, first, second, *rest):
    if len(rest) > 1:
        rest[1][...] = rest[0][...]
    rest[-1][...] = merged(factor, first[...], second[...])


def bundle_kernel(level_5, level_6, third, fourth, chained, near, out):
    out[:BLK] = level_5[...]
    out[BLK : 2 * BLK] = level_6[...]
    out[2 * BLK : 3 * BLK] = merged(0.5, third[...], fourth[...])
    out[3 * BLK : 5 * BLK] = packed(chained[...].astype(F32)).astype(BF)
    out[5 * BLK :] = packed(near[...].astype(F32)).astype(BF)


EDGE = 2 * BLK
LEVEL_5 = 3 * BLK
SECOND = 3 * BLK


def grads_5_kernel(level_4, own, side, out):
    out[:BLK] = level_4[...]
    out[BLK : BLK + SECOND] = own[...]
    out[BLK + SECOND :] = side[...]


def grads_6(pos, own, other):
    row = lax.broadcasted_iota(jnp.int32, (8, BLK), 0)
    col = lax.broadcasted_iota(jnp.int32, (8, BLK), 1)
    pairs = jnp.where(col // 2 == row, 1.0, 0.0).astype(BF)
    low, high = by_side(pos, own, other)
    blocks = []
    for rows in (low, high):
        both = [rows[at : at + 8] for at in (LEVEL_5, LEVEL_5 + SECOND)]
        blocks.append(dot(pairs, jnp.concatenate(both, axis=0).astype(BF)))
    y_low = pos[0] // 2 % 2 == 0
    edges = []
    for rows, mine in ((high, jnp.logical_not(y_low)), (low, y_low)):
        here, there = rows[EDGE : EDGE + BLK], rows[EDGE + SECOND : EDGE + SECOND + BLK]
        edges.append(jnp.where(mine, here, there))
    return jnp.concatenate(blocks, axis=0), edges


def grads_7_kernel(pos, own, other, level_6, up, down, level_6_out, level_7_out, far_out):
    z_even = pos[0] // 4 % 2 == 0
    from_up, from_down = up[-BLK:].astype(F32), down[-BLK:].astype(F32)
    half = from_up.shape[1] // 2
    came_6 = jnp.where(z_even, from_down[:, :half], from_up[:, :half]).astype(BF)
    level_6_out[...] = came_6
    level_7_out[...] = merged(1.0, level_6[...], came_6)
    low, high = by_side(pos, own[...].astype(F32), other[...].astype(F32))
    at = slice(EDGE + SECOND, EDGE + SECOND + BLK)
    y_low = pos[0] // 2 % 2 == 0
    left = jnp.where(y_low, from_up[:, half:], high[at])
    right = jnp.where(y_low, low[at], from_down[:, half:])
    far_out[...] = jnp.where(pos[0] % 2 == 0, left, right).astype(BF)


def local_units(qkv, coarse, number):
    query = head(qkv, number).astype(F32)
    key = head(qkv, 2 + number).astype(F32)
    return (
        normed(query),
        normed(key),
        head(qkv, 4 + number),
        normed(head(coarse, number)),
        normed(head(coarse, 2 + number)),
        head(coarse, 4 + number).astype(BF),
    )


def local_weights(units, band, pairs):
    (qn, _), (kn, _), _, (qc, _), (kc, _), _ = units
    near = jnp.exp(dot_nt(qn.astype(BF), kn.astype(BF)) * SCALE) * band
    far = jnp.exp(dot_nt(qc.astype(BF), kc.astype(BF)) * SCALE) * pairs
    return near, far


def local_forward_kernel(
    qkv_ref, coarse_ref, band, pairs, spread, out, probs, turned, units_out, scales_out
):
    qkv = qkv_ref[...]
    coarse = coarse_ref[...]
    for number in range(2):
        units = local_units(qkv, coarse, number)
        near, far = (array.astype(BF) for array in local_weights(units, band[...], pairs[...]))
        total = dot(near, with_ones(units[2]))
        part = dot(far, with_ones(units[5]))
        out[:, number * 2 * DH : (number + 1) * 2 * DH] = total + dot_two(spread[...], part)
        probs[:, number * T : (number + 1) * T] = near
        probs[:, (2 + number) * T : (3 + number) * T] = far
        swapped = (units[1], units[0], units[2], units[4], units[3], units[5])
        near, far = (array.astype(BF) for array in local_weights(swapped, band[...], pairs[...]))
        turned[:, number * T : (number + 1) * T] = near
        turned[:, (2 + number) * T : (3 + number) * T] = far
        for place, (unit, scale) in enumerate((units[0], units[1], units[3], units[4])):
            at = slice((2 * place + number) * DH, (2 * place + number + 1) * DH)
            units_out[:, at] = unit
            scales_out[:, at] = jnp.broadcast_to(scale, (T, DH))


def by_side(pos, ours, others):
    even = pos[0] % 2 == 0
    return jnp.where(even, ours, others), jnp.where(even, others, ours)


def remote_rows(pos, arrived, far, levels):
    left, right = by_side(pos, far, arrived[BLK:])
    return jnp.concatenate([left, right, arrived[:BLK]] + levels, axis=0)


def own_rows(fine, coarse):
    return jnp.concatenate([fine[:BLK], fine[T - BLK :], coarse[224:]], axis=0)


def exists(pos, shape, axis):
    where = lax.broadcasted_iota(jnp.int32, shape, axis)
    no_left = jnp.logical_and(pos[0] == 0, where < BLK)
    no_right = jnp.logical_and(pos[0] == 31, jnp.logical_and(where >= BLK, where < NEAR))
    return jnp.where(jnp.logical_or(no_left, no_right), 0.0, 1.0)


def remote_weights(pos, query, remote, meets, number):
    key, key_scale = normed(head(remote, number))
    value = head(remote, 2 + number).astype(BF)
    weights = jnp.exp(dot_nt(query, key.astype(BF)) * SCALE) * meets * exists(pos, (REM, FAR), 1)
    return weights, key, key_scale, value


def gathered_rows(pos, far, mine_ref, theirs_ref):
    mine = mine_ref[...].astype(F32)
    theirs = theirs_ref[...].astype(F32)
    levels = []
    for level in range(3):
        at = slice(level * BLK, (level + 1) * BLK)
        levels += by_side(pos, unpacked(mine[at]), unpacked(theirs[at]))
    arrived = unpacked(theirs[5 * BLK :])
    return remote_rows(pos, arrived, far[...].astype(F32), levels), theirs


def turn_far_kernel(
    pos, weights_ref, near, far, mine_ref, theirs_ref, own_out, other_out, query_out
):
    even = pos[0] % 2 == 0
    rows, theirs = gathered_rows(pos, far, mine_ref, theirs_ref)
    known = near[...].astype(F32)
    left, right = by_side(pos, known[BLK:], unpacked(theirs[3 * BLK : 5 * BLK]))
    other = jnp.concatenate([left, right, known[:BLK], rows[3 * BLK :]], axis=0)
    for array, out in ((rows, own_out), (other, other_out)):
        turned = array.T
        out[...] = jnp.where(even, half_of_rows(turned, 0), half_of_rows(turned, 1)).astype(BF)
    query_out[...] = dot(rows.astype(BF), weights_ref[0]).astype(BF)


def remote_forward_kernel(
    pos, weights_ref, qkv_ref, coarse_ref, local_ref, d_attn, far, mine_ref, theirs_ref,
    meets, rim, gather,
    attn_out, both_out, level_4_out, share_out, remote_out,
):
    rows, _ = gathered_rows(pos, far, mine_ref, theirs_ref)
    even = pos[0] % 2 == 0
    rows = rows.astype(BF)
    remote = jnp.concatenate([dot(rows, weights_ref[part]) for part in (1, 2)], axis=1)
    remote = remote.astype(BF)
    remote_out[...] = remote
    remote = remote.astype(F32)
    d_nums, d_dens = [], []
    for number in range(2):
        fine = qkv_ref[:, number * DH : (number + 1) * DH].astype(F32)
        query = normed(own_rows(fine, coarse_ref[:, number * DH : (number + 1) * DH]))[0]
        weights, _, _, value = remote_weights(
            pos, query.astype(BF), remote, meets[...], number
        )
        part = dot(weights.astype(BF), with_ones(value)).astype(BF)
        total = local_ref[:, number * 2 * DH : (number + 1) * 2 * DH] + dot(rim[...], part)
        cols = slice(number * DH, (number + 1) * DH)
        inverse = 1.0 / total[:, DH:]
        attn = total[:, :DH] * inverse
        attn_out[:, cols] = attn.astype(BF)
        d_num = (d_attn[:, cols].astype(F32) * inverse).astype(BF)
        d_den = -jnp.sum(d_num.astype(F32) * attn, axis=-1, keepdims=True)
        d_nums.append(d_num)
        d_dens.append(jnp.broadcast_to(d_den, (T, DH)))
    both = jnp.concatenate(d_nums + [pack_den(*d_dens)], axis=1)
    both_out[...] = both
    sums = dot(gather[224:256, :], both)
    for number in range(2):
        den_sums = jnp.broadcast_to(packed_den(sums, number), (NEAR, DH))
        for offset, full, row_sums in (
            (0, d_nums[number].astype(F32), head(sums, number)),
            (2 * DH, d_dens[number], den_sums),
        ):
            at = slice(offset + number * DH, offset + (number + 1) * DH)
            first = full[:BLK]
            last = full[T - BLK :]
            level_4_out[:, at] = row_sums[:BLK].astype(BF)
            share = [
                jnp.where(even, last, first),
                jnp.where(even, first, last),
                row_sums[BLK:],
            ]
            share_out[:, at] = jnp.concatenate(share, axis=0).astype(BF)


def local_backward_kernel(
    pos, qkv_ref, coarse_ref, probs, turned, units_ref, scales_ref, attn_ref, both_ref,
    remote_ref, meets, gather, unmean,
    y_out, dkv_out,
):
    remote = remote_ref[...].astype(F32)
    both = both_ref[...]
    y_out[:T, T:] = attn_ref[...]
    sums = dot(gather[...], both)
    dens = both[:, 2 * DH :]
    dens_c = pack_den(*(jnp.broadcast_to(packed_den(sums, number), (T, DH)) for number in (0, 1)))
    lane = lax.broadcasted_iota(jnp.int32, (T, DH), 1)
    dqns, dkns, dvns, tables = [], [], [], []
    for number in range(2):
        cols = slice(number * DH, (number + 1) * DH)
        vals = slice((2 + number) * DH, (3 + number) * DH)
        qn, kn, qc, kc = (head(units_ref, 2 * place + number) for place in range(4))
        qc_scale, kc_scale = (head(scales_ref, 2 * place + number) for place in (2, 3))
        picks = jnp.where(lane // 2 == number, 1.0, 0.0).astype(BF)
        sides = []
        for place, d_num, den, value, query, key in (
            (0, head(both, number), dens, head(qkv_ref, 4 + number), qn, kn),
            (2, head(sums, number).astype(BF), dens_c,
             head(coarse_ref, 4 + number).astype(BF), qc, kc),
        ):
            at = slice((place + number) * T, (place + number + 1) * T)
            grad = jnp.concatenate([d_num, den], axis=1)
            value = jnp.concatenate([value, picks], axis=1)
            weights, weights_t = probs[:, at], turned[:, at]
            d_score = (weights * dot_nt(grad, value) * SCALE).astype(BF)
            d_score_t = (weights_t * dot_nt(value, grad) * SCALE).astype(BF)
            sides.append(
                (
                    dot(d_score, key.astype(BF)),
                    dot(d_score_t, query.astype(BF)),
                    dot(weights_t, d_num),
                )
            )
        (dqn, dkn, dvn), (dqc, dkc, dvc) = sides
        query = own_rows(qn, qc).astype(BF)
        weights, key_r, key_scale, value_r = remote_weights(
            pos, query, remote, meets[...], number
        )
        d_num_r = own_rows(head(both, number).astype(F32), head(sums, number)).astype(BF)
        den_r = own_rows(dens.astype(F32), dens_c.astype(F32)).astype(BF)
        picks = picks[:FAR]
        d_rem = dot_nt(
            jnp.concatenate([d_num_r, den_r], axis=1), jnp.concatenate([value_r, picks], axis=1)
        )
        d_rem = (weights * d_rem * SCALE).astype(BF)
        y_out[2 * T : 2 * T + FAR, cols] = norm_back(
            key_r, key_scale, dot_tn(d_rem, query)
        ).astype(BF)
        y_out[2 * T : 2 * T + FAR, vals] = dot_tn(weights.astype(BF), d_num_r).astype(BF)
        dqr = dot(d_rem, key_r.astype(BF))
        dqns.append(
            jnp.concatenate(
                [dqn[:BLK] + dqr[:BLK], dqn[BLK : T - BLK], dqn[T - BLK :] + dqr[BLK:NEAR]], axis=0
            )
        )
        dqc = jnp.concatenate([dqc[:224], dqc[224:] + dqr[NEAR:]], axis=0)
        dkns.append(dkn)
        dvns.append(dvn)
        tables += [norm_back(qc, qc_scale, dqc), norm_back(kc, kc_scale, dkc), dvc]
    table = dot(unmean[...], jnp.concatenate(tables, axis=1).astype(BF))
    for number in range(2):
        cols = slice(number * DH, (number + 1) * DH)
        vals = slice((2 + number) * DH, (3 + number) * DH)
        qn, kn = (head(units_ref, 2 * place + number) for place in (0, 1))
        q_scale, k_scale = (head(scales_ref, 2 * place + number) for place in (0, 1))
        dq, dk, dv = (head(table, 3 * number + place) for place in range(3))
        y_out[:T, cols] = (norm_back(qn, q_scale, dqns[number]) + dq).astype(BF)
        dk = norm_back(kn, k_scale, dkns[number]) + dk
        dv = dvns[number] + dv
        dkv_out[:, cols] = dk
        dkv_out[:, vals] = dv
        y_out[T : 2 * T, cols] = dk.astype(BF)
        y_out[T : 2 * T, vals] = dv.astype(BF)


def remote_backward_kernel(
    pos, qkv_ref, coarse_ref, local_ref, remote_ref, own_ref, other_ref, g_far, g_6, g_7,
    met, rim_mean, dkv_out,
):
    other = other_ref[...].astype(F32)
    at = slice(LEVEL_5 + SECOND, LEVEL_5 + SECOND + 8)
    sides = by_side(pos, own_ref[...].astype(F32)[at], other[at])
    levels = list(sides) + [g_6[...].astype(F32), g_7[...].astype(F32)]
    grads = remote_rows(pos, other[:NEAR], g_far[...].astype(F32), levels)
    for number in range(2):
        query = normed(head(remote_ref, number).astype(F32))[0].astype(BF)
        k_cols = slice((2 + number) * DH, (3 + number) * DH)
        v_cols = slice((4 + number) * DH, (5 + number) * DH)
        key, key_scale = normed(
            own_rows(qkv_ref[:, k_cols].astype(F32), coarse_ref[:, k_cols])
        )
        vals = own_rows(qkv_ref[:, v_cols].astype(F32), coarse_ref[:, v_cols]).astype(BF)
        weights = jnp.exp(dot_nt(query, key.astype(BF)) * SCALE)
        weights = weights * met[...] * exists(pos, (FAR, REM), 0)
        d_num = head(grads, number).astype(BF)
        d_den = head(grads, 2 + number)[:, :1]
        d_score = (weights * (dot_nt(d_num, vals) + d_den) * SCALE).astype(BF)
        dk = norm_back(key, key_scale, dot_tn(d_score, query))
        dv = dot_tn(weights.astype(BF), d_num)
        more = dot_two(rim_mean[...], jnp.concatenate([dk, dv], axis=1))
        k_cols = slice(number * DH, (number + 1) * DH)
        v_cols = slice((2 + number) * DH, (3 + number) * DH)
        dkv_out[:, k_cols] = (local_ref[:, k_cols] + more[:, :DH]).astype(BF)
        dkv_out[:, v_cols] = (local_ref[:, v_cols] + more[:, DH:]).astype(BF)


def weight_part(pos, step, own_half, other_half, own, other, own_far, other_far, out):
    z = pos[0] // 4
    width = own_half.shape[0] // 8
    at = pl.ds(pl.multiple_of((z + step) % 8 * width, width), width)
    for cols in (slice(0, T), slice(T, 2 * T)):
        total = dot(own_half[at, cols], own[:T, cols])
        total += dot(other_half[at, cols], other[:T, cols])
        out[:width, cols] = total.astype(BF)
    total = dot(own_half[at, :T], own[T : 2 * T]) + dot(own_far[at, :], own[2 * T :])
    total += dot(other_half[at, :T], other[T : 2 * T])
    total += dot(other_far[at, :], other[2 * T :])
    out[:width, 2 * T :] = total.astype(BF)


def first_weight_kernel(pos, g_own, g_other, *refs):
    up, down, level_6_out = refs[-3:]
    weight_part(pos, 4, *refs[:-3], up)
    weight_part(pos, 5, *refs[:-3], down)
    level_6, edges = grads_6(pos, g_own[...].astype(F32), g_other[...].astype(F32))
    level_6_out[...] = level_6.astype(BF)
    rows = up.shape[0] - BLK
    for out, edge in zip((up, down), edges):
        out[rows:] = jnp.concatenate([level_6, edge], axis=1).astype(BF)


def weight_kernel(steps, pos, *refs):
    for step, out in zip(steps, refs[-len(steps) :]):
        weight_part(pos, step, *refs[: -len(steps)], out)


def own_weight_kernel(pos, *refs):
    keep, send, total = refs[-3:]
    weight_part(pos, 0, *refs[:-3], total)
    half = total.shape[0] // 2
    low = pos[0] // 2 % 2 == 0
    first, second = total[:half].astype(F32), total[half:].astype(F32)
    keep[...] = jnp.where(low, first, second).astype(BF)
    send[...] = jnp.where(low, second, first).astype(BF)


def add_kernel(up, part_up, down, part_down, up_out, down_out):
    rows = part_up.shape[0]
    up_out[...] = (up[:rows].astype(F32) + part_up[...].astype(F32)).astype(BF)
    down_out[...] = (down[:rows].astype(F32) + part_down[...].astype(F32)).astype(BF)


def by_row_half(pos, total, straight, cross):
    low = pos[0] // 2 % 2 == 0
    half = total.shape[0] // 2
    straight[...] = jnp.where(low, total[:half], total[half:]).astype(BF)
    cross[...] = jnp.where(low, total[half:], total[:half]).astype(BF)


def third_step_kernel(pos, up, part_up, down, part_down, up_out, straight, cross):
    up_out[...] = (up[...].astype(F32) + part_up[...].astype(F32)).astype(BF)
    by_row_half(pos, down[...].astype(F32) + part_down[...].astype(F32), straight, cross)


def last_step_kernel(pos, up, part, straight, cross):
    by_row_half(pos, up[...].astype(F32) + part[...].astype(F32), straight, cross)


def finish_kernel(*refs):
    w_qkv, w_out = refs[-2:]
    total = refs[0][...].astype(F32)
    for ref in refs[1:-2]:
        total += ref[...].astype(F32)
    w_qkv[0] = total[:, :T]
    w_qkv[1] = total[:, 2 * T : 3 * T]
    w_qkv[2] = total[:, 3 * T :]
    w_out[...] = total[:, T : 2 * T]


def grad_x_kernel(pos, y, dkv, weights, *outs):
    x = pos[1] % 4
    side = pos[1] // 4
    for step in range(4):
        for turn in range(2):
            target = (side + turn) % 2 * 4 + (x + step) % 4
            rows = pl.ds(pl.multiple_of(target * T, T), T)
            total = dot_nt(y[:T, :T], weights[0, rows, :])
            total += dot_nt(dkv[:, :T], weights[1, rows, :])
            total += dot_nt(dkv[:, T:], weights[2, rows, :])
            outs[step][turn * T : (turn + 1) * T] = total.astype(BF)


def sum_x_kernel(first, second, third, fourth, keep, send):
    total = first[...].astype(F32) + second[...].astype(F32)
    total = total + third[...].astype(F32) + fourth[...].astype(F32)
    keep[...] = total[:T]
    send[...] = total[T:].astype(BF)


def last_x_kernel(keep, came, out):
    out[...] = (keep[...] + came[...].astype(F32)).astype(BF)


def local(tokens, w_qkv, w_out, grad_out):
    const = {name: jnp.asarray(array) for name, array in tables().items()}
    head_count = lax.axis_size("head")
    weights = jnp.transpose(w_qkv, (1, 0, 2))
    width = tokens.shape[1]
    wide = 3 * T

    def swap(array, bit):
        return lax.ppermute(array, "ctx", [(i, i ^ bit) for i in range(32)])

    def chain(array):
        pairs = [(i, (i + 1) % 32) for i in range(1, 32, 2)]
        return lax.ppermute(array, "ctx", pairs + [(b, a) for a, b in pairs])

    def turn_z(array, step, side=0):
        return lax.ppermute(
            array, "ctx", [(i, (i // 4 + step) % 8 * 4 + (i % 4 ^ side)) for i in range(32)]
        )

    call = Calls()

    near, far, level_5 = call(
        edges_kernel, [((NEAR, width), BF), ((BLK, width), BF), ((BLK, width // 2), BF)],
        tokens, placed=True,
    )
    side = swap(level_5, 2)
    qkv, coarse = call(
        project_kernel, [((T, wide), BF), ((ROWS, wide), F32)], tokens, weights, const["mean"]
    )
    far, level_6 = call(
        functools.partial(merge_kernel, 0.5), [((BLK, width), BF), ((BLK, width // 2), BF)],
        level_5, side, far, flops=1e3)
    sixes = [swap(level_6, bit) for bit in (4, 8, 12)]
    chained = chain(far)
    forward, probs, turned, units, scales = call(
        local_forward_kernel,
        [((T, 2 * T), F32)] + [((T, 4 * T), BF)] * 2 + [((T, 4 * T), F32)] * 2,
        qkv, coarse, const["band"], const["pairs"], const["spread"],
    )
    (mine,) = call(
        bundle_kernel, [((9 * BLK, width // 2), BF)], side, *sixes, chained, near, flops=1e3)
    theirs = swap(mine, 1)
    d_attn, own_half, other_half = call(
        d_attn_kernel,
        [((T, T), BF), ((width // 2, 2 * T), BF), ((width // 2, 2 * T), BF)],
        grad_out, w_out, tokens, placed=True,
    )
    sent_half = swap(other_half, 1)
    attn, both, g_4, g_share, remote = call(
        remote_forward_kernel,
        [
            ((T, T), BF), ((T, 3 * DH), BF), ((BLK, 2 * T), BF), ((3 * BLK, 2 * T), BF),
            ((FAR, 2 * T), BF),
        ],
        weights, qkv, coarse, forward, d_attn, chained, mine, theirs,
        const["meets"], const["rim"], const["gather"], placed=True,
    )
    g_side = swap(g_share, 2)
    y, dkv_local = call(
        local_backward_kernel, [((2 * T + FAR, 2 * T), BF), ((T, 2 * T), F32)],
        qkv, coarse, probs, turned, units, scales, attn, both, remote,
        const["meets"], const["gather"], const["unmean"], placed=True,
    )
    other_y = swap(y, 1)
    (g_own,) = call(
        grads_5_kernel, [((7 * BLK, 2 * T), BF)], g_4, g_share, g_side, flops=1e3
    )
    g_other = swap(g_own, 1)
    own_far, other_far, remote_q = call(
        turn_far_kernel, [((width // 2, FAR), BF)] * 2 + [((FAR, T), BF)],
        weights, near, chained, mine, theirs, placed=True,
    )
    chunk = width // 16
    factors = (own_half, sent_half, y, other_y, own_far, other_far)
    whole, half = ((chunk, 4 * T), BF), ((chunk // 2, 4 * T), BF)
    small = ((BLK, 2 * T), BF)
    message = ((chunk + BLK, 4 * T), BF)
    up, down, g_6 = call(
        first_weight_kernel, [message, message, small], g_own, g_other, *factors, placed=True
    )
    up, down = turn_z(up, 1), turn_z(down, -1)
    keep, send, _ = call(own_weight_kernel, [half, half, whole], *factors, placed=True)
    from_side = swap(send, 2)
    steps = (3, 6, 2, 7, 1)
    products = call(
        functools.partial(weight_kernel, steps), [whole] * 5, *factors, placed=True
    )
    parts = dict(zip(steps, products))
    came_6, g_7, g_far = call(
        grads_7_kernel, [small] * 3, g_own, g_other, g_6, up, down, placed=True, flops=1e3
    )
    came_7 = swap(g_7, 8)
    up, down = call(
        add_kernel, [whole] * 2, up, parts[3], down, parts[6], after=[from_side], flops=1e3
    )
    up, down = turn_z(up, 1), turn_z(down, -1)
    (dkv,) = call(
        remote_backward_kernel, [((T, 2 * T), BF)],
        qkv, coarse, dkv_local, remote_q, g_own, g_other, g_far, came_6, came_7,
        const["met"], const["rim_mean"], placed=True,
    )
    if head_count == 8:
        pieces = call(grad_x_kernel, [((2 * T, T), BF)] * 4, y, dkv, weights, placed=True)

        def turn_x(array, step):
            pairs = [(i, i // 4 * 4 + (i % 4 + step) % 4) for i in range(8)]
            return lax.ppermute(array, "head", pairs)

        came = [turn_x(pieces[step], step) for step in (1, 2, 3)]
    up, straight, cross = call(
        third_step_kernel, [whole, half, half],
        up, parts[2], down, parts[7], placed=True, flops=1e3,
    )
    up = turn_z(up, 1)
    from_down = [turn_z(straight, -1), turn_z(cross, -1, 2)]
    if head_count == 8:
        keep_x, send_x = call(
            sum_x_kernel, [((T, T), F32), ((T, T), BF)], pieces[0], *came, flops=1e3
        )
        came_x = lax.ppermute(send_x, "head", [(i, i ^ 4) for i in range(8)])
    straight, cross = call(
        last_step_kernel, [half, half], up, parts[1], placed=True, flops=1e3
    )
    from_up = [turn_z(straight, 1), turn_z(cross, 1, 2)]
    grad_wqkv, grad_wout = call(
        finish_kernel, [((3, chunk // 2, T), F32), ((chunk // 2, T), F32)],
        keep, from_side, *from_down, *from_up,
    )
    if head_count == 8:
        (grad_x,) = call(last_x_kernel, [((T, T), BF)], keep_x, came_x)
    else:
        flat = jnp.transpose(weights, (1, 0, 2)).reshape(width, wide)
        grad_x = dot_nt(jnp.concatenate([y[:T, :T], dkv], axis=1), flat).astype(BF)
    return grad_x, jnp.transpose(grad_wqkv, (1, 0, 2)), grad_wout.T


def solution(mesh):
    placed = (P("ctx", None), P(None, None, "head"), P("head", None), P("ctx", None))
    return jax.shard_map(
        local,
        mesh=mesh,
        in_specs=placed,
        out_specs=(P("ctx", "head"), P("ctx", None, "head"), P("head", "ctx")),
        check_vma=False,
    )
```

```python
import functools

import jax
import jax.numpy as jnp
import numpy as np
from jax import lax
from jax.experimental import pallas as pl
from jax.experimental.pallas import tpu as pltpu
from jax.sharding import PartitionSpec as P

DH = 128
BLK = 16
T = 256
ROWS = 256
NEAR = 2 * BLK
REM = 64
FAR = 96
SCALE = DH**-0.5
BF = jnp.bfloat16
F32 = jnp.float32

STARTS = {1: 0, 2: 128, 3: 192, 4: 224, 5: 240, 6: 248, 7: 252}


def tables():
    spread = np.zeros((T, ROWS), np.float32)
    mean = np.zeros((ROWS, T), np.float32)
    pairs = np.zeros((ROWS, ROWS), np.float32)
    for level, start in STARTS.items():
        factor = 2**level
        for row in range(T // factor):
            spread[row * factor : (row + 1) * factor, start + row] = 1.0
            mean[start + row, row * factor : (row + 1) * factor] = 1.0 / factor
        if level <= 3:
            for block in range(T // factor // BLK):
                other = start + (block ^ 1) * BLK
                mine = start + block * BLK
                pairs[mine : mine + BLK, other : other + BLK] = 1.0
    block_of = np.arange(T) // BLK
    band = (np.abs(block_of[:, None] - block_of[None, :]) <= 1).astype(np.float32)
    rim = np.zeros((T, REM), np.float32)
    rim[:BLK, :BLK] = np.eye(BLK)
    rim[T - BLK :, BLK:NEAR] = np.eye(BLK)
    rim[:, NEAR:] = spread[:, 224:]
    rim_mean = rim.copy()
    rim_mean[:, NEAR:] = mean.T[:, 224:]
    meets = np.zeros((REM, FAR), np.float32)
    meets[0:16, 0:16] = 1.0
    meets[16:32, 16:32] = 1.0
    meets[32:48, 32:48] = 1.0
    meets[48:56, 48:64] = 1.0
    meets[56:60, 64:80] = 1.0
    meets[60:62, 80:96] = 1.0
    bf = lambda array: np.asarray(array, dtype=BF)
    return {
        "spread": bf(spread),
        "gather": bf(spread.T),
        "mean": bf(mean),
        "unmean": bf(mean.T),
        "band": band,
        "pairs": pairs,
        "rim": bf(rim),
        "rim_mean": bf(rim_mean),
        "meets": meets,
        "met": np.ascontiguousarray(meets.T),
    }


def dot(left, right):
    return jnp.dot(left, right, preferred_element_type=F32)


def dot_nt(left, right):
    return lax.dot_general(left, right, (((1,), (1,)), ((), ())), preferred_element_type=F32)


def dot_tn(left, right):
    return lax.dot_general(left, right, (((0,), (0,)), ((), ())), preferred_element_type=F32)


def dot_two(exact, right):
    high = right.astype(BF)
    low = (right - high.astype(F32)).astype(BF)
    return dot(exact, high) + dot(exact, low)


def normed(values):
    scale = lax.rsqrt(jnp.mean(values * values, axis=-1, keepdims=True) + 1e-06)
    return values * scale, scale


def norm_back(unit, scale, grad):
    return scale * (grad - unit * jnp.mean(grad * unit, axis=-1, keepdims=True))


def head(array, number):
    return array[:, number * DH : (number + 1) * DH]


def pack_den(d_den_0, d_den_1):
    lane = lax.broadcasted_iota(jnp.int32, (T, DH), 1)
    total = jnp.zeros((T, DH), F32)
    for number, array in enumerate((d_den_0, d_den_1)):
        high = array.astype(BF).astype(F32)
        total = jnp.where(lane == 2 * number, high, total)
        total = jnp.where(lane == 2 * number + 1, array - high, total)
    return total.astype(BF)


def packed_den(sums, number):
    at = 2 * DH + 2 * number
    return sums[:, at : at + 1] + sums[:, at + 1 : at + 2]


def with_ones(values):
    return jnp.concatenate([values, jnp.ones_like(values)], axis=1)


class Calls:
    def __init__(self):
        self.token = None

    def __call__(self, kernel, outs, *args, placed=False, after=(), flops=1e10):
        first = tuple(after) if self.token is None else (self.token,) + tuple(after)
        skipped = len(first)
        args = first + args
        specs = [pl.BlockSpec(memory_space=pltpu.VMEM)] * len(args)

        def body(*refs):
            refs = refs[skipped:-1]
            if placed:
                kernel((lax.axis_index("ctx"), lax.axis_index("head")), *refs)
            else:
                kernel(*refs)

        shapes = [jax.ShapeDtypeStruct(shape, dtype) for shape, dtype in outs]
        shapes.append(jax.ShapeDtypeStruct((8, 128), F32))
        results = pl.pallas_call(
            body,
            out_shape=tuple(shapes),
            in_specs=specs,
            out_specs=tuple(pl.BlockSpec(memory_space=pltpu.VMEM) for _ in shapes),
            compiler_params=pltpu.CompilerParams(vmem_limit_bytes=44 * 1024 * 1024),
            cost_estimate=pl.CostEstimate(
                flops=int(flops), bytes_accessed=1000, transcendentals=0
            ),
        )(*args)
        self.token = results[-1]
        return results[:-1]


def packed(rows):
    half = rows.shape[1] // 2
    return jnp.concatenate([rows[:, :half], rows[:, half:]], axis=0)


def unpacked(rows):
    half = rows.shape[0] // 2
    return jnp.concatenate([rows[:half], rows[half:]], axis=1)


def edges_kernel(pos, tokens, near_out, far_out, level_5_out):
    even = pos[0] % 2 == 0
    row = lax.broadcasted_iota(jnp.int32, (BLK, T), 0)
    col = lax.broadcasted_iota(jnp.int32, (BLK, T), 1)
    mean = dot(jnp.where(col // BLK == row, 1.0 / BLK, 0.0).astype(BF), tokens[...])
    row = lax.broadcasted_iota(jnp.int32, (8, T), 0)
    col = lax.broadcasted_iota(jnp.int32, (8, T), 1)
    wide = dot(jnp.where(col // NEAR == row, 1.0 / NEAR, 0.0).astype(BF), tokens[...])
    first = tokens[:BLK].astype(F32)
    last = tokens[T - BLK :].astype(F32)
    near_out[:BLK] = mean.astype(BF)
    near_out[BLK:] = jnp.where(even, last, first).astype(BF)
    far_out[...] = jnp.where(even, first, last).astype(BF)
    level_5_out[...] = packed(wide).astype(BF)


def project_kernel(tokens, weights, mean, qkv_out, coarse_out):
    tok = tokens[...]
    parts = [dot(tok, weights[number]).astype(BF) for number in range(3)]
    qkv = jnp.concatenate(parts, axis=1)
    qkv_out[...] = qkv
    coarse_out[...] = dot(mean[...], qkv)


def half_of_rows(whole, number):
    width = whole.shape[0] // 32
    return jnp.concatenate(
        [whole[(2 * j + number) * width : (2 * j + number + 1) * width] for j in range(16)], axis=0
    )


def d_attn_kernel(pos, grad_out, w_out, tokens, d_attn_out, own_out, other_out):
    d_attn_out[...] = dot_nt(grad_out[...], w_out[...]).astype(BF)
    even = pos[0] % 2 == 0
    for number, array in enumerate((tokens, grad_out)):
        cols = slice(number * T, (number + 1) * T)
        turned = array[...].T
        halves = half_of_rows(turned, 0), half_of_rows(turned, 1)
        own_out[:, cols] = jnp.where(even, halves[0], halves[1])
        other_out[:, cols] = jnp.where(even, halves[1], halves[0])


def merged(factor, first, second):
    row = lax.broadcasted_iota(jnp.int32, (BLK, BLK), 0)
    col = lax.broadcasted_iota(jnp.int32, (BLK, BLK), 1)
    same = row // 8 == col // 8
    source = col % 8 // 2
    left = jnp.where(jnp.logical_and(same, source == row % 8), factor, 0.0).astype(BF)
    right = jnp.where(jnp.logical_and(same, source + 4 == row % 8), factor, 0.0).astype(BF)
    return (dot(left, first) + dot(right, second)).astype(BF)


def merge_kernel(factor, first, second, *rest):
    if len(rest) > 1:
        rest[1][...] = rest[0][...]
    rest[-1][...] = merged(factor, first[...], second[...])


def bundle_kernel(level_5, level_6, third, fourth, chained, near, out):
    out[:BLK] = level_5[...]
    out[BLK : 2 * BLK] = level_6[...]
    out[2 * BLK : 3 * BLK] = merged(0.5, third[...], fourth[...])
    out[3 * BLK : 5 * BLK] = packed(chained[...].astype(F32)).astype(BF)
    out[5 * BLK :] = packed(near[...].astype(F32)).astype(BF)


EDGE = 2 * BLK
LEVEL_5 = 3 * BLK
SECOND = 3 * BLK


def grads_5_kernel(level_4, own, side, out):
    out[:BLK] = level_4[...]
    out[BLK : BLK + SECOND] = own[...]
    out[BLK + SECOND :] = side[...]


def grads_6(pos, own, other):
    row = lax.broadcasted_iota(jnp.int32, (8, BLK), 0)
    col = lax.broadcasted_iota(jnp.int32, (8, BLK), 1)
    pairs = jnp.where(col // 2 == row, 1.0, 0.0).astype(BF)
    low, high = by_side(pos, own, other)
    blocks = []
    for rows in (low, high):
        both = [rows[at : at + 8] for at in (LEVEL_5, LEVEL_5 + SECOND)]
        blocks.append(dot(pairs, jnp.concatenate(both, axis=0).astype(BF)))
    y_low = pos[0] // 2 % 2 == 0
    edges = []
    for rows, mine in ((high, jnp.logical_not(y_low)), (low, y_low)):
        here, there = rows[EDGE : EDGE + BLK], rows[EDGE + SECOND : EDGE + SECOND + BLK]
        edges.append(jnp.where(mine, here, there))
    return jnp.concatenate(blocks, axis=0), edges


def grads_7_kernel(pos, own, other, level_6, up, down, level_6_out, level_7_out, far_out):
    z_even = pos[0] // 4 % 2 == 0
    from_up, from_down = up[-BLK:].astype(F32), down[-BLK:].astype(F32)
    half = from_up.shape[1] // 2
    came_6 = jnp.where(z_even, from_down[:, :half], from_up[:, :half]).astype(BF)
    level_6_out[...] = came_6
    level_7_out[...] = merged(1.0, level_6[...], came_6)
    low, high = by_side(pos, own[...].astype(F32), other[...].astype(F32))
    at = slice(EDGE + SECOND, EDGE + SECOND + BLK)
    y_low = pos[0] // 2 % 2 == 0
    left = jnp.where(y_low, from_up[:, half:], high[at])
    right = jnp.where(y_low, low[at], from_down[:, half:])
    far_out[...] = jnp.where(pos[0] % 2 == 0, left, right).astype(BF)


def local_units(qkv, coarse, number):
    query = head(qkv, number).astype(F32)
    key = head(qkv, 2 + number).astype(F32)
    return (
        normed(query),
        normed(key),
        head(qkv, 4 + number),
        normed(head(coarse, number)),
        normed(head(coarse, 2 + number)),
        head(coarse, 4 + number).astype(BF),
    )


def local_weights(units, band, pairs):
    (qn, _), (kn, _), _, (qc, _), (kc, _), _ = units
    near = jnp.exp(dot_nt(qn.astype(BF), kn.astype(BF)) * SCALE) * band
    far = jnp.exp(dot_nt(qc.astype(BF), kc.astype(BF)) * SCALE) * pairs
    return near, far


def local_forward_kernel(
    qkv_ref, coarse_ref, band, pairs, spread, out, probs, turned, units_out, scales_out
):
    qkv = qkv_ref[...]
    coarse = coarse_ref[...]
    for number in range(2):
        units = local_units(qkv, coarse, number)
        near, far = (array.astype(BF) for array in local_weights(units, band[...], pairs[...]))
        total = dot(near, with_ones(units[2]))
        part = dot(far, with_ones(units[5]))
        out[:, number * 2 * DH : (number + 1) * 2 * DH] = total + dot_two(spread[...], part)
        probs[:, number * T : (number + 1) * T] = near
        probs[:, (2 + number) * T : (3 + number) * T] = far
        swapped = (units[1], units[0], units[2], units[4], units[3], units[5])
        near, far = (array.astype(BF) for array in local_weights(swapped, band[...], pairs[...]))
        turned[:, number * T : (number + 1) * T] = near
        turned[:, (2 + number) * T : (3 + number) * T] = far
        for place, (unit, scale) in enumerate((units[0], units[1], units[3], units[4])):
            at = slice((2 * place + number) * DH, (2 * place + number + 1) * DH)
            units_out[:, at] = unit
            scales_out[:, at] = jnp.broadcast_to(scale, (T, DH))


def by_side(pos, ours, others):
    even = pos[0] % 2 == 0
    return jnp.where(even, ours, others), jnp.where(even, others, ours)


def remote_rows(pos, arrived, far, levels):
    left, right = by_side(pos, far, arrived[BLK:])
    return jnp.concatenate([left, right, arrived[:BLK]] + levels, axis=0)


def own_rows(fine, coarse):
    return jnp.concatenate([fine[:BLK], fine[T - BLK :], coarse[224:]], axis=0)


def exists(pos, shape, axis):
    where = lax.broadcasted_iota(jnp.int32, shape, axis)
    no_left = jnp.logical_and(pos[0] == 0, where < BLK)
    no_right = jnp.logical_and(pos[0] == 31, jnp.logical_and(where >= BLK, where < NEAR))
    return jnp.where(jnp.logical_or(no_left, no_right), 0.0, 1.0)


def remote_weights(pos, query, remote, meets, number):
    key, key_scale = normed(head(remote, number))
    value = head(remote, 2 + number).astype(BF)
    weights = jnp.exp(dot_nt(query, key.astype(BF)) * SCALE) * meets * exists(pos, (REM, FAR), 1)
    return weights, key, key_scale, value


def gathered_rows(pos, far, mine_ref, theirs_ref):
    mine = mine_ref[...].astype(F32)
    theirs = theirs_ref[...].astype(F32)
    levels = []
    for level in range(3):
        at = slice(level * BLK, (level + 1) * BLK)
        levels += by_side(pos, unpacked(mine[at]), unpacked(theirs[at]))
    arrived = unpacked(theirs[5 * BLK :])
    return remote_rows(pos, arrived, far[...].astype(F32), levels), theirs


def turn_far_kernel(
    pos, weights_ref, near, far, mine_ref, theirs_ref, own_out, other_out, query_out
):
    even = pos[0] % 2 == 0
    rows, theirs = gathered_rows(pos, far, mine_ref, theirs_ref)
    known = near[...].astype(F32)
    left, right = by_side(pos, known[BLK:], unpacked(theirs[3 * BLK : 5 * BLK]))
    other = jnp.concatenate([left, right, known[:BLK], rows[3 * BLK :]], axis=0)
    for array, out in ((rows, own_out), (other, other_out)):
        turned = array.T
        out[...] = jnp.where(even, half_of_rows(turned, 0), half_of_rows(turned, 1)).astype(BF)
    query_out[...] = dot(rows.astype(BF), weights_ref[0]).astype(BF)


def remote_forward_kernel(
    pos, weights_ref, qkv_ref, coarse_ref, local_ref, d_attn, far, mine_ref, theirs_ref,
    meets, rim, gather,
    attn_out, both_out, level_4_out, share_out, remote_out,
):
    rows, _ = gathered_rows(pos, far, mine_ref, theirs_ref)
    even = pos[0] % 2 == 0
    rows = rows.astype(BF)
    remote = jnp.concatenate([dot(rows, weights_ref[part]) for part in (1, 2)], axis=1)
    remote = remote.astype(BF)
    remote_out[...] = remote
    remote = remote.astype(F32)
    d_nums, d_dens = [], []
    for number in range(2):
        fine = qkv_ref[:, number * DH : (number + 1) * DH].astype(F32)
        query = normed(own_rows(fine, coarse_ref[:, number * DH : (number + 1) * DH]))[0]
        weights, _, _, value = remote_weights(
            pos, query.astype(BF), remote, meets[...], number
        )
        part = dot(weights.astype(BF), with_ones(value)).astype(BF)
        total = local_ref[:, number * 2 * DH : (number + 1) * 2 * DH] + dot(rim[...], part)
        cols = slice(number * DH, (number + 1) * DH)
        inverse = 1.0 / total[:, DH:]
        attn = total[:, :DH] * inverse
        attn_out[:, cols] = attn.astype(BF)
        d_num = (d_attn[:, cols].astype(F32) * inverse).astype(BF)
        d_den = -jnp.sum(d_num.astype(F32) * attn, axis=-1, keepdims=True)
        d_nums.append(d_num)
        d_dens.append(jnp.broadcast_to(d_den, (T, DH)))
    both = jnp.concatenate(d_nums + [pack_den(*d_dens)], axis=1)
    both_out[...] = both
    sums = dot(gather[224:256, :], both)
    for number in range(2):
        den_sums = jnp.broadcast_to(packed_den(sums, number), (NEAR, DH))
        for offset, full, row_sums in (
            (0, d_nums[number].astype(F32), head(sums, number)),
            (2 * DH, d_dens[number], den_sums),
        ):
            at = slice(offset + number * DH, offset + (number + 1) * DH)
            first = full[:BLK]
            last = full[T - BLK :]
            level_4_out[:, at] = row_sums[:BLK].astype(BF)
            share = [
                jnp.where(even, last, first),
                jnp.where(even, first, last),
                row_sums[BLK:],
            ]
            share_out[:, at] = jnp.concatenate(share, axis=0).astype(BF)


def local_backward_kernel(
    pos, qkv_ref, coarse_ref, probs, turned, units_ref, scales_ref, attn_ref, both_ref,
    remote_ref, meets, gather, unmean,
    y_out, dkv_out,
):
    remote = remote_ref[...].astype(F32)
    both = both_ref[...]
    y_out[:T, T:] = attn_ref[...]
    sums = dot(gather[...], both)
    dens = both[:, 2 * DH :]
    dens_c = pack_den(*(jnp.broadcast_to(packed_den(sums, number), (T, DH)) for number in (0, 1)))
    lane = lax.broadcasted_iota(jnp.int32, (T, DH), 1)
    dqns, dkns, dvns, tables = [], [], [], []
    for number in range(2):
        cols = slice(number * DH, (number + 1) * DH)
        vals = slice((2 + number) * DH, (3 + number) * DH)
        qn, kn, qc, kc = (head(units_ref, 2 * place + number) for place in range(4))
        qc_scale, kc_scale = (head(scales_ref, 2 * place + number) for place in (2, 3))
        picks = jnp.where(lane // 2 == number, 1.0, 0.0).astype(BF)
        sides = []
        for place, d_num, den, value, query, key in (
            (0, head(both, number), dens, head(qkv_ref, 4 + number), qn, kn),
            (2, head(sums, number).astype(BF), dens_c,
             head(coarse_ref, 4 + number).astype(BF), qc, kc),
        ):
            at = slice((place + number) * T, (place + number + 1) * T)
            grad = jnp.concatenate([d_num, den], axis=1)
            value = jnp.concatenate([value, picks], axis=1)
            weights, weights_t = probs[:, at], turned[:, at]
            d_score = (weights * dot_nt(grad, value) * SCALE).astype(BF)
            d_score_t = (weights_t * dot_nt(value, grad) * SCALE).astype(BF)
            sides.append(
                (
                    dot(d_score, key.astype(BF)),
                    dot(d_score_t, query.astype(BF)),
                    dot(weights_t, d_num),
                )
            )
        (dqn, dkn, dvn), (dqc, dkc, dvc) = sides
        query = own_rows(qn, qc).astype(BF)
        weights, key_r, key_scale, value_r = remote_weights(
            pos, query, remote, meets[...], number
        )
        d_num_r = own_rows(head(both, number).astype(F32), head(sums, number)).astype(BF)
        den_r = own_rows(dens.astype(F32), dens_c.astype(F32)).astype(BF)
        picks = picks[:FAR]
        d_rem = dot_nt(
            jnp.concatenate([d_num_r, den_r], axis=1), jnp.concatenate([value_r, picks], axis=1)
        )
        d_rem = (weights * d_rem * SCALE).astype(BF)
        y_out[2 * T : 2 * T + FAR, cols] = norm_back(
            key_r, key_scale, dot_tn(d_rem, query)
        ).astype(BF)
        y_out[2 * T : 2 * T + FAR, vals] = dot_tn(weights.astype(BF), d_num_r).astype(BF)
        dqr = dot(d_rem, key_r.astype(BF))
        dqns.append(
            jnp.concatenate(
                [dqn[:BLK] + dqr[:BLK], dqn[BLK : T - BLK], dqn[T - BLK :] + dqr[BLK:NEAR]], axis=0
            )
        )
        dqc = jnp.concatenate([dqc[:224], dqc[224:] + dqr[NEAR:]], axis=0)
        dkns.append(dkn)
        dvns.append(dvn)
        tables += [norm_back(qc, qc_scale, dqc), norm_back(kc, kc_scale, dkc), dvc]
    table = dot(unmean[...], jnp.concatenate(tables, axis=1).astype(BF))
    for number in range(2):
        cols = slice(number * DH, (number + 1) * DH)
        vals = slice((2 + number) * DH, (3 + number) * DH)
        qn, kn = (head(units_ref, 2 * place + number) for place in (0, 1))
        q_scale, k_scale = (head(scales_ref, 2 * place + number) for place in (0, 1))
        dq, dk, dv = (head(table, 3 * number + place) for place in range(3))
        y_out[:T, cols] = (norm_back(qn, q_scale, dqns[number]) + dq).astype(BF)
        dk = norm_back(kn, k_scale, dkns[number]) + dk
        dv = dvns[number] + dv
        dkv_out[:, cols] = dk
        dkv_out[:, vals] = dv
        y_out[T : 2 * T, cols] = dk.astype(BF)
        y_out[T : 2 * T, vals] = dv.astype(BF)


def remote_backward_kernel(
    pos, qkv_ref, coarse_ref, local_ref, remote_ref, own_ref, other_ref, g_far, g_6, g_7,
    met, rim_mean, dkv_out,
):
    other = other_ref[...].astype(F32)
    at = slice(LEVEL_5 + SECOND, LEVEL_5 + SECOND + 8)
    sides = by_side(pos, own_ref[...].astype(F32)[at], other[at])
    levels = list(sides) + [g_6[...].astype(F32), g_7[...].astype(F32)]
    grads = remote_rows(pos, other[:NEAR], g_far[...].astype(F32), levels)
    for number in range(2):
        query = normed(head(remote_ref, number).astype(F32))[0].astype(BF)
        k_cols = slice((2 + number) * DH, (3 + number) * DH)
        v_cols = slice((4 + number) * DH, (5 + number) * DH)
        key, key_scale = normed(
            own_rows(qkv_ref[:, k_cols].astype(F32), coarse_ref[:, k_cols])
        )
        vals = own_rows(qkv_ref[:, v_cols].astype(F32), coarse_ref[:, v_cols]).astype(BF)
        weights = jnp.exp(dot_nt(query, key.astype(BF)) * SCALE)
        weights = weights * met[...] * exists(pos, (FAR, REM), 0)
        d_num = head(grads, number).astype(BF)
        d_den = head(grads, 2 + number)[:, :1]
        d_score = (weights * (dot_nt(d_num, vals) + d_den) * SCALE).astype(BF)
        dk = norm_back(key, key_scale, dot_tn(d_score, query))
        dv = dot_tn(weights.astype(BF), d_num)
        more = dot_two(rim_mean[...], jnp.concatenate([dk, dv], axis=1))
        k_cols = slice(number * DH, (number + 1) * DH)
        v_cols = slice((2 + number) * DH, (3 + number) * DH)
        dkv_out[:, k_cols] = (local_ref[:, k_cols] + more[:, :DH]).astype(BF)
        dkv_out[:, v_cols] = (local_ref[:, v_cols] + more[:, DH:]).astype(BF)


def weight_part(pos, step, own_half, other_half, own, other, own_far, other_far, out):
    z = pos[0] // 4
    width = own_half.shape[0] // 8
    at = pl.ds(pl.multiple_of((z + step) % 8 * width, width), width)
    for cols in (slice(0, T), slice(T, 2 * T)):
        total = dot(own_half[at, cols], own[:T, cols])
        total += dot(other_half[at, cols], other[:T, cols])
        out[:width, cols] = total.astype(BF)
    total = dot(own_half[at, :T], own[T : 2 * T]) + dot(own_far[at, :], own[2 * T :])
    total += dot(other_half[at, :T], other[T : 2 * T])
    total += dot(other_far[at, :], other[2 * T :])
    out[:width, 2 * T :] = total.astype(BF)


def first_weight_kernel(pos, g_own, g_other, *refs):
    up, down, level_6_out = refs[-3:]
    weight_part(pos, 4, *refs[:-3], up)
    weight_part(pos, 5, *refs[:-3], down)
    level_6, edges = grads_6(pos, g_own[...].astype(F32), g_other[...].astype(F32))
    level_6_out[...] = level_6.astype(BF)
    rows = up.shape[0] - BLK
    for out, edge in zip((up, down), edges):
        out[rows:] = jnp.concatenate([level_6, edge], axis=1).astype(BF)


def weight_kernel(steps, pos, *refs):
    for step, out in zip(steps, refs[-len(steps) :]):
        weight_part(pos, step, *refs[: -len(steps)], out)


def own_weight_kernel(pos, *refs):
    keep_0, keep_1, send, total = refs[-4:]
    half = total.shape[0] // 2
    low = pos[0] // 2 % 2 == 0
    for step, keep in enumerate((keep_0, keep_1)):
        weight_part(pos, step, *refs[:-4], total)
        first, second = total[:half].astype(F32), total[half:].astype(F32)
        keep[...] = jnp.where(low, first, second).astype(BF)
        send[step * half : (step + 1) * half] = jnp.where(low, second, first).astype(BF)


def add_kernel(up, part_up, down, part_down, up_out, down_out):
    rows = part_up.shape[0]
    up_out[...] = (up[:rows].astype(F32) + part_up[...].astype(F32)).astype(BF)
    down_out[...] = (down[:rows].astype(F32) + part_down[...].astype(F32)).astype(BF)


def by_row_half(pos, total, straight, cross):
    low = pos[0] // 2 % 2 == 0
    half = total.shape[0] // 2
    straight[...] = jnp.where(low, total[:half], total[half:]).astype(BF)
    cross[...] = jnp.where(low, total[half:], total[:half]).astype(BF)


def third_step_kernel(pos, up, part_up, down, part_down, *outs):
    by_row_half(pos, up[...].astype(F32) + part_up[...].astype(F32), *outs[:2])
    by_row_half(pos, down[...].astype(F32) + part_down[...].astype(F32), *outs[2:])


def last_step_kernel(cross, straight, keep, side, out):
    total = cross[...].astype(F32) + straight[...].astype(F32)
    rows = total.shape[0]
    out[...] = (total + keep[...].astype(F32) + side[rows:].astype(F32)).astype(BF)


def finish_kernel(*refs):
    w_qkv, w_out = refs[-2:]
    total = refs[0][...].astype(F32)
    for ref in refs[1:-2]:
        total += ref[: total.shape[0]].astype(F32)
    w_qkv[0] = total[:, :T]
    w_qkv[1] = total[:, 2 * T : 3 * T]
    w_qkv[2] = total[:, 3 * T :]
    w_out[...] = total[:, T : 2 * T]


def grad_x_kernel(pos, y, dkv, weights, *outs):
    x = pos[1] % 4
    side = pos[1] // 4
    for step in range(4):
        for turn in range(2):
            target = (side + turn) % 2 * 4 + (x + step) % 4
            rows = pl.ds(pl.multiple_of(target * T, T), T)
            total = dot_nt(y[:T, :T], weights[0, rows, :])
            total += dot_nt(dkv[:, :T], weights[1, rows, :])
            total += dot_nt(dkv[:, T:], weights[2, rows, :])
            outs[step][turn * T : (turn + 1) * T] = total.astype(BF)


def sum_x_kernel(first, second, third, fourth, keep, send):
    total = first[...].astype(F32) + second[...].astype(F32)
    total = total + third[...].astype(F32) + fourth[...].astype(F32)
    keep[...] = total[:T]
    send[...] = total[T:].astype(BF)


def last_x_kernel(keep, came, out):
    out[...] = (keep[...] + came[...].astype(F32)).astype(BF)


def local(tokens, w_qkv, w_out, grad_out):
    const = {name: jnp.asarray(array) for name, array in tables().items()}
    head_count = lax.axis_size("head")
    weights = jnp.transpose(w_qkv, (1, 0, 2))
    width = tokens.shape[1]
    wide = 3 * T

    def swap(array, bit):
        return lax.ppermute(array, "ctx", [(i, i ^ bit) for i in range(32)])

    def chain(array):
        pairs = [(i, (i + 1) % 32) for i in range(1, 32, 2)]
        return lax.ppermute(array, "ctx", pairs + [(b, a) for a, b in pairs])

    def turn_z(array, step, side=0):
        return lax.ppermute(
            array, "ctx", [(i, (i // 4 + step) % 8 * 4 + (i % 4 ^ side)) for i in range(32)]
        )

    call = Calls()

    near, far, level_5 = call(
        edges_kernel, [((NEAR, width), BF), ((BLK, width), BF), ((BLK, width // 2), BF)],
        tokens, placed=True,
    )
    side = swap(level_5, 2)
    qkv, coarse = call(
        project_kernel, [((T, wide), BF), ((ROWS, wide), F32)], tokens, weights, const["mean"]
    )
    far, level_6 = call(
        functools.partial(merge_kernel, 0.5), [((BLK, width), BF), ((BLK, width // 2), BF)],
        level_5, side, far, flops=1e3)
    sixes = [swap(level_6, bit) for bit in (4, 8, 12)]
    chained = chain(far)
    forward, probs, turned, units, scales = call(
        local_forward_kernel,
        [((T, 2 * T), F32)] + [((T, 4 * T), BF)] * 2 + [((T, 4 * T), F32)] * 2,
        qkv, coarse, const["band"], const["pairs"], const["spread"],
    )
    (mine,) = call(
        bundle_kernel, [((9 * BLK, width // 2), BF)], side, *sixes, chained, near, flops=1e3)
    theirs = swap(mine, 1)
    d_attn, own_half, other_half = call(
        d_attn_kernel,
        [((T, T), BF), ((width // 2, 2 * T), BF), ((width // 2, 2 * T), BF)],
        grad_out, w_out, tokens, placed=True,
    )
    sent_half = swap(other_half, 1)
    attn, both, g_4, g_share, remote = call(
        remote_forward_kernel,
        [
            ((T, T), BF), ((T, 3 * DH), BF), ((BLK, 2 * T), BF), ((3 * BLK, 2 * T), BF),
            ((FAR, 2 * T), BF),
        ],
        weights, qkv, coarse, forward, d_attn, chained, mine, theirs,
        const["meets"], const["rim"], const["gather"], placed=True,
    )
    g_side = swap(g_share, 2)
    y, dkv_local = call(
        local_backward_kernel, [((2 * T + FAR, 2 * T), BF), ((T, 2 * T), F32)],
        qkv, coarse, probs, turned, units, scales, attn, both, remote,
        const["meets"], const["gather"], const["unmean"], placed=True,
    )
    other_y = swap(y, 1)
    (g_own,) = call(
        grads_5_kernel, [((7 * BLK, 2 * T), BF)], g_4, g_share, g_side, flops=1e3
    )
    g_other = swap(g_own, 1)
    own_far, other_far, remote_q = call(
        turn_far_kernel, [((width // 2, FAR), BF)] * 2 + [((FAR, T), BF)],
        weights, near, chained, mine, theirs, placed=True,
    )
    chunk = width // 16
    factors = (own_half, sent_half, y, other_y, own_far, other_far)
    whole, half = ((chunk, 4 * T), BF), ((chunk // 2, 4 * T), BF)
    small = ((BLK, 2 * T), BF)
    message = ((chunk + BLK, 4 * T), BF)
    up, down, g_6 = call(
        first_weight_kernel, [message, message, small], g_own, g_other, *factors, placed=True
    )
    up, down = turn_z(up, 1), turn_z(down, -1)
    keep, keep_1, send, _ = call(
        own_weight_kernel, [half, half, whole, whole], *factors, placed=True
    )
    from_side = swap(send, 2)
    steps = (3, 6, 2, 7)
    products = call(
        functools.partial(weight_kernel, steps), [whole] * 4, *factors, placed=True
    )
    parts = dict(zip(steps, products))
    came_6, g_7, g_far = call(
        grads_7_kernel, [small] * 3, g_own, g_other, g_6, up, down, placed=True, flops=1e3
    )
    came_7 = swap(g_7, 8)
    up, down = call(
        add_kernel, [whole] * 2, up, parts[3], down, parts[6], after=[from_side], flops=1e3
    )
    up, down = turn_z(up, 1), turn_z(down, -1)
    (dkv,) = call(
        remote_backward_kernel, [((T, 2 * T), BF)],
        qkv, coarse, dkv_local, remote_q, g_own, g_other, g_far, came_6, came_7,
        const["met"], const["rim_mean"], placed=True,
    )
    if head_count == 8:
        pieces = call(grad_x_kernel, [((2 * T, T), BF)] * 4, y, dkv, weights, placed=True)

        def turn_x(array, step):
            pairs = [(i, i // 4 * 4 + (i % 4 + step) % 4) for i in range(8)]
            return lax.ppermute(array, "head", pairs)

        came = [turn_x(pieces[step], step) for step in (1, 2, 3)]
    up_straight, up_cross, straight, cross = call(
        third_step_kernel, [half] * 4, up, parts[2], down, parts[7], placed=True, flops=1e3
    )
    up = [turn_z(up_cross, 1, 2), turn_z(up_straight, 1)]
    from_down = [turn_z(straight, -1), turn_z(cross, -1, 2)]
    if head_count == 8:
        keep_x, send_x = call(
            sum_x_kernel, [((T, T), F32), ((T, T), BF)], pieces[0], *came, flops=1e3
        )
        came_x = lax.ppermute(send_x, "head", [(i, i ^ 4) for i in range(8)])
    (last,) = call(last_step_kernel, [half], *up, keep_1, from_side, flops=1e3)
    from_up = [turn_z(last, 1)]
    grad_wqkv, grad_wout = call(
        finish_kernel, [((3, chunk // 2, T), F32), ((chunk // 2, T), F32)],
        keep, from_side, *from_down, *from_up,
    )
    if head_count == 8:
        (grad_x,) = call(last_x_kernel, [((T, T), BF)], keep_x, came_x)
    else:
        flat = jnp.transpose(weights, (1, 0, 2)).reshape(width, wide)
        grad_x = dot_nt(jnp.concatenate([y[:T, :T], dkv], axis=1), flat).astype(BF)
    return grad_x, jnp.transpose(grad_wqkv, (1, 0, 2)), grad_wout.T


def solution(mesh):
    placed = (P("ctx", None), P(None, None, "head"), P("head", None), P("ctx", None))
    return jax.shard_map(
        local,
        mesh=mesh,
        in_specs=placed,
        out_specs=(P("ctx", "head"), P("ctx", None, "head"), P("head", "ctx")),
        check_vma=False,
    )
```

```python
import functools

import jax
import jax.numpy as jnp
import numpy as np
from jax import lax
from jax.experimental import pallas as pl
from jax.experimental.pallas import tpu as pltpu
from jax.sharding import PartitionSpec as P

DH = 128
BLK = 16
T = 256
ROWS = 256
NEAR = 2 * BLK
REM = 64
FAR = 96
SCALE = DH**-0.5
BF = jnp.bfloat16
F32 = jnp.float32

STARTS = {1: 0, 2: 128, 3: 192, 4: 224, 5: 240, 6: 248, 7: 252}


def tables():
    spread = np.zeros((T, ROWS), np.float32)
    mean = np.zeros((ROWS, T), np.float32)
    pairs = np.zeros((ROWS, ROWS), np.float32)
    for level, start in STARTS.items():
        factor = 2**level
        for row in range(T // factor):
            spread[row * factor : (row + 1) * factor, start + row] = 1.0
            mean[start + row, row * factor : (row + 1) * factor] = 1.0 / factor
        if level <= 3:
            for block in range(T // factor // BLK):
                other = start + (block ^ 1) * BLK
                mine = start + block * BLK
                pairs[mine : mine + BLK, other : other + BLK] = 1.0
    block_of = np.arange(T) // BLK
    band = (np.abs(block_of[:, None] - block_of[None, :]) <= 1).astype(np.float32)
    rim = np.zeros((T, REM), np.float32)
    rim[:BLK, :BLK] = np.eye(BLK)
    rim[T - BLK :, BLK:NEAR] = np.eye(BLK)
    rim[:, NEAR:] = spread[:, 224:]
    rim_mean = rim.copy()
    rim_mean[:, NEAR:] = mean.T[:, 224:]
    meets = np.zeros((REM, FAR), np.float32)
    meets[0:16, 0:16] = 1.0
    meets[16:32, 16:32] = 1.0
    meets[32:48, 32:48] = 1.0
    meets[48:56, 48:64] = 1.0
    meets[56:60, 64:80] = 1.0
    meets[60:62, 80:96] = 1.0
    bf = lambda array: np.asarray(array, dtype=BF)
    return {
        "spread": bf(spread),
        "gather": bf(spread.T),
        "mean": bf(mean),
        "unmean": bf(mean.T),
        "band": band,
        "pairs": pairs,
        "rim": bf(rim),
        "rim_mean": bf(rim_mean),
        "meets": meets,
        "met": np.ascontiguousarray(meets.T),
    }


def dot(left, right):
    return jnp.dot(left, right, preferred_element_type=F32)


def dot_nt(left, right):
    return lax.dot_general(left, right, (((1,), (1,)), ((), ())), preferred_element_type=F32)


def dot_tn(left, right):
    return lax.dot_general(left, right, (((0,), (0,)), ((), ())), preferred_element_type=F32)


def dot_two(exact, right):
    high = right.astype(BF)
    low = (right - high.astype(F32)).astype(BF)
    return dot(exact, high) + dot(exact, low)


def normed(values):
    scale = lax.rsqrt(jnp.mean(values * values, axis=-1, keepdims=True) + 1e-06)
    return values * scale, scale


def norm_back(unit, scale, grad):
    return scale * (grad - unit * jnp.mean(grad * unit, axis=-1, keepdims=True))


def head(array, number):
    return array[:, number * DH : (number + 1) * DH]


def pack_den(d_den_0, d_den_1):
    lane = lax.broadcasted_iota(jnp.int32, (T, DH), 1)
    total = jnp.zeros((T, DH), F32)
    for number, array in enumerate((d_den_0, d_den_1)):
        high = array.astype(BF).astype(F32)
        total = jnp.where(lane == 2 * number, high, total)
        total = jnp.where(lane == 2 * number + 1, array - high, total)
    return total.astype(BF)


def packed_den(sums, number):
    at = 2 * DH + 2 * number
    return sums[:, at : at + 1] + sums[:, at + 1 : at + 2]


def with_ones(values):
    return jnp.concatenate([values, jnp.ones_like(values)], axis=1)


class Calls:
    def __init__(self):
        self.token = None

    def __call__(self, kernel, outs, *args, placed=False, after=(), flops=1e10):
        first = tuple(after) if self.token is None else (self.token,) + tuple(after)
        skipped = len(first)
        args = first + args
        specs = [pl.BlockSpec(memory_space=pltpu.VMEM)] * len(args)

        def body(*refs):
            refs = refs[skipped:-1]
            if placed:
                kernel((lax.axis_index("ctx"), lax.axis_index("head")), *refs)
            else:
                kernel(*refs)

        shapes = [jax.ShapeDtypeStruct(shape, dtype) for shape, dtype in outs]
        shapes.append(jax.ShapeDtypeStruct((8, 128), F32))
        results = pl.pallas_call(
            body,
            out_shape=tuple(shapes),
            in_specs=specs,
            out_specs=tuple(pl.BlockSpec(memory_space=pltpu.VMEM) for _ in shapes),
            compiler_params=pltpu.CompilerParams(vmem_limit_bytes=44 * 1024 * 1024),
            cost_estimate=pl.CostEstimate(
                flops=int(flops), bytes_accessed=1000, transcendentals=0
            ),
        )(*args)
        self.token = results[-1]
        return results[:-1]


def packed(rows):
    half = rows.shape[1] // 2
    return jnp.concatenate([rows[:, :half], rows[:, half:]], axis=0)


def unpacked(rows):
    half = rows.shape[0] // 2
    return jnp.concatenate([rows[:half], rows[half:]], axis=1)


def edges_kernel(pos, tokens, near_out, far_out, level_5_out):
    even = pos[0] % 2 == 0
    row = lax.broadcasted_iota(jnp.int32, (BLK, T), 0)
    col = lax.broadcasted_iota(jnp.int32, (BLK, T), 1)
    mean = dot(jnp.where(col // BLK == row, 1.0 / BLK, 0.0).astype(BF), tokens[...])
    row = lax.broadcasted_iota(jnp.int32, (8, T), 0)
    col = lax.broadcasted_iota(jnp.int32, (8, T), 1)
    wide = dot(jnp.where(col // NEAR == row, 1.0 / NEAR, 0.0).astype(BF), tokens[...])
    first = tokens[:BLK].astype(F32)
    last = tokens[T - BLK :].astype(F32)
    near_out[:BLK] = mean.astype(BF)
    near_out[BLK:] = jnp.where(even, last, first).astype(BF)
    far_out[...] = jnp.where(even, first, last).astype(BF)
    level_5_out[...] = packed(wide).astype(BF)


def project_kernel(tokens, weights, mean, qkv_out, coarse_out):
    tok = tokens[...]
    parts = [dot(tok, weights[number]).astype(BF) for number in range(3)]
    qkv = jnp.concatenate(parts, axis=1)
    qkv_out[...] = qkv
    coarse_out[...] = dot(mean[...], qkv)


def half_of_rows(whole, number):
    width = whole.shape[0] // 32
    return jnp.concatenate(
        [whole[(2 * j + number) * width : (2 * j + number + 1) * width] for j in range(16)], axis=0
    )


def d_attn_kernel(pos, grad_out, w_out, tokens, d_attn_out, own_out, other_out):
    d_attn_out[...] = dot_nt(grad_out[...], w_out[...]).astype(BF)
    even = pos[0] % 2 == 0
    for number, array in enumerate((tokens, grad_out)):
        cols = slice(number * T, (number + 1) * T)
        turned = array[...].T
        halves = half_of_rows(turned, 0), half_of_rows(turned, 1)
        own_out[:, cols] = jnp.where(even, halves[0], halves[1])
        other_out[:, cols] = jnp.where(even, halves[1], halves[0])


def merged(factor, first, second):
    row = lax.broadcasted_iota(jnp.int32, (BLK, BLK), 0)
    col = lax.broadcasted_iota(jnp.int32, (BLK, BLK), 1)
    same = row // 8 == col // 8
    source = col % 8 // 2
    left = jnp.where(jnp.logical_and(same, source == row % 8), factor, 0.0).astype(BF)
    right = jnp.where(jnp.logical_and(same, source + 4 == row % 8), factor, 0.0).astype(BF)
    return (dot(left, first) + dot(right, second)).astype(BF)


def merge_kernel(factor, first, second, *rest):
    if len(rest) > 1:
        rest[1][...] = rest[0][...]
    rest[-1][...] = merged(factor, first[...], second[...])


def bundle_kernel(level_5, level_6, third, fourth, chained, near, out):
    out[:BLK] = level_5[...]
    out[BLK : 2 * BLK] = level_6[...]
    out[2 * BLK : 3 * BLK] = merged(0.5, third[...], fourth[...])
    out[3 * BLK : 5 * BLK] = packed(chained[...].astype(F32)).astype(BF)
    out[5 * BLK :] = packed(near[...].astype(F32)).astype(BF)


EDGE = 2 * BLK
LEVEL_5 = 3 * BLK
SECOND = 3 * BLK


def grads_5_kernel(level_4, own, side, out):
    out[:BLK] = level_4[...]
    out[BLK : BLK + SECOND] = own[...]
    out[BLK + SECOND :] = side[...]


def grads_6(pos, own, other):
    row = lax.broadcasted_iota(jnp.int32, (8, BLK), 0)
    col = lax.broadcasted_iota(jnp.int32, (8, BLK), 1)
    pairs = jnp.where(col // 2 == row, 1.0, 0.0).astype(BF)
    low, high = by_side(pos, own, other)
    blocks = []
    for rows in (low, high):
        both = [rows[at : at + 8] for at in (LEVEL_5, LEVEL_5 + SECOND)]
        blocks.append(dot(pairs, jnp.concatenate(both, axis=0).astype(BF)))
    y_low = pos[0] // 2 % 2 == 0
    edges = []
    for rows, mine in ((high, jnp.logical_not(y_low)), (low, y_low)):
        here, there = rows[EDGE : EDGE + BLK], rows[EDGE + SECOND : EDGE + SECOND + BLK]
        edges.append(jnp.where(mine, here, there))
    return jnp.concatenate(blocks, axis=0), edges


def grads_7_kernel(pos, own, other, level_6, up, down, level_6_out, level_7_out, far_out):
    z_even = pos[0] // 4 % 2 == 0
    from_up, from_down = up[-BLK:].astype(F32), down[-BLK:].astype(F32)
    half = from_up.shape[1] // 2
    came_6 = jnp.where(z_even, from_down[:, :half], from_up[:, :half]).astype(BF)
    level_6_out[...] = came_6
    level_7_out[...] = merged(1.0, level_6[...], came_6)
    low, high = by_side(pos, own[...].astype(F32), other[...].astype(F32))
    at = slice(EDGE + SECOND, EDGE + SECOND + BLK)
    y_low = pos[0] // 2 % 2 == 0
    left = jnp.where(y_low, from_up[:, half:], high[at])
    right = jnp.where(y_low, low[at], from_down[:, half:])
    far_out[...] = jnp.where(pos[0] % 2 == 0, left, right).astype(BF)


def local_units(qkv, coarse, number):
    query = head(qkv, number).astype(F32)
    key = head(qkv, 2 + number).astype(F32)
    return (
        normed(query),
        normed(key),
        head(qkv, 4 + number),
        normed(head(coarse, number)),
        normed(head(coarse, 2 + number)),
        head(coarse, 4 + number).astype(BF),
    )


def local_weights(units, band, pairs):
    (qn, _), (kn, _), _, (qc, _), (kc, _), _ = units
    near = jnp.exp(dot_nt(qn.astype(BF), kn.astype(BF)) * SCALE) * band
    far = jnp.exp(dot_nt(qc.astype(BF), kc.astype(BF)) * SCALE) * pairs
    return near, far


def local_forward_kernel(
    qkv_ref, coarse_ref, band, pairs, spread, out, probs, turned, units_out, scales_out
):
    qkv = qkv_ref[...]
    coarse = coarse_ref[...]
    for number in range(2):
        units = local_units(qkv, coarse, number)
        near, far = (array.astype(BF) for array in local_weights(units, band[...], pairs[...]))
        total = dot(near, with_ones(units[2]))
        part = dot(far, with_ones(units[5]))
        out[:, number * 2 * DH : (number + 1) * 2 * DH] = total + dot_two(spread[...], part)
        probs[:, number * T : (number + 1) * T] = near
        probs[:, (2 + number) * T : (3 + number) * T] = far
        swapped = (units[1], units[0], units[2], units[4], units[3], units[5])
        near, far = (array.astype(BF) for array in local_weights(swapped, band[...], pairs[...]))
        turned[:, number * T : (number + 1) * T] = near
        turned[:, (2 + number) * T : (3 + number) * T] = far
        for place, (unit, scale) in enumerate((units[0], units[1], units[3], units[4])):
            at = slice((2 * place + number) * DH, (2 * place + number + 1) * DH)
            units_out[:, at] = unit
            scales_out[:, at] = jnp.broadcast_to(scale, (T, DH))


def by_side(pos, ours, others):
    even = pos[0] % 2 == 0
    return jnp.where(even, ours, others), jnp.where(even, others, ours)


def remote_rows(pos, arrived, far, levels):
    left, right = by_side(pos, far, arrived[BLK:])
    return jnp.concatenate([left, right, arrived[:BLK]] + levels, axis=0)


def own_rows(fine, coarse):
    return jnp.concatenate([fine[:BLK], fine[T - BLK :], coarse[224:]], axis=0)


def exists(pos, shape, axis):
    where = lax.broadcasted_iota(jnp.int32, shape, axis)
    no_left = jnp.logical_and(pos[0] == 0, where < BLK)
    no_right = jnp.logical_and(pos[0] == 31, jnp.logical_and(where >= BLK, where < NEAR))
    return jnp.where(jnp.logical_or(no_left, no_right), 0.0, 1.0)


def remote_weights(pos, query, remote, meets, number):
    key, key_scale = normed(head(remote, number))
    value = head(remote, 2 + number).astype(BF)
    weights = jnp.exp(dot_nt(query, key.astype(BF)) * SCALE) * meets * exists(pos, (REM, FAR), 1)
    return weights, key, key_scale, value


def gathered_rows(pos, far, mine_ref, theirs_ref):
    mine = mine_ref[...].astype(F32)
    theirs = theirs_ref[...].astype(F32)
    levels = []
    for level in range(3):
        at = slice(level * BLK, (level + 1) * BLK)
        levels += by_side(pos, unpacked(mine[at]), unpacked(theirs[at]))
    arrived = unpacked(theirs[5 * BLK :])
    return remote_rows(pos, arrived, far[...].astype(F32), levels), theirs


def turn_far_kernel(
    pos, weights_ref, near, far, mine_ref, theirs_ref, own_out, other_out, query_out
):
    even = pos[0] % 2 == 0
    rows, theirs = gathered_rows(pos, far, mine_ref, theirs_ref)
    known = near[...].astype(F32)
    left, right = by_side(pos, known[BLK:], unpacked(theirs[3 * BLK : 5 * BLK]))
    other = jnp.concatenate([left, right, known[:BLK], rows[3 * BLK :]], axis=0)
    for array, out in ((rows, own_out), (other, other_out)):
        turned = array.T
        out[...] = jnp.where(even, half_of_rows(turned, 0), half_of_rows(turned, 1)).astype(BF)
    query_out[...] = dot(rows.astype(BF), weights_ref[0]).astype(BF)


def remote_forward_kernel(
    pos, weights_ref, qkv_ref, coarse_ref, local_ref, d_attn, far, mine_ref, theirs_ref,
    meets, rim, gather,
    attn_out, both_out, level_4_out, share_out, remote_out,
):
    rows, _ = gathered_rows(pos, far, mine_ref, theirs_ref)
    even = pos[0] % 2 == 0
    rows = rows.astype(BF)
    remote = jnp.concatenate([dot(rows, weights_ref[part]) for part in (1, 2)], axis=1)
    remote = remote.astype(BF)
    remote_out[...] = remote
    remote = remote.astype(F32)
    d_nums, d_dens = [], []
    for number in range(2):
        fine = qkv_ref[:, number * DH : (number + 1) * DH].astype(F32)
        query = normed(own_rows(fine, coarse_ref[:, number * DH : (number + 1) * DH]))[0]
        weights, _, _, value = remote_weights(
            pos, query.astype(BF), remote, meets[...], number
        )
        part = dot(weights.astype(BF), with_ones(value)).astype(BF)
        total = local_ref[:, number * 2 * DH : (number + 1) * 2 * DH] + dot(rim[...], part)
        cols = slice(number * DH, (number + 1) * DH)
        inverse = 1.0 / total[:, DH:]
        attn = total[:, :DH] * inverse
        attn_out[:, cols] = attn.astype(BF)
        d_num = (d_attn[:, cols].astype(F32) * inverse).astype(BF)
        d_den = -jnp.sum(d_num.astype(F32) * attn, axis=-1, keepdims=True)
        d_nums.append(d_num)
        d_dens.append(jnp.broadcast_to(d_den, (T, DH)))
    both = jnp.concatenate(d_nums + [pack_den(*d_dens)], axis=1)
    both_out[...] = both
    sums = dot(gather[224:256, :], both)
    for number in range(2):
        den_sums = jnp.broadcast_to(packed_den(sums, number), (NEAR, DH))
        for offset, full, row_sums in (
            (0, d_nums[number].astype(F32), head(sums, number)),
            (2 * DH, d_dens[number], den_sums),
        ):
            at = slice(offset + number * DH, offset + (number + 1) * DH)
            first = full[:BLK]
            last = full[T - BLK :]
            level_4_out[:, at] = row_sums[:BLK].astype(BF)
            share = [
                jnp.where(even, last, first),
                jnp.where(even, first, last),
                row_sums[BLK:],
            ]
            share_out[:, at] = jnp.concatenate(share, axis=0).astype(BF)


def local_backward_kernel(
    pos, qkv_ref, coarse_ref, probs, turned, units_ref, scales_ref, attn_ref, both_ref,
    remote_ref, meets, gather, unmean,
    y_out, dkv_out,
):
    remote = remote_ref[...].astype(F32)
    both = both_ref[...]
    y_out[:T, T:] = attn_ref[...]
    sums = dot(gather[...], both)
    dens = both[:, 2 * DH :]
    dens_c = pack_den(*(jnp.broadcast_to(packed_den(sums, number), (T, DH)) for number in (0, 1)))
    lane = lax.broadcasted_iota(jnp.int32, (T, DH), 1)
    dqns, dkns, dvns, tables = [], [], [], []
    for number in range(2):
        cols = slice(number * DH, (number + 1) * DH)
        vals = slice((2 + number) * DH, (3 + number) * DH)
        qn, kn, qc, kc = (head(units_ref, 2 * place + number) for place in range(4))
        qc_scale, kc_scale = (head(scales_ref, 2 * place + number) for place in (2, 3))
        picks = jnp.where(lane // 2 == number, 1.0, 0.0).astype(BF)
        sides = []
        for place, d_num, den, value, query, key in (
            (0, head(both, number), dens, head(qkv_ref, 4 + number), qn, kn),
            (2, head(sums, number).astype(BF), dens_c,
             head(coarse_ref, 4 + number).astype(BF), qc, kc),
        ):
            at = slice((place + number) * T, (place + number + 1) * T)
            grad = jnp.concatenate([d_num, den], axis=1)
            value = jnp.concatenate([value, picks], axis=1)
            weights, weights_t = probs[:, at], turned[:, at]
            d_score = (weights * dot_nt(grad, value) * SCALE).astype(BF)
            d_score_t = (weights_t * dot_nt(value, grad) * SCALE).astype(BF)
            sides.append(
                (
                    dot(d_score, key.astype(BF)),
                    dot(d_score_t, query.astype(BF)),
                    dot(weights_t, d_num),
                )
            )
        (dqn, dkn, dvn), (dqc, dkc, dvc) = sides
        query = own_rows(qn, qc).astype(BF)
        weights, key_r, key_scale, value_r = remote_weights(
            pos, query, remote, meets[...], number
        )
        d_num_r = own_rows(head(both, number).astype(F32), head(sums, number)).astype(BF)
        den_r = own_rows(dens.astype(F32), dens_c.astype(F32)).astype(BF)
        picks = picks[:FAR]
        d_rem = dot_nt(
            jnp.concatenate([d_num_r, den_r], axis=1), jnp.concatenate([value_r, picks], axis=1)
        )
        d_rem = (weights * d_rem * SCALE).astype(BF)
        y_out[2 * T : 2 * T + FAR, cols] = norm_back(
            key_r, key_scale, dot_tn(d_rem, query)
        ).astype(BF)
        y_out[2 * T : 2 * T + FAR, vals] = dot_tn(weights.astype(BF), d_num_r).astype(BF)
        dqr = dot(d_rem, key_r.astype(BF))
        dqns.append(
            jnp.concatenate(
                [dqn[:BLK] + dqr[:BLK], dqn[BLK : T - BLK], dqn[T - BLK :] + dqr[BLK:NEAR]], axis=0
            )
        )
        dqc = jnp.concatenate([dqc[:224], dqc[224:] + dqr[NEAR:]], axis=0)
        dkns.append(dkn)
        dvns.append(dvn)
        tables += [norm_back(qc, qc_scale, dqc), norm_back(kc, kc_scale, dkc), dvc]
    table = dot(unmean[...], jnp.concatenate(tables, axis=1).astype(BF))
    for number in range(2):
        cols = slice(number * DH, (number + 1) * DH)
        vals = slice((2 + number) * DH, (3 + number) * DH)
        qn, kn = (head(units_ref, 2 * place + number) for place in (0, 1))
        q_scale, k_scale = (head(scales_ref, 2 * place + number) for place in (0, 1))
        dq, dk, dv = (head(table, 3 * number + place) for place in range(3))
        y_out[:T, cols] = (norm_back(qn, q_scale, dqns[number]) + dq).astype(BF)
        dk = norm_back(kn, k_scale, dkns[number]) + dk
        dv = dvns[number] + dv
        dkv_out[:, cols] = dk
        dkv_out[:, vals] = dv
        y_out[T : 2 * T, cols] = dk.astype(BF)
        y_out[T : 2 * T, vals] = dv.astype(BF)


def remote_backward_kernel(
    pos, qkv_ref, coarse_ref, local_ref, remote_ref, own_ref, other_ref, g_far, g_6, g_7,
    met, rim_mean, dkv_out,
):
    other = other_ref[...].astype(F32)
    at = slice(LEVEL_5 + SECOND, LEVEL_5 + SECOND + 8)
    sides = by_side(pos, own_ref[...].astype(F32)[at], other[at])
    levels = list(sides) + [g_6[...].astype(F32), g_7[...].astype(F32)]
    grads = remote_rows(pos, other[:NEAR], g_far[...].astype(F32), levels)
    for number in range(2):
        query = normed(head(remote_ref, number).astype(F32))[0].astype(BF)
        k_cols = slice((2 + number) * DH, (3 + number) * DH)
        v_cols = slice((4 + number) * DH, (5 + number) * DH)
        key, key_scale = normed(
            own_rows(qkv_ref[:, k_cols].astype(F32), coarse_ref[:, k_cols])
        )
        vals = own_rows(qkv_ref[:, v_cols].astype(F32), coarse_ref[:, v_cols]).astype(BF)
        weights = jnp.exp(dot_nt(query, key.astype(BF)) * SCALE)
        weights = weights * met[...] * exists(pos, (FAR, REM), 0)
        d_num = head(grads, number).astype(BF)
        d_den = head(grads, 2 + number)[:, :1]
        d_score = (weights * (dot_nt(d_num, vals) + d_den) * SCALE).astype(BF)
        dk = norm_back(key, key_scale, dot_tn(d_score, query))
        dv = dot_tn(weights.astype(BF), d_num)
        more = dot_two(rim_mean[...], jnp.concatenate([dk, dv], axis=1))
        k_cols = slice(number * DH, (number + 1) * DH)
        v_cols = slice((2 + number) * DH, (3 + number) * DH)
        dkv_out[:, k_cols] = (local_ref[:, k_cols] + more[:, :DH]).astype(BF)
        dkv_out[:, v_cols] = (local_ref[:, v_cols] + more[:, DH:]).astype(BF)


def weight_part(pos, step, own_half, other_half, own, other, own_far, other_far, out):
    z = pos[0] // 4
    width = own_half.shape[0] // 8
    at = pl.ds(pl.multiple_of((z + step) % 8 * width, width), width)
    for cols in (slice(0, T), slice(T, 2 * T)):
        total = dot(own_half[at, cols], own[:T, cols])
        total += dot(other_half[at, cols], other[:T, cols])
        out[:width, cols] = total.astype(BF)
    total = dot(own_half[at, :T], own[T : 2 * T]) + dot(own_far[at, :], own[2 * T :])
    total += dot(other_half[at, :T], other[T : 2 * T])
    total += dot(other_far[at, :], other[2 * T :])
    out[:width, 2 * T :] = total.astype(BF)


def first_weight_kernel(pos, g_own, g_other, *refs):
    up, down, level_6_out = refs[-3:]
    weight_part(pos, 4, *refs[:-3], up)
    weight_part(pos, 5, *refs[:-3], down)
    level_6, edges = grads_6(pos, g_own[...].astype(F32), g_other[...].astype(F32))
    level_6_out[...] = level_6.astype(BF)
    rows = up.shape[0] - BLK
    for out, edge in zip((up, down), edges):
        out[rows:] = jnp.concatenate([level_6, edge], axis=1).astype(BF)


def weight_kernel(steps, pos, *refs):
    for step, out in zip(steps, refs[-len(steps) :]):
        weight_part(pos, step, *refs[: -len(steps)], out)


def own_weight_kernel(pos, *refs):
    keep_0, keep_1, send, total = refs[-4:]
    half = total.shape[0] // 2
    low = pos[0] // 2 % 2 == 0
    for step, keep in enumerate((keep_0, keep_1)):
        weight_part(pos, step, *refs[:-4], total)
        first, second = total[:half].astype(F32), total[half:].astype(F32)
        keep[...] = jnp.where(low, first, second).astype(BF)
        send[step * half : (step + 1) * half] = jnp.where(low, second, first).astype(BF)


def add_kernel(up, part_up, down, part_down, up_out, down_out):
    rows = part_up.shape[0]
    up_out[...] = (up[:rows].astype(F32) + part_up[...].astype(F32)).astype(BF)
    down_out[...] = (down[:rows].astype(F32) + part_down[...].astype(F32)).astype(BF)


def by_row_half(pos, total, straight, cross):
    low = pos[0] // 2 % 2 == 0
    half = total.shape[0] // 2
    straight[...] = jnp.where(low, total[:half], total[half:]).astype(BF)
    cross[...] = jnp.where(low, total[half:], total[:half]).astype(BF)


def third_step_kernel(pos, up, part_up, down, part_down, *outs):
    by_row_half(pos, up[...].astype(F32) + part_up[...].astype(F32), *outs[:2])
    by_row_half(pos, down[...].astype(F32) + part_down[...].astype(F32), *outs[2:])


def last_step_kernel(cross, straight, keep, side, out):
    total = cross[...].astype(F32) + straight[...].astype(F32)
    rows = total.shape[0]
    out[...] = (total + keep[...].astype(F32) + side[rows:].astype(F32)).astype(BF)


def finish_kernel(*refs):
    w_qkv, w_out = refs[-2:]
    total = refs[0][...].astype(F32)
    for ref in refs[1:-2]:
        total += ref[: total.shape[0]].astype(F32)
    w_qkv[0] = total[:, :T]
    w_qkv[1] = total[:, 2 * T : 3 * T]
    w_qkv[2] = total[:, 3 * T :]
    w_out[...] = total[:, T : 2 * T]


def grad_x_kernel(pos, y, dkv, weights, *outs):
    x = pos[1] % 4
    side = pos[1] // 4
    for step in range(4):
        for turn in range(2):
            target = (side + turn) % 2 * 4 + (x + step) % 4
            rows = pl.ds(pl.multiple_of(target * T, T), T)
            total = dot_nt(y[:T, :T], weights[0, rows, :])
            total += dot_nt(dkv[:, :T], weights[1, rows, :])
            total += dot_nt(dkv[:, T:], weights[2, rows, :])
            outs[step][turn * T : (turn + 1) * T] = total.astype(BF)


def sum_x_kernel(first, second, third, fourth, keep, send):
    total = first[...].astype(F32) + second[...].astype(F32)
    total = total + third[...].astype(F32) + fourth[...].astype(F32)
    keep[...] = total[:T]
    send[...] = total[T:].astype(BF)


def last_x_kernel(keep, came, out):
    out[...] = (keep[...] + came[...].astype(F32)).astype(BF)


def local(tokens, w_qkv, w_out, grad_out):
    const = {name: jnp.asarray(array) for name, array in tables().items()}
    head_count = lax.axis_size("head")
    weights = jnp.transpose(w_qkv, (1, 0, 2))
    width = tokens.shape[1]
    wide = 3 * T

    def swap(array, bit):
        return lax.ppermute(array, "ctx", [(i, i ^ bit) for i in range(32)])

    def chain(array):
        pairs = [(i, (i + 1) % 32) for i in range(1, 32, 2)]
        return lax.ppermute(array, "ctx", pairs + [(b, a) for a, b in pairs])

    def turn_z(array, step, side=0):
        return lax.ppermute(
            array, "ctx", [(i, (i // 4 + step) % 8 * 4 + (i % 4 ^ side)) for i in range(32)]
        )

    call = Calls()

    near, far, level_5 = call(
        edges_kernel, [((NEAR, width), BF), ((BLK, width), BF), ((BLK, width // 2), BF)],
        tokens, placed=True,
    )
    side = swap(level_5, 2)
    qkv, coarse = call(
        project_kernel, [((T, wide), BF), ((ROWS, wide), F32)], tokens, weights, const["mean"]
    )
    far, level_6 = call(
        functools.partial(merge_kernel, 0.5), [((BLK, width), BF), ((BLK, width // 2), BF)],
        level_5, side, far, flops=1e3)
    sixes = [swap(level_6, bit) for bit in (4, 8, 12)]
    chained = chain(far)
    forward, probs, turned, units, scales = call(
        local_forward_kernel,
        [((T, 2 * T), F32)] + [((T, 4 * T), BF)] * 2 + [((T, 4 * T), F32)] * 2,
        qkv, coarse, const["band"], const["pairs"], const["spread"],
    )
    (mine,) = call(
        bundle_kernel, [((9 * BLK, width // 2), BF)], side, *sixes, chained, near, flops=1e3)
    theirs = swap(mine, 1)
    d_attn, own_half, other_half = call(
        d_attn_kernel,
        [((T, T), BF), ((width // 2, 2 * T), BF), ((width // 2, 2 * T), BF)],
        grad_out, w_out, tokens, placed=True,
    )
    sent_half = swap(other_half, 1)
    attn, both, g_4, g_share, remote = call(
        remote_forward_kernel,
        [
            ((T, T), BF), ((T, 3 * DH), BF), ((BLK, 2 * T), BF), ((3 * BLK, 2 * T), BF),
            ((FAR, 2 * T), BF),
        ],
        weights, qkv, coarse, forward, d_attn, chained, mine, theirs,
        const["meets"], const["rim"], const["gather"], placed=True,
    )
    g_side = swap(g_share, 2)
    y, dkv_local = call(
        local_backward_kernel, [((2 * T + FAR, 2 * T), BF), ((T, 2 * T), F32)],
        qkv, coarse, probs, turned, units, scales, attn, both, remote,
        const["meets"], const["gather"], const["unmean"], placed=True,
    )
    other_y = swap(y, 1)
    (g_own,) = call(
        grads_5_kernel, [((7 * BLK, 2 * T), BF)], g_4, g_share, g_side, flops=1e3
    )
    g_other = swap(g_own, 1)
    own_far, other_far, remote_q = call(
        turn_far_kernel, [((width // 2, FAR), BF)] * 2 + [((FAR, T), BF)],
        weights, near, chained, mine, theirs, placed=True,
    )
    chunk = width // 16
    factors = (own_half, sent_half, y, other_y, own_far, other_far)
    whole, half = ((chunk, 4 * T), BF), ((chunk // 2, 4 * T), BF)
    small = ((BLK, 2 * T), BF)
    message = ((chunk + BLK, 4 * T), BF)
    up, down, g_6 = call(
        first_weight_kernel, [message, message, small], g_own, g_other, *factors, placed=True
    )
    up, down = turn_z(up, 1), turn_z(down, -1)
    keep, keep_1, send, _ = call(
        own_weight_kernel, [half, half, whole, whole], *factors, placed=True
    )
    from_side = swap(send, 2)
    steps = (3, 6, 2, 7)
    products = call(
        functools.partial(weight_kernel, steps), [whole] * 4, *factors, placed=True
    )
    parts = dict(zip(steps, products))
    came_6, g_7, g_far = call(
        grads_7_kernel, [small] * 3, g_own, g_other, g_6, up, down, placed=True, flops=1e3
    )
    came_7 = swap(g_7, 8)
    up, down = call(
        add_kernel, [whole] * 2, up, parts[3], down, parts[6], after=[from_side], flops=1e3
    )
    up, down = turn_z(up, 1), turn_z(down, -1)
    (dkv,) = call(
        remote_backward_kernel, [((T, 2 * T), BF)],
        qkv, coarse, dkv_local, remote_q, g_own, g_other, g_far, came_6, came_7,
        const["met"], const["rim_mean"], placed=True,
    )
    if head_count == 8:
        pieces = call(grad_x_kernel, [((2 * T, T), BF)] * 4, y, dkv, weights, placed=True)

        def turn_x(array, step):
            pairs = [(i, i // 4 * 4 + (i % 4 + step) % 4) for i in range(8)]
            return lax.ppermute(array, "head", pairs)

        came = [turn_x(pieces[step], step) for step in (1, 2, 3)]
    up_straight, up_cross, straight, cross = call(
        third_step_kernel, [half] * 4, up, parts[2], down, parts[7], placed=True, flops=1e3
    )
    up = [turn_z(up_cross, 1, 2), turn_z(up_straight, 1)]
    from_down = [turn_z(cross, -1, 2), turn_z(straight, -1)]
    if head_count == 8:
        keep_x, send_x = call(
            sum_x_kernel, [((T, T), F32), ((T, T), BF)], pieces[0], *came, flops=1e3
        )
        came_x = lax.ppermute(send_x, "head", [(i, i ^ 4) for i in range(8)])
    (last,) = call(last_step_kernel, [half], *up, keep_1, from_side, flops=1e3)
    from_up = [turn_z(last, 1)]
    grad_wqkv, grad_wout = call(
        finish_kernel, [((3, chunk // 2, T), F32), ((chunk // 2, T), F32)],
        keep, from_side, *from_down, *from_up,
    )
    if head_count == 8:
        (grad_x,) = call(last_x_kernel, [((T, T), BF)], keep_x, came_x)
    else:
        flat = jnp.transpose(weights, (1, 0, 2)).reshape(width, wide)
        grad_x = dot_nt(jnp.concatenate([y[:T, :T], dkv], axis=1), flat).astype(BF)
    return grad_x, jnp.transpose(grad_wqkv, (1, 0, 2)), grad_wout.T


def solution(mesh):
    placed = (P("ctx", None), P(None, None, "head"), P("head", None), P("ctx", None))
    return jax.shard_map(
        local,
        mesh=mesh,
        in_specs=placed,
        out_specs=(P("ctx", "head"), P("ctx", None, "head"), P("head", "ctx")),
        check_vma=False,
    )
```

```python
import functools

import jax
import jax.numpy as jnp
import numpy as np
from jax import lax
from jax.experimental import pallas as pl
from jax.experimental.pallas import tpu as pltpu
from jax.sharding import PartitionSpec as P

DH = 128
BLK = 16
T = 256
ROWS = 256
NEAR = 2 * BLK
REM = 64
FAR = 96
SCALE = DH**-0.5
BF = jnp.bfloat16
F32 = jnp.float32

STARTS = {1: 0, 2: 128, 3: 192, 4: 224, 5: 240, 6: 248, 7: 252}


def tables():
    spread = np.zeros((T, ROWS), np.float32)
    mean = np.zeros((ROWS, T), np.float32)
    pairs = np.zeros((ROWS, ROWS), np.float32)
    for level, start in STARTS.items():
        factor = 2**level
        for row in range(T // factor):
            spread[row * factor : (row + 1) * factor, start + row] = 1.0
            mean[start + row, row * factor : (row + 1) * factor] = 1.0 / factor
        if level <= 3:
            for block in range(T // factor // BLK):
                other = start + (block ^ 1) * BLK
                mine = start + block * BLK
                pairs[mine : mine + BLK, other : other + BLK] = 1.0
    block_of = np.arange(T) // BLK
    band = (np.abs(block_of[:, None] - block_of[None, :]) <= 1).astype(np.float32)
    rim = np.zeros((T, REM), np.float32)
    rim[:BLK, :BLK] = np.eye(BLK)
    rim[T - BLK :, BLK:NEAR] = np.eye(BLK)
    rim[:, NEAR:] = spread[:, 224:]
    rim_mean = rim.copy()
    rim_mean[:, NEAR:] = mean.T[:, 224:]
    meets = np.zeros((REM, FAR), np.float32)
    meets[0:16, 0:16] = 1.0
    meets[16:32, 16:32] = 1.0
    meets[32:48, 32:48] = 1.0
    meets[48:56, 48:64] = 1.0
    meets[56:60, 64:80] = 1.0
    meets[60:62, 80:96] = 1.0
    bf = lambda array: np.asarray(array, dtype=BF)
    return {
        "spread": bf(spread),
        "gather": bf(spread.T),
        "mean": bf(mean),
        "unmean": bf(mean.T),
        "band": band,
        "pairs": pairs,
        "rim": bf(rim),
        "rim_mean": bf(rim_mean),
        "meets": meets,
        "met": np.ascontiguousarray(meets.T),
    }


def dot(left, right):
    return jnp.dot(left, right, preferred_element_type=F32)


def dot_nt(left, right):
    return lax.dot_general(left, right, (((1,), (1,)), ((), ())), preferred_element_type=F32)


def dot_tn(left, right):
    return lax.dot_general(left, right, (((0,), (0,)), ((), ())), preferred_element_type=F32)


def dot_two(exact, right):
    high = right.astype(BF)
    low = (right - high.astype(F32)).astype(BF)
    return dot(exact, high) + dot(exact, low)


def normed(values):
    scale = lax.rsqrt(jnp.mean(values * values, axis=-1, keepdims=True) + 1e-06)
    return values * scale, scale


def norm_back(unit, scale, grad):
    return scale * (grad - unit * jnp.mean(grad * unit, axis=-1, keepdims=True))


def head(array, number):
    return array[:, number * DH : (number + 1) * DH]


def pack_den(d_den_0, d_den_1):
    lane = lax.broadcasted_iota(jnp.int32, (T, DH), 1)
    total = jnp.zeros((T, DH), F32)
    for number, array in enumerate((d_den_0, d_den_1)):
        high = array.astype(BF).astype(F32)
        total = jnp.where(lane == 2 * number, high, total)
        total = jnp.where(lane == 2 * number + 1, array - high, total)
    return total.astype(BF)


def packed_den(sums, number):
    at = 2 * DH + 2 * number
    return sums[:, at : at + 1] + sums[:, at + 1 : at + 2]


def with_ones(values):
    return jnp.concatenate([values, jnp.ones_like(values)], axis=1)


class Calls:
    def __init__(self):
        self.token = None

    def __call__(self, kernel, outs, *args, placed=False, after=(), flops=1e10):
        first = tuple(after) if self.token is None else (self.token,) + tuple(after)
        skipped = len(first)
        args = first + args
        specs = [pl.BlockSpec(memory_space=pltpu.VMEM)] * len(args)

        def body(*refs):
            refs = refs[skipped:-1]
            if placed:
                kernel((lax.axis_index("ctx"), lax.axis_index("head")), *refs)
            else:
                kernel(*refs)

        shapes = [jax.ShapeDtypeStruct(shape, dtype) for shape, dtype in outs]
        shapes.append(jax.ShapeDtypeStruct((8, 128), F32))
        results = pl.pallas_call(
            body,
            out_shape=tuple(shapes),
            in_specs=specs,
            out_specs=tuple(pl.BlockSpec(memory_space=pltpu.VMEM) for _ in shapes),
            compiler_params=pltpu.CompilerParams(vmem_limit_bytes=44 * 1024 * 1024),
            cost_estimate=pl.CostEstimate(
                flops=int(flops), bytes_accessed=1000, transcendentals=0
            ),
        )(*args)
        self.token = results[-1]
        return results[:-1]


def packed(rows):
    half = rows.shape[1] // 2
    return jnp.concatenate([rows[:, :half], rows[:, half:]], axis=0)


def unpacked(rows):
    half = rows.shape[0] // 2
    return jnp.concatenate([rows[:half], rows[half:]], axis=1)


def edges_kernel(pos, tokens, near_out, far_out, level_5_out):
    even = pos[0] % 2 == 0
    row = lax.broadcasted_iota(jnp.int32, (BLK, T), 0)
    col = lax.broadcasted_iota(jnp.int32, (BLK, T), 1)
    mean = dot(jnp.where(col // BLK == row, 1.0 / BLK, 0.0).astype(BF), tokens[...])
    row = lax.broadcasted_iota(jnp.int32, (8, T), 0)
    col = lax.broadcasted_iota(jnp.int32, (8, T), 1)
    wide = dot(jnp.where(col // NEAR == row, 1.0 / NEAR, 0.0).astype(BF), tokens[...])
    first = tokens[:BLK].astype(F32)
    last = tokens[T - BLK :].astype(F32)
    near_out[:BLK] = mean.astype(BF)
    near_out[BLK:] = jnp.where(even, last, first).astype(BF)
    far_out[...] = jnp.where(even, first, last).astype(BF)
    level_5_out[...] = packed(wide).astype(BF)


def project_kernel(tokens, weights, mean, qkv_out, coarse_out):
    tok = tokens[...]
    parts = [dot(tok, weights[number]).astype(BF) for number in range(3)]
    qkv = jnp.concatenate(parts, axis=1)
    qkv_out[...] = qkv
    coarse_out[...] = dot(mean[...], qkv)


def half_of_rows(whole, number):
    width = whole.shape[0] // 32
    return jnp.concatenate(
        [whole[(2 * j + number) * width : (2 * j + number + 1) * width] for j in range(16)], axis=0
    )


def d_attn_kernel(pos, grad_out, w_out, tokens, d_attn_out, own_out, other_out):
    d_attn_out[...] = dot_nt(grad_out[...], w_out[...]).astype(BF)
    even = pos[0] % 2 == 0
    for number, array in enumerate((tokens, grad_out)):
        cols = slice(number * T, (number + 1) * T)
        turned = array[...].T
        halves = half_of_rows(turned, 0), half_of_rows(turned, 1)
        own_out[:, cols] = jnp.where(even, halves[0], halves[1])
        other_out[:, cols] = jnp.where(even, halves[1], halves[0])


def merged(factor, first, second):
    row = lax.broadcasted_iota(jnp.int32, (BLK, BLK), 0)
    col = lax.broadcasted_iota(jnp.int32, (BLK, BLK), 1)
    same = row // 8 == col // 8
    source = col % 8 // 2
    left = jnp.where(jnp.logical_and(same, source == row % 8), factor, 0.0).astype(BF)
    right = jnp.where(jnp.logical_and(same, source + 4 == row % 8), factor, 0.0).astype(BF)
    return (dot(left, first) + dot(right, second)).astype(BF)


def merge_kernel(factor, first, second, *rest):
    if len(rest) > 1:
        rest[1][...] = rest[0][...]
    rest[-1][...] = merged(factor, first[...], second[...])


def bundle_kernel(level_5, level_6, third, fourth, chained, near, out):
    out[:BLK] = level_5[...]
    out[BLK : 2 * BLK] = level_6[...]
    out[2 * BLK : 3 * BLK] = merged(0.5, third[...], fourth[...])
    out[3 * BLK : 5 * BLK] = packed(chained[...].astype(F32)).astype(BF)
    out[5 * BLK :] = packed(near[...].astype(F32)).astype(BF)


EDGE = 2 * BLK
LEVEL_5 = 3 * BLK
SECOND = 3 * BLK


def grads_5_kernel(level_4, own, side, out):
    out[:BLK] = level_4[...]
    out[BLK : BLK + SECOND] = own[...]
    out[BLK + SECOND :] = side[...]


def grads_6(pos, own, other):
    row = lax.broadcasted_iota(jnp.int32, (8, BLK), 0)
    col = lax.broadcasted_iota(jnp.int32, (8, BLK), 1)
    pairs = jnp.where(col // 2 == row, 1.0, 0.0).astype(BF)
    low, high = by_side(pos, own, other)
    blocks = []
    for rows in (low, high):
        both = [rows[at : at + 8] for at in (LEVEL_5, LEVEL_5 + SECOND)]
        blocks.append(dot(pairs, jnp.concatenate(both, axis=0).astype(BF)))
    y_low = pos[0] // 2 % 2 == 0
    edges = []
    for rows, mine in ((high, jnp.logical_not(y_low)), (low, y_low)):
        here, there = rows[EDGE : EDGE + BLK], rows[EDGE + SECOND : EDGE + SECOND + BLK]
        edges.append(jnp.where(mine, here, there))
    return jnp.concatenate(blocks, axis=0), edges


def grads_7_kernel(pos, own, other, level_6, up, down, level_6_out, level_7_out, far_out):
    z_even = pos[0] // 4 % 2 == 0
    from_up, from_down = up[-BLK:].astype(F32), down[-BLK:].astype(F32)
    half = from_up.shape[1] // 2
    came_6 = jnp.where(z_even, from_down[:, :half], from_up[:, :half]).astype(BF)
    level_6_out[...] = came_6
    level_7_out[...] = merged(1.0, level_6[...], came_6)
    low, high = by_side(pos, own[...].astype(F32), other[...].astype(F32))
    at = slice(EDGE + SECOND, EDGE + SECOND + BLK)
    y_low = pos[0] // 2 % 2 == 0
    left = jnp.where(y_low, from_up[:, half:], high[at])
    right = jnp.where(y_low, low[at], from_down[:, half:])
    far_out[...] = jnp.where(pos[0] % 2 == 0, left, right).astype(BF)


def local_units(qkv, coarse, number):
    query = head(qkv, number).astype(F32)
    key = head(qkv, 2 + number).astype(F32)
    return (
        normed(query),
        normed(key),
        head(qkv, 4 + number),
        normed(head(coarse, number)),
        normed(head(coarse, 2 + number)),
        head(coarse, 4 + number).astype(BF),
    )


def local_weights(units, band, pairs):
    (qn, _), (kn, _), _, (qc, _), (kc, _), _ = units
    near = jnp.exp(dot_nt(qn.astype(BF), kn.astype(BF)) * SCALE) * band
    far = jnp.exp(dot_nt(qc.astype(BF), kc.astype(BF)) * SCALE) * pairs
    return near, far


def local_forward_kernel(
    qkv_ref, coarse_ref, band, pairs, spread, out, probs, turned, units_out, scales_out
):
    qkv = qkv_ref[...]
    coarse = coarse_ref[...]
    for number in range(2):
        units = local_units(qkv, coarse, number)
        near, far = (array.astype(BF) for array in local_weights(units, band[...], pairs[...]))
        total = dot(near, with_ones(units[2]))
        part = dot(far, with_ones(units[5]))
        out[:, number * 2 * DH : (number + 1) * 2 * DH] = total + dot_two(spread[...], part)
        probs[:, number * T : (number + 1) * T] = near
        probs[:, (2 + number) * T : (3 + number) * T] = far
        swapped = (units[1], units[0], units[2], units[4], units[3], units[5])
        near, far = (array.astype(BF) for array in local_weights(swapped, band[...], pairs[...]))
        turned[:, number * T : (number + 1) * T] = near
        turned[:, (2 + number) * T : (3 + number) * T] = far
        for place, (unit, scale) in enumerate((units[0], units[1], units[3], units[4])):
            at = slice((2 * place + number) * DH, (2 * place + number + 1) * DH)
            units_out[:, at] = unit
            scales_out[:, at] = jnp.broadcast_to(scale, (T, DH))


def by_side(pos, ours, others):
    even = pos[0] % 2 == 0
    return jnp.where(even, ours, others), jnp.where(even, others, ours)


def remote_rows(pos, arrived, far, levels):
    left, right = by_side(pos, far, arrived[BLK:])
    return jnp.concatenate([left, right, arrived[:BLK]] + levels, axis=0)


def own_rows(fine, coarse):
    return jnp.concatenate([fine[:BLK], fine[T - BLK :], coarse[224:]], axis=0)


def exists(pos, shape, axis):
    where = lax.broadcasted_iota(jnp.int32, shape, axis)
    no_left = jnp.logical_and(pos[0] == 0, where < BLK)
    no_right = jnp.logical_and(pos[0] == 31, jnp.logical_and(where >= BLK, where < NEAR))
    return jnp.where(jnp.logical_or(no_left, no_right), 0.0, 1.0)


def remote_weights(pos, query, remote, meets, number):
    key, key_scale = normed(head(remote, number))
    value = head(remote, 2 + number).astype(BF)
    weights = jnp.exp(dot_nt(query, key.astype(BF)) * SCALE) * meets * exists(pos, (REM, FAR), 1)
    return weights, key, key_scale, value


def gathered_rows(pos, far, mine_ref, theirs_ref):
    mine = mine_ref[...].astype(F32)
    theirs = theirs_ref[...].astype(F32)
    levels = []
    for level in range(3):
        at = slice(level * BLK, (level + 1) * BLK)
        levels += by_side(pos, unpacked(mine[at]), unpacked(theirs[at]))
    arrived = unpacked(theirs[5 * BLK :])
    return remote_rows(pos, arrived, far[...].astype(F32), levels), theirs


def turn_far_kernel(
    pos, weights_ref, near, far, mine_ref, theirs_ref, own_out, other_out, query_out
):
    even = pos[0] % 2 == 0
    rows, theirs = gathered_rows(pos, far, mine_ref, theirs_ref)
    known = near[...].astype(F32)
    left, right = by_side(pos, known[BLK:], unpacked(theirs[3 * BLK : 5 * BLK]))
    other = jnp.concatenate([left, right, known[:BLK], rows[3 * BLK :]], axis=0)
    for array, out in ((rows, own_out), (other, other_out)):
        turned = array.T
        out[...] = jnp.where(even, half_of_rows(turned, 0), half_of_rows(turned, 1)).astype(BF)
    query_out[...] = dot(rows.astype(BF), weights_ref[0]).astype(BF)


def remote_forward_kernel(
    pos, weights_ref, qkv_ref, coarse_ref, local_ref, d_attn, far, mine_ref, theirs_ref,
    meets, rim, gather,
    attn_out, both_out, level_4_out, share_out, remote_out,
):
    rows, _ = gathered_rows(pos, far, mine_ref, theirs_ref)
    even = pos[0] % 2 == 0
    rows = rows.astype(BF)
    remote = jnp.concatenate([dot(rows, weights_ref[part]) for part in (1, 2)], axis=1)
    remote = remote.astype(BF)
    remote_out[...] = remote
    remote = remote.astype(F32)
    d_nums, d_dens = [], []
    for number in range(2):
        fine = qkv_ref[:, number * DH : (number + 1) * DH].astype(F32)
        query = normed(own_rows(fine, coarse_ref[:, number * DH : (number + 1) * DH]))[0]
        weights, _, _, value = remote_weights(
            pos, query.astype(BF), remote, meets[...], number
        )
        part = dot(weights.astype(BF), with_ones(value)).astype(BF)
        total = local_ref[:, number * 2 * DH : (number + 1) * 2 * DH] + dot(rim[...], part)
        cols = slice(number * DH, (number + 1) * DH)
        inverse = 1.0 / total[:, DH:]
        attn = total[:, :DH] * inverse
        attn_out[:, cols] = attn.astype(BF)
        d_num = (d_attn[:, cols].astype(F32) * inverse).astype(BF)
        d_den = -jnp.sum(d_num.astype(F32) * attn, axis=-1, keepdims=True)
        d_nums.append(d_num)
        d_dens.append(jnp.broadcast_to(d_den, (T, DH)))
    both = jnp.concatenate(d_nums + [pack_den(*d_dens)], axis=1)
    both_out[...] = both
    sums = dot(gather[224:256, :], both)
    for number in range(2):
        den_sums = jnp.broadcast_to(packed_den(sums, number), (NEAR, DH))
        for offset, full, row_sums in (
            (0, d_nums[number].astype(F32), head(sums, number)),
            (2 * DH, d_dens[number], den_sums),
        ):
            at = slice(offset + number * DH, offset + (number + 1) * DH)
            first = full[:BLK]
            last = full[T - BLK :]
            level_4_out[:, at] = row_sums[:BLK].astype(BF)
            share = [
                jnp.where(even, last, first),
                jnp.where(even, first, last),
                row_sums[BLK:],
            ]
            share_out[:, at] = jnp.concatenate(share, axis=0).astype(BF)


def local_backward_kernel(
    pos, qkv_ref, coarse_ref, probs, turned, units_ref, scales_ref, attn_ref, both_ref,
    remote_ref, meets, gather, unmean,
    y_out, dkv_out,
):
    remote = remote_ref[...].astype(F32)
    both = both_ref[...]
    y_out[:T, T:] = attn_ref[...]
    sums = dot(gather[...], both)
    dens = both[:, 2 * DH :]
    dens_c = pack_den(*(jnp.broadcast_to(packed_den(sums, number), (T, DH)) for number in (0, 1)))
    lane = lax.broadcasted_iota(jnp.int32, (T, DH), 1)
    dqns, dkns, dvns, tables = [], [], [], []
    for number in range(2):
        cols = slice(number * DH, (number + 1) * DH)
        vals = slice((2 + number) * DH, (3 + number) * DH)
        qn, kn, qc, kc = (head(units_ref, 2 * place + number) for place in range(4))
        qc_scale, kc_scale = (head(scales_ref, 2 * place + number) for place in (2, 3))
        picks = jnp.where(lane // 2 == number, 1.0, 0.0).astype(BF)
        sides = []
        for place, d_num, den, value, query, key in (
            (0, head(both, number), dens, head(qkv_ref, 4 + number), qn, kn),
            (2, head(sums, number).astype(BF), dens_c,
             head(coarse_ref, 4 + number).astype(BF), qc, kc),
        ):
            at = slice((place + number) * T, (place + number + 1) * T)
            grad = jnp.concatenate([d_num, den], axis=1)
            value = jnp.concatenate([value, picks], axis=1)
            weights, weights_t = probs[:, at], turned[:, at]
            d_score = (weights * dot_nt(grad, value) * SCALE).astype(BF)
            d_score_t = (weights_t * dot_nt(value, grad) * SCALE).astype(BF)
            sides.append(
                (
                    dot(d_score, key.astype(BF)),
                    dot(d_score_t, query.astype(BF)),
                    dot(weights_t, d_num),
                )
            )
        (dqn, dkn, dvn), (dqc, dkc, dvc) = sides
        query = own_rows(qn, qc).astype(BF)
        weights, key_r, key_scale, value_r = remote_weights(
            pos, query, remote, meets[...], number
        )
        d_num_r = own_rows(head(both, number).astype(F32), head(sums, number)).astype(BF)
        den_r = own_rows(dens.astype(F32), dens_c.astype(F32)).astype(BF)
        picks = picks[:FAR]
        d_rem = dot_nt(
            jnp.concatenate([d_num_r, den_r], axis=1), jnp.concatenate([value_r, picks], axis=1)
        )
        d_rem = (weights * d_rem * SCALE).astype(BF)
        y_out[2 * T : 2 * T + FAR, cols] = norm_back(
            key_r, key_scale, dot_tn(d_rem, query)
        ).astype(BF)
        y_out[2 * T : 2 * T + FAR, vals] = dot_tn(weights.astype(BF), d_num_r).astype(BF)
        dqr = dot(d_rem, key_r.astype(BF))
        dqns.append(
            jnp.concatenate(
                [dqn[:BLK] + dqr[:BLK], dqn[BLK : T - BLK], dqn[T - BLK :] + dqr[BLK:NEAR]], axis=0
            )
        )
        dqc = jnp.concatenate([dqc[:224], dqc[224:] + dqr[NEAR:]], axis=0)
        dkns.append(dkn)
        dvns.append(dvn)
        tables += [norm_back(qc, qc_scale, dqc), norm_back(kc, kc_scale, dkc), dvc]
    table = dot(unmean[...], jnp.concatenate(tables, axis=1).astype(BF))
    for number in range(2):
        cols = slice(number * DH, (number + 1) * DH)
        vals = slice((2 + number) * DH, (3 + number) * DH)
        qn, kn = (head(units_ref, 2 * place + number) for place in (0, 1))
        q_scale, k_scale = (head(scales_ref, 2 * place + number) for place in (0, 1))
        dq, dk, dv = (head(table, 3 * number + place) for place in range(3))
        y_out[:T, cols] = (norm_back(qn, q_scale, dqns[number]) + dq).astype(BF)
        dk = norm_back(kn, k_scale, dkns[number]) + dk
        dv = dvns[number] + dv
        dkv_out[:, cols] = dk
        dkv_out[:, vals] = dv
        y_out[T : 2 * T, cols] = dk.astype(BF)
        y_out[T : 2 * T, vals] = dv.astype(BF)


def remote_backward_kernel(
    pos, qkv_ref, coarse_ref, local_ref, remote_ref, own_ref, other_ref, g_far, g_6, g_7,
    met, rim_mean, dkv_out,
):
    other = other_ref[...].astype(F32)
    at = slice(LEVEL_5 + SECOND, LEVEL_5 + SECOND + 8)
    sides = by_side(pos, own_ref[...].astype(F32)[at], other[at])
    levels = list(sides) + [g_6[...].astype(F32), g_7[...].astype(F32)]
    grads = remote_rows(pos, other[:NEAR], g_far[...].astype(F32), levels)
    for number in range(2):
        query = normed(head(remote_ref, number).astype(F32))[0].astype(BF)
        k_cols = slice((2 + number) * DH, (3 + number) * DH)
        v_cols = slice((4 + number) * DH, (5 + number) * DH)
        key, key_scale = normed(
            own_rows(qkv_ref[:, k_cols].astype(F32), coarse_ref[:, k_cols])
        )
        vals = own_rows(qkv_ref[:, v_cols].astype(F32), coarse_ref[:, v_cols]).astype(BF)
        weights = jnp.exp(dot_nt(query, key.astype(BF)) * SCALE)
        weights = weights * met[...] * exists(pos, (FAR, REM), 0)
        d_num = head(grads, number).astype(BF)
        d_den = head(grads, 2 + number)[:, :1]
        d_score = (weights * (dot_nt(d_num, vals) + d_den) * SCALE).astype(BF)
        dk = norm_back(key, key_scale, dot_tn(d_score, query))
        dv = dot_tn(weights.astype(BF), d_num)
        more = dot_two(rim_mean[...], jnp.concatenate([dk, dv], axis=1))
        k_cols = slice(number * DH, (number + 1) * DH)
        v_cols = slice((2 + number) * DH, (3 + number) * DH)
        dkv_out[:, k_cols] = (local_ref[:, k_cols] + more[:, :DH]).astype(BF)
        dkv_out[:, v_cols] = (local_ref[:, v_cols] + more[:, DH:]).astype(BF)


def weight_part(pos, step, own_half, other_half, own, other, own_far, other_far, out):
    z = pos[0] // 4
    width = own_half.shape[0] // 8
    at = pl.ds(pl.multiple_of((z + step) % 8 * width, width), width)
    for cols in (slice(0, T), slice(T, 2 * T)):
        total = dot(own_half[at, cols], own[:T, cols])
        total += dot(other_half[at, cols], other[:T, cols])
        out[:width, cols] = total.astype(BF)
    total = dot(own_half[at, :T], own[T : 2 * T]) + dot(own_far[at, :], own[2 * T :])
    total += dot(other_half[at, :T], other[T : 2 * T])
    total += dot(other_far[at, :], other[2 * T :])
    out[:width, 2 * T :] = total.astype(BF)


def first_weight_kernel(pos, g_own, g_other, *refs):
    up, down, level_6_out = refs[-3:]
    weight_part(pos, 4, *refs[:-3], up)
    weight_part(pos, 5, *refs[:-3], down)
    level_6, edges = grads_6(pos, g_own[...].astype(F32), g_other[...].astype(F32))
    level_6_out[...] = level_6.astype(BF)
    rows = up.shape[0] - BLK
    for out, edge in zip((up, down), edges):
        out[rows:] = jnp.concatenate([level_6, edge], axis=1).astype(BF)


def weight_kernel(steps, pos, *refs):
    for step, out in zip(steps, refs[-len(steps) :]):
        weight_part(pos, step, *refs[: -len(steps)], out)


def own_weight_kernel(pos, *refs):
    keep_0, keep_1, send, total = refs[-4:]
    half = total.shape[0] // 2
    low = pos[0] // 2 % 2 == 0
    for step, keep in enumerate((keep_0, keep_1)):
        weight_part(pos, step, *refs[:-4], total)
        first, second = total[:half].astype(F32), total[half:].astype(F32)
        keep[...] = jnp.where(low, first, second).astype(BF)
        send[step * half : (step + 1) * half] = jnp.where(low, second, first).astype(BF)


def add_kernel(up, part_up, down, part_down, up_out, down_out):
    rows = part_up.shape[0]
    up_out[...] = (up[:rows].astype(F32) + part_up[...].astype(F32)).astype(BF)
    down_out[...] = (down[:rows].astype(F32) + part_down[...].astype(F32)).astype(BF)


def by_row_half(pos, total, straight, cross):
    low = pos[0] // 2 % 2 == 0
    half = total.shape[0] // 2
    straight[...] = jnp.where(low, total[:half], total[half:]).astype(BF)
    cross[...] = jnp.where(low, total[half:], total[:half]).astype(BF)


def third_step_kernel(pos, up, part_up, down, part_down, *outs):
    by_row_half(pos, up[...].astype(F32) + part_up[...].astype(F32), *outs[:2])
    by_row_half(pos, down[...].astype(F32) + part_down[...].astype(F32), *outs[2:])


def last_step_kernel(cross, straight, keep, side, out):
    total = cross[...].astype(F32) + straight[...].astype(F32)
    rows = total.shape[0]
    out[...] = (total + keep[...].astype(F32) + side[rows:].astype(F32)).astype(BF)


def finish_kernel(*refs):
    w_qkv, w_out = refs[-2:]
    total = refs[0][...].astype(F32)
    for ref in refs[1:-2]:
        total += ref[: total.shape[0]].astype(F32)
    w_qkv[0] = total[:, :T]
    w_qkv[1] = total[:, 2 * T : 3 * T]
    w_qkv[2] = total[:, 3 * T :]
    w_out[...] = total[:, T : 2 * T]


def grad_x_kernel(steps, pos, y, dkv, weights, *outs):
    x = pos[1] % 4
    side = pos[1] // 4
    for number, step in enumerate(steps):
        for turn in range(2):
            target = (side + turn) % 2 * 4 + (x + step) % 4
            rows = pl.ds(pl.multiple_of(target * T, T), T)
            total = dot_nt(y[:T, :T], weights[0, rows, :])
            total += dot_nt(dkv[:, :T], weights[1, rows, :])
            total += dot_nt(dkv[:, T:], weights[2, rows, :])
            outs[number][turn * T : (turn + 1) * T] = total.astype(BF)


def sum_x_kernel(first, second, third, fourth, keep, send):
    total = first[...].astype(F32) + second[...].astype(F32)
    total = total + third[...].astype(F32) + fourth[...].astype(F32)
    keep[...] = total[:T]
    send[...] = total[T:].astype(BF)


def last_x_kernel(keep, came, out):
    out[...] = (keep[...] + came[...].astype(F32)).astype(BF)


def local(tokens, w_qkv, w_out, grad_out):
    const = {name: jnp.asarray(array) for name, array in tables().items()}
    head_count = lax.axis_size("head")
    weights = jnp.transpose(w_qkv, (1, 0, 2))
    width = tokens.shape[1]
    wide = 3 * T

    def swap(array, bit):
        return lax.ppermute(array, "ctx", [(i, i ^ bit) for i in range(32)])

    def chain(array):
        pairs = [(i, (i + 1) % 32) for i in range(1, 32, 2)]
        return lax.ppermute(array, "ctx", pairs + [(b, a) for a, b in pairs])

    def turn_z(array, step, side=0):
        return lax.ppermute(
            array, "ctx", [(i, (i // 4 + step) % 8 * 4 + (i % 4 ^ side)) for i in range(32)]
        )

    call = Calls()

    near, far, level_5 = call(
        edges_kernel, [((NEAR, width), BF), ((BLK, width), BF), ((BLK, width // 2), BF)],
        tokens, placed=True,
    )
    side = swap(level_5, 2)
    qkv, coarse = call(
        project_kernel, [((T, wide), BF), ((ROWS, wide), F32)], tokens, weights, const["mean"]
    )
    far, level_6 = call(
        functools.partial(merge_kernel, 0.5), [((BLK, width), BF), ((BLK, width // 2), BF)],
        level_5, side, far, flops=1e3)
    sixes = [swap(level_6, bit) for bit in (4, 8, 12)]
    chained = chain(far)
    forward, probs, turned, units, scales = call(
        local_forward_kernel,
        [((T, 2 * T), F32)] + [((T, 4 * T), BF)] * 2 + [((T, 4 * T), F32)] * 2,
        qkv, coarse, const["band"], const["pairs"], const["spread"],
    )
    (mine,) = call(
        bundle_kernel, [((9 * BLK, width // 2), BF)], side, *sixes, chained, near, flops=1e3)
    theirs = swap(mine, 1)
    d_attn, own_half, other_half = call(
        d_attn_kernel,
        [((T, T), BF), ((width // 2, 2 * T), BF), ((width // 2, 2 * T), BF)],
        grad_out, w_out, tokens, placed=True,
    )
    sent_half = swap(other_half, 1)
    attn, both, g_4, g_share, remote = call(
        remote_forward_kernel,
        [
            ((T, T), BF), ((T, 3 * DH), BF), ((BLK, 2 * T), BF), ((3 * BLK, 2 * T), BF),
            ((FAR, 2 * T), BF),
        ],
        weights, qkv, coarse, forward, d_attn, chained, mine, theirs,
        const["meets"], const["rim"], const["gather"], placed=True,
    )
    g_side = swap(g_share, 2)
    y, dkv_local = call(
        local_backward_kernel, [((2 * T + FAR, 2 * T), BF), ((T, 2 * T), F32)],
        qkv, coarse, probs, turned, units, scales, attn, both, remote,
        const["meets"], const["gather"], const["unmean"], placed=True,
    )
    other_y = swap(y, 1)
    (g_own,) = call(
        grads_5_kernel, [((7 * BLK, 2 * T), BF)], g_4, g_share, g_side, flops=1e3
    )
    g_other = swap(g_own, 1)
    own_far, other_far, remote_q = call(
        turn_far_kernel, [((width // 2, FAR), BF)] * 2 + [((FAR, T), BF)],
        weights, near, chained, mine, theirs, placed=True,
    )
    chunk = width // 16
    factors = (own_half, sent_half, y, other_y, own_far, other_far)
    whole, half = ((chunk, 4 * T), BF), ((chunk // 2, 4 * T), BF)
    small = ((BLK, 2 * T), BF)
    message = ((chunk + BLK, 4 * T), BF)
    up, down, g_6 = call(
        first_weight_kernel, [message, message, small], g_own, g_other, *factors, placed=True
    )
    up, down = turn_z(up, 1), turn_z(down, -1)
    keep, keep_1, send, _ = call(
        own_weight_kernel, [half, half, whole, whole], *factors, placed=True
    )
    from_side = swap(send, 2)
    steps = (3, 6, 2, 7)
    products = call(
        functools.partial(weight_kernel, steps), [whole] * 4, *factors, placed=True
    )
    parts = dict(zip(steps, products))
    came_6, g_7, g_far = call(
        grads_7_kernel, [small] * 3, g_own, g_other, g_6, up, down, placed=True, flops=1e3
    )
    came_7 = swap(g_7, 8)
    up, down = call(
        add_kernel, [whole] * 2, up, parts[3], down, parts[6], after=[from_side], flops=1e3
    )
    up, down = turn_z(up, 1), turn_z(down, -1)
    (dkv,) = call(
        remote_backward_kernel, [((T, 2 * T), BF)],
        qkv, coarse, dkv_local, remote_q, g_own, g_other, g_far, came_6, came_7,
        const["met"], const["rim_mean"], placed=True,
    )
    if head_count == 8:
        pieces = call(
            functools.partial(grad_x_kernel, (1, 2, 3)), [((2 * T, T), BF)] * 3,
            y, dkv, weights, placed=True,
        )

        def turn_x(array, step):
            pairs = [(i, i // 4 * 4 + (i % 4 + step) % 4) for i in range(8)]
            return lax.ppermute(array, "head", pairs)

        came = [turn_x(pieces[step - 1], step) for step in (1, 2, 3)]
    up_straight, up_cross, straight, cross = call(
        third_step_kernel, [half] * 4, up, parts[2], down, parts[7], placed=True, flops=1e3
    )
    up = [turn_z(up_cross, 1, 2), turn_z(up_straight, 1)]
    from_down = [turn_z(cross, -1, 2), turn_z(straight, -1)]
    if head_count == 8:
        (piece,) = call(
            functools.partial(grad_x_kernel, (0,)), [((2 * T, T), BF)],
            y, dkv, weights, placed=True, flops=1e3,
        )
        keep_x, send_x = call(
            sum_x_kernel, [((T, T), F32), ((T, T), BF)], piece, *came, flops=1e3
        )
        came_x = lax.ppermute(send_x, "head", [(i, i ^ 4) for i in range(8)])
    (last,) = call(last_step_kernel, [half], *up, keep_1, from_side, flops=1e3)
    from_up = [turn_z(last, 1)]
    grad_wqkv, grad_wout = call(
        finish_kernel, [((3, chunk // 2, T), F32), ((chunk // 2, T), F32)],
        keep, from_side, *from_down, *from_up,
    )
    if head_count == 8:
        (grad_x,) = call(last_x_kernel, [((T, T), BF)], keep_x, came_x)
    else:
        flat = jnp.transpose(weights, (1, 0, 2)).reshape(width, wide)
        grad_x = dot_nt(jnp.concatenate([y[:T, :T], dkv], axis=1), flat).astype(BF)
    return grad_x, jnp.transpose(grad_wqkv, (1, 0, 2)), grad_wout.T


def solution(mesh):
    placed = (P("ctx", None), P(None, None, "head"), P("head", None), P("ctx", None))
    return jax.shard_map(
        local,
        mesh=mesh,
        in_specs=placed,
        out_specs=(P("ctx", "head"), P("ctx", None, "head"), P("head", "ctx")),
        check_vma=False,
    )
```
